32 devices in a mesh: batch: 8 (over z, x), chan: 4 (over y, core).
Axes of the slice: x: 2, y: 2, z: 4, core: 2. Of those that a mesh axis runs over, the one named last changes fastest.
Arguments:
- features: bfloat16 [64, 628, 2304], P('batch', 'chan'), may hold values from -40 to 40
- crops: int32 [64, 2, 2], P('batch'), may hold values from 0 to 16
- flips: int32 [64, 2], P('batch'), may hold values from 0 to 1
- gain_in: bfloat16 [628], P('chan'), may hold values from 0.099609375 to 1.8984375
- shift_in: bfloat16 [628], P('chan'), may hold values from -3 to 3
- w_reduce: bfloat16 [628, 132], P('chan'), may hold values from -0.25 to 0.25
- gain_mid: bfloat16 [132], P('chan'), may hold values from 0.099609375 to 1.8984375
- shift_mid: bfloat16 [132], P('chan'), may hold values from -3 to 3
- w_spread: bfloat16 [132, 3, 3, 33], P('chan'), may hold values from -0.1875 to 0.1875
- d_passed: bfloat16 [128, 628, 1024], P('batch', 'chan'), may hold values from -3 to 3
- d_new: bfloat16 [128, 33, 1024], P('batch', None, 'chan'), may hold values from -6 to 6
Outputs:
- passed: bfloat16 [128, 628, 1024], P('batch', 'chan')
- new_maps: bfloat16 [128, 33, 1024], P('batch', None, 'chan')
- features_grad: float32 [64, 628, 2304], P('batch', 'chan')
- w_reduce_grad: float32 [628, 132], P('chan')
- w_spread_grad: float32 [132, 3, 3, 33], P('chan')
- gain_in_grad: float32 [628], P('chan')
- shift_in_grad: float32 [628], P('chan')
- gain_mid_grad: float32 [132], P('chan')
- shift_mid_grad: float32 [132], P('chan')
The draws below stay inside these ranges and needn't reach their ends.
All inputs are finite; a program needn't handle non-finite values.
Results may differ from the reference program's by a relative error of at most 0.0067.
Values may be sent and summed in bfloat16 or wider, within the bound.
A program may use at most 256 MiB of HBM per device.

```python
import jax
import jax.numpy as jnp
from jax import lax

IN_CH = 628
BOT = 132
NEW = 33
H = 32
W = 32
MARGIN = 8
ITEMS = 64
IMAGES = 128
CELLS = 1024


def draw_features(key, part):
    key = jax.random.fold_in(key, 11)
    key_noise, key_scale, key_mean = jax.random.split(key, 3)
    item_index = jnp.arange(ITEMS, dtype=jnp.float32).reshape((ITEMS, 1, 1))
    rising = jnp.exp(jnp.log(3.0) * item_index / max(ITEMS - 1, 1))
    shape = (ITEMS, IN_CH, (H + 2 * MARGIN) * (W + 2 * MARGIN))
    noise = jax.random.truncated_normal(key_noise, -4.0, 4.0, shape, jnp.float32)
    scales = jnp.exp(jax.random.uniform(key_scale, (IN_CH, 1), jnp.float32, jnp.log(0.3), jnp.log(3.0)))
    means = jax.random.uniform(key_mean, (IN_CH, 1), jnp.float32, -1.0, 1.0)
    return ((noise * scales + means) * rising).astype(jnp.bfloat16)


def place_ends(values, stream_key, least, largest):
    dims = values.shape
    index_at = [jax.random.randint(jax.random.fold_in(stream_key, axis), (), 0, dims[axis]) for axis in range(len(dims))]
    values = values.at[tuple(index_at)].set(least)
    longest = dims.index(max(dims))
    index_at[longest] = (index_at[longest] + 1) % dims[longest]
    return values.at[tuple(index_at)].set(largest)


def levels(stream_key, dims, shards, smallest, top_value):
    factor_of, own = 1.0, jax.random.fold_in(stream_key, 6)
    for axis_at, parts in shards:
        heights = jnp.exp(jax.random.uniform(jax.random.fold_in(own, axis_at), (parts,), jnp.float32, smallest / len(shards), top_value / len(shards)))
        factor_of = factor_of * jnp.repeat(heights, dims[axis_at] // parts).reshape([-1 if axis == axis_at else 1 for axis in range(len(dims))])
    return factor_of


def normal_values(key, dims, scale, limit, shards=(), kind=jnp.bfloat16):
    drawn = jax.random.normal(key, dims, jnp.float32) * scale
    if len(shards) > 0:
        drawn = levels(key, dims, shards, -0.22, 0.18) * drawn
    return jnp.clip(drawn, min=-limit, max=limit).astype(kind)


def setup_inputs(seed: int = 0) -> dict:
    key_list = jax.random.split(jax.random.key(seed), 12)
    features = draw_features(jax.random.fold_in(key_list[11], 71), 0)
    crops = place_ends(jax.random.randint(key_list[1], (ITEMS, 2, 2), 0, 2 * MARGIN + 1), jax.random.fold_in(key_list[1], 1), 0, 2 * MARGIN).astype(jnp.int32)
    flips = place_ends(jax.random.randint(key_list[2], (ITEMS, 2), 0, 2), jax.random.fold_in(key_list[2], 1), 0, 1).astype(jnp.int32)
    gain_in = jnp.clip(1.0 + 0.18 * jax.random.normal(key_list[3], (IN_CH,), jnp.float32), 0.099609375, 1.8984375).astype(jnp.bfloat16)
    shift_in = normal_values(key_list[4], (IN_CH,), 0.5, 3.0, ((0, 4),))
    w_reduce = normal_values(key_list[5], (IN_CH, BOT), IN_CH ** -0.5, 0.25, ((0, 4),))
    gain_mid = jnp.clip(1.0 + 0.18 * jax.random.normal(key_list[6], (BOT,), jnp.float32), 0.099609375, 1.8984375).astype(jnp.bfloat16)
    shift_mid = normal_values(key_list[7], (BOT,), 0.5, 3.0, ((0, 4),))
    w_spread = normal_values(key_list[8], (BOT, 3, 3, NEW), (9 * BOT) ** -0.5, 0.1875, ((0, 4),))
    d_passed = normal_values(key_list[9], (IMAGES, IN_CH, CELLS), 0.5, 3.0, ((0, 8), (1, 4)))
    d_new = normal_values(key_list[10], (IMAGES, NEW, CELLS), 1.0, 6.0, ((0, 8), (2, 4)))
    return {"features": features, "crops": crops, "flips": flips, "gain_in": gain_in, "shift_in": shift_in, "w_reduce": w_reduce, "gain_mid": gain_mid, "shift_mid": shift_mid, "w_spread": w_spread, "d_passed": d_passed, "d_new": d_new}


@jax.custom_vjp
def low(v):
    return lax.optimization_barrier(v.astype(jnp.bfloat16)).astype(jnp.float32)

@jax.custom_vjp
def low_back(v):
    return v

def low_keep(v):
    return (low(v), None)

def low_pass(kept, grad):
    return (grad,)

def back_keep(v):
    return (v, None)

def back_low(kept, grad):
    return (low(grad),)
low.defvjp(low_keep, low_pass)
low_back.defvjp(back_keep, back_low)
epsilon = 1e-05

def cropped(feature_maps, crops, flips):
    channels = feature_maps.shape[1]
    grids = feature_maps.reshape((feature_maps.shape[0], channels, H + 2 * MARGIN, W + 2 * MARGIN))

    def crop_one(item_map, offset, flip_flag):
        window = lax.dynamic_slice(item_map, (jnp.int32(0), offset[0].astype(jnp.int32), offset[1].astype(jnp.int32)), (channels, H, W))
        return jnp.where(flip_flag > 0, window[:, :, ::-1], window)
    per_item = jax.vmap(jax.vmap(crop_one, in_axes=(None, 0, 0)))(grids, crops, flips)
    return per_item.reshape((-1, channels, H * W))

def normalize(values, gain, shift):
    mean_val = lax.optimization_barrier(jnp.mean(values, axis=(0, 2), keepdims=True))
    var_val = lax.optimization_barrier(jnp.mean(jnp.square(values - mean_val), axis=(0, 2), keepdims=True))
    return (values - mean_val) * lax.rsqrt(var_val + epsilon) * gain[:, None] + shift[:, None]

def reference(features, crops, flips, gain_in, shift_in, w_reduce, gain_mid, shift_mid, w_spread, d_passed, d_new):

    def forward(feature_maps, gain_one, shift_one, weight_one, gain_two, shift_two, weight_two):
        views = cropped(feature_maps, crops, flips)
        act_in = low(jax.nn.silu(normalize(views, gain_one, shift_one)))
        middle = low_back(jnp.einsum('ncp,ck->nkp', act_in, weight_one, precision=lax.Precision.HIGHEST))
        act_mid = low(jax.nn.silu(normalize(middle, gain_two, shift_two)))
        grid_mid = act_mid.reshape((act_mid.shape[0], act_mid.shape[1], H, W))
        new_part = lax.conv_general_dilated(grid_mid, weight_two, (1, 1), ((1, 1), (1, 1)), dimension_numbers=('NCHW', 'IHWO', 'NCHW'), precision=lax.Precision.HIGHEST)
        return (views, new_part.reshape((new_part.shape[0], new_part.shape[1], H * W)))
    primal = (features.astype(jnp.float32), gain_in.astype(jnp.float32), shift_in.astype(jnp.float32), w_reduce.astype(jnp.float32), gain_mid.astype(jnp.float32), shift_mid.astype(jnp.float32), w_spread.astype(jnp.float32))
    outputs, pullback = jax.vjp(forward, *primal)
    gradients = pullback((d_passed.astype(jnp.float32), d_new.astype(jnp.float32)))
    return (outputs[0].astype(jnp.bfloat16), outputs[1].astype(jnp.bfloat16), gradients[0], gradients[3], gradients[6], gradients[1], gradients[2], gradients[4], gradients[5])
```

```python
import functools

import jax
import jax.numpy as jnp
from jax import lax
from jax.experimental import pallas as pl
from jax.experimental.pallas import tpu as pltpu
from jax.sharding import PartitionSpec as P

H = 32
W = 32
MARGIN = 8
GRID = H + 2 * MARGIN
CELLS = H * W
EPS = 1e-05
CHUNK = 256
SPAN = 512
STRIDE = 8 * GRID
TAPS = 9
MID_PAD = 144
NEW_PAD = 48
F32 = jnp.float32
BF16 = jnp.bfloat16
MESH = pl.DeviceIdType.MESH
VMEM_LIMIT = 62 * 2**20


def dot(a, b):
    return jnp.dot(a, b, preferred_element_type=F32)


def dot_nt(a, b):
    return lax.dot_general(a, b, (((1,), (1,)), ((), ())), preferred_element_type=F32)


def iota(shape, axis):
    return lax.broadcasted_iota(jnp.int32, shape, axis)


def lane_fold(values):
    total = values[:, 0:128]
    for at in range(128, values.shape[1], 128):
        total = total + values[:, at : at + 128]
    return total


def cols_to_row(pad_ref, values):
    pad_ref[0 : values.shape[0], :] = values
    halves = [
        jnp.sum(jnp.transpose(pad_ref[at : at + 128, :]), axis=0, keepdims=True)
        for at in (0, 128)
    ]
    return jnp.concatenate(halves, axis=1)


def row_to_cols(out_ref, row):
    rows = out_ref.shape[0]
    for at in (0, 128):
        height = min(128, rows - at)
        square = jnp.broadcast_to(row[:, at : at + 128], (128, 128))
        out_ref[at : at + height, :] = jnp.transpose(square)[0:height, :]


def window_start(crops_ref, j, v):
    start = crops_ref[j, v, 0] * GRID + crops_ref[j, v, 1]
    base = jnp.minimum((start // 128) * 128, GRID * GRID - 3 * STRIDE - SPAN)
    return pl.multiple_of(base, 128), start - base


def chunk_target(offset, flip, cell):
    col = cell & (W - 1)
    row = cell >> 5
    return offset + row * GRID + jnp.where(flip > 0, W - 1 - col, col)


def crop_kernel(crops_ref, flips_ref, x_ref, views_ref, stats_ref, mean_ref, dev_ref, pad_ref):
    j = pl.program_id(0)
    count = 2 * CELLS
    total = None
    for v in range(2):
        base, offset = window_start(crops_ref, j, v)
        target = chunk_target(offset, flips_ref[j, v], iota((1, CHUNK), 1))
        select = (iota((SPAN, CHUNK), 0) == target).astype(BF16)
        for k in range(CELLS // CHUNK):
            span = x_ref[0, :, pl.ds(pl.multiple_of(base + STRIDE * k, 128), SPAN)]
            part = dot(span, select)
            views_ref[v, :, CHUNK * k : CHUNK * (k + 1)] = part.astype(BF16)
            folded = lane_fold(part)
            total = folded if total is None else total + folded
    mean = jnp.sum(total, axis=1, keepdims=True) / count
    squares = None
    for v in range(2):
        for k in range(CELLS // CHUNK):
            part = views_ref[v, :, CHUNK * k : CHUNK * (k + 1)].astype(F32) - mean
            folded = lane_fold(part * part)
            squares = folded if squares is None else squares + folded
    dev = jnp.sum(squares, axis=1, keepdims=True)

    @pl.when(j == 0)
    def _():
        mean_ref[...] = jnp.zeros_like(mean_ref)
        dev_ref[...] = jnp.zeros_like(dev_ref)
        pad_ref[...] = jnp.zeros_like(pad_ref)

    before = lax.convert_element_type(j, F32)
    old = mean_ref[...]
    delta = mean - old
    share = 1.0 / (before + 1.0)
    mean_ref[...] = old + delta * share
    dev_ref[...] = dev_ref[...] + dev + delta * delta * (count * before * share)

    @pl.when(j == pl.num_programs(0) - 1)
    def _():
        lane = iota(mean_ref.shape, 1)
        stats_ref[...] = jnp.zeros_like(stats_ref)
        stats_ref[0:1, :] = cols_to_row(pad_ref, jnp.where(lane == 0, mean_ref[...], 0.0))
        stats_ref[1:2, :] = cols_to_row(pad_ref, jnp.where(lane == 0, dev_ref[...], 0.0))


def crop_views(features, crops, flips):
    items, channels, cells = features.shape
    return pl.pallas_call(
        crop_kernel,
        grid=(items,),
        in_specs=[
            pl.BlockSpec(memory_space=pltpu.SMEM),
            pl.BlockSpec(memory_space=pltpu.SMEM),
            pl.BlockSpec((1, channels, cells), lambda j: (j, 0, 0)),
        ],
        out_specs=[
            pl.BlockSpec((2, channels, CELLS), lambda j: (j, 0, 0)),
            pl.BlockSpec((8, 256), lambda j: (0, 0)),
        ],
        out_shape=[
            jax.ShapeDtypeStruct((2 * items, channels, CELLS), BF16),
            jax.ShapeDtypeStruct((8, 256), F32),
        ],
        scratch_shapes=[
            pltpu.VMEM((channels, 128), F32),
            pltpu.VMEM((channels, 128), F32),
            pltpu.VMEM((256, 128), F32),
        ],
        compiler_params=pltpu.CompilerParams(vmem_limit_bytes=VMEM_LIMIT),
        name="crop_views",
    )(crops, flips, features)


def place_kernel(crops_ref, flips_ref, coef_ref, x_ref, dpre_ref, dpass_ref, out_ref):
    j = pl.program_id(0)
    coef = coef_ref[0 : x_ref.shape[1], :]
    mean, slant, level, gain = (coef[:, at : at + 1] for at in range(4))
    out_ref[...] = jnp.zeros_like(out_ref)
    for v in range(2):
        base, offset = window_start(crops_ref, j, v)
        target = chunk_target(offset, flips_ref[j, v], iota((CHUNK, 1), 0))
        select = (iota((CHUNK, SPAN), 1) == target).astype(BF16)
        for k in range(CELLS // CHUNK):
            cols = slice(CHUNK * k, CHUNK * (k + 1))
            x = x_ref[v, :, cols].astype(F32)
            grad = gain * dpre_ref[v, :, cols].astype(F32) + dpass_ref[v, :, cols].astype(F32)
            grad = grad + ((x - mean) * slant + level)
            span = pl.ds(pl.multiple_of(base + STRIDE * k, 128), SPAN)
            out_ref[0, :, span] += dot(grad.astype(BF16), select)


def place_views(crops, flips, coef, views, dpre, d_passed):
    items = crops.shape[0]
    channels = views.shape[1]
    pair = pl.BlockSpec((2, channels, CELLS), lambda j: (j, 0, 0))
    return pl.pallas_call(
        place_kernel,
        grid=(items,),
        in_specs=[
            pl.BlockSpec(memory_space=pltpu.SMEM),
            pl.BlockSpec(memory_space=pltpu.SMEM),
            pl.BlockSpec(coef.shape, lambda j: (0, 0)),
            pair,
            pair,
            pair,
        ],
        out_specs=pl.BlockSpec((1, channels, GRID * GRID), lambda j: (j, 0, 0)),
        out_shape=jax.ShapeDtypeStruct((items, channels, GRID * GRID), F32),
        compiler_params=pltpu.CompilerParams(vmem_limit_bytes=VMEM_LIMIT),
        name="place_views",
    )(crops, flips, coef, views, dpre, d_passed)


def sigmoid(v):
    return 0.5 * jnp.tanh(0.5 * v) + 0.5


def combine(parts, count):
    groups = parts.shape[0]
    mean = parts[0, 0:1, :]
    dev = parts[0, 1:2, :]
    for at in range(1, groups):
        mean = mean + parts[at, 0:1, :]
        dev = dev + parts[at, 1:2, :]
    mean = mean / groups
    spread = None
    for at in range(groups):
        off = parts[at, 0:1, :] - mean
        spread = off * off if spread is None else spread + off * off
    return mean, dev + spread * count


def layer_kernel(
    nb,
    views_hbm,
    stats_ref,
    params_ref,
    wr_in,
    wsp_in,
    dnew_hbm,
    dpre_hbm,
    coef_ref,
    new_ref,
    wrg_ref,
    wsg_ref,
    grads_ref,
    x_sc,
    act_sc,
    slope_sc,
    half_out,
    half_in,
    pair_sc,
    far_sc,
    d_sc,
    dcol_sc,
    mid_sc,
    actm_sc,
    dm_out,
    dm_in,
    t_sc,
    dn_sc,
    dnf_sc,
    par_sc,
    wsp_sc,
    wr_sc,
    wrt_sc,
    wb_sc,
    wf_sc,
    stat_sc,
    cstat_sc,
    msg_sc,
    cmsg_sc,
    col_sc,
    colm_sc,
    padc_sc,
    padm_sc,
    acc_sc,
    accm_sc,
    wg_sc,
    wsg_sc,
    wsgo_sc,
    wsgi_sc,
    rs_out,
    rs_in,
    ag_sc,
    newo_sc,
    newi_sc,
    load_sem,
    store_sem,
    half_s,
    half_r,
    far_s,
    far_r,
    dm_s,
    dm_r,
    bat_s,
    bat_r,
    chan_s,
    chan_r,
    own_sem,
):
    bi, ci = lax.axis_index("batch"), lax.axis_index("chan")
    y, c = ci // 2, lax.rem(ci, 2)
    n_views, n_in = x_sc.shape[0], x_sc.shape[1]
    quarter = n_views // 4
    local_count = float(n_views * CELLS)
    owned_count = float(quarter * CELLS)
    pixels = float(nb) * local_count
    mate = (bi, 2 * y + (1 - c))
    across = (bi, 2 * (1 - y) + c)

    def batch_peer(k):
        return (lax.rem(bi + k, nb), ci)

    def chan_peer(k):
        return (bi, lax.rem(ci + k, 4))

    barrier = pltpu.get_barrier_semaphore()

    def greet(k, carry):
        pl.semaphore_signal(barrier, inc=1, device_id=batch_peer(k), device_id_type=MESH)
        return carry

    lax.fori_loop(1, nb, greet, 0)
    for k in range(1, 4):
        pl.semaphore_signal(barrier, inc=1, device_id=chan_peer(k), device_id_type=MESH)
    pl.semaphore_wait(barrier, nb + 2)

    def batch_copy(kind, k, src, dst):
        return pltpu.make_async_remote_copy(
            src_ref=src,
            dst_ref=dst,
            send_sem=bat_s.at[kind, k],
            recv_sem=bat_r.at[kind, k],
            device_id=batch_peer(k),
            device_id_type=MESH,
        )

    def batch_send(kind, src_of, dst):
        def step(k, carry):
            batch_copy(kind, k, src_of(lax.rem(bi + k, nb)), dst.at[bi]).start()
            return carry

        lax.fori_loop(1, nb, step, 0)

    def batch_wait(kind, src_of, dst):
        def step(k, carry):
            other = lax.rem(bi + nb - k, nb)
            batch_copy(kind, k, src_of(lax.rem(bi + k, nb)), dst.at[other]).wait()
            return carry

        lax.fori_loop(1, nb, step, 0)

    def chan_copy(kind, k, src, dst):
        return pltpu.make_async_remote_copy(
            src_ref=src,
            dst_ref=dst,
            send_sem=chan_s.at[kind, k],
            recv_sem=chan_r.at[kind, k],
            device_id=chan_peer(k),
            device_id_type=MESH,
        )

    def chan_send(kind, src_of, dst):
        for k in range(1, 4):
            chan_copy(kind, k, src_of(lax.rem(ci + k, 4)), dst.at[ci]).start()

    def chan_wait(kind, src_of, dst):
        for k in range(1, 4):
            other = lax.rem(ci + 4 - k, 4)
            chan_copy(kind, k, src_of(lax.rem(ci + k, 4)), dst.at[other]).wait()

    def same(ref):
        return lambda other: ref

    def load(n):
        return pltpu.make_async_copy(views_hbm.at[n], x_sc.at[n], load_sem.at[n])

    def load_step(n, carry):
        load(n).start()
        return carry

    stat_sc[0, bi] = stats_ref[...]
    batch_send(0, same(stats_ref), stat_sc.at[0])
    lax.fori_loop(0, n_views, load_step, 0)
    par_sc[ci] = params_ref[...]
    chan_send(0, same(params_ref), par_sc)
    wsp_sc[ci] = wsp_in[...]
    chan_send(1, same(wsp_in), wsp_sc)
    own_new = pltpu.make_async_copy(dnew_hbm.at[:, c], dn_sc.at[ci], own_sem)
    own_new.start()
    dnew_of = lambda other: dnew_hbm.at[:, lax.rem(other, 2)]
    chan_send(2, dnew_of, dn_sc)

    padc_sc[...] = jnp.zeros_like(padc_sc)
    padm_sc[...] = jnp.zeros_like(padm_sc)
    acc_sc[...] = jnp.zeros_like(acc_sc)
    accm_sc[...] = jnp.zeros_like(accm_sc)
    wg_sc[...] = jnp.zeros_like(wg_sc)
    wsg_sc[...] = jnp.zeros_like(wsg_sc)
    dnf_sc[...] = jnp.zeros_like(dnf_sc)
    wr_sc[...] = jnp.zeros_like(wr_sc)
    wr_sc[:, 0 : wr_in.shape[1]] = wr_in[...]
    eye = (iota((MID_PAD, MID_PAD), 0) == iota((MID_PAD, MID_PAD), 1)).astype(BF16)
    wrt_sc[...] = dot_nt(eye, wr_sc[...]).astype(BF16)
    gain_row = params_ref[0:1, :]
    shift_row = params_ref[1:2, :]

    batch_wait(0, same(stats_ref), stat_sc.at[0])
    mean_row, dev_row = combine(stat_sc[0], local_count)
    rstd_row = lax.rsqrt(dev_row / pixels + EPS)
    row_to_cols(col_sc.at[0], mean_row)
    row_to_cols(col_sc.at[1], rstd_row)
    row_to_cols(col_sc.at[2], rstd_row * gain_row)
    row_to_cols(col_sc.at[3], shift_row)

    def wide(ref, at):
        col = ref[at]
        return jnp.concatenate([col, col], axis=1)

    def slot_view(i, core):
        h = jnp.where(i < quarter, 1 - y, y)
        return quarter * (2 * h + core) + lax.rem(i, quarter)

    def activate(n):
        mean, scale, shift = wide(col_sc, 0), wide(col_sc, 2), wide(col_sc, 3)
        for k in range(CELLS // CHUNK):
            cols = slice(CHUNK * k, CHUNK * (k + 1))
            pre = (x_sc[n, :, cols].astype(F32) - mean) * scale + shift
            s = sigmoid(pre)
            act = pre * s
            slope_sc[n, :, cols] = (s + act * (1.0 - s)).astype(BF16)
            act_sc[n, :, cols] = act.astype(BF16)

    def partial(n, k):
        return dot(wrt_sc[...], act_sc[n, :, CHUNK * k : CHUNK * (k + 1)])

    def half_copy(i):
        return pltpu.make_async_remote_copy(
            src_ref=half_out.at[i],
            dst_ref=half_in.at[i],
            send_sem=half_s.at[i],
            recv_sem=half_r.at[i],
            device_id=mate,
            device_id_type=MESH,
        )

    def far_copy(i):
        return pltpu.make_async_remote_copy(
            src_ref=pair_sc.at[i],
            dst_ref=far_sc.at[i],
            send_sem=far_s.at[i],
            recv_sem=far_r.at[i],
            device_id=across,
            device_id_type=MESH,
        )

    def forward(i, carry):
        theirs, mine = slot_view(i, 1 - c), slot_view(i, c)
        load(theirs).wait()
        activate(theirs)
        for k in range(CELLS // CHUNK):
            cols = slice(CHUNK * k, CHUNK * (k + 1))
            half_out[i, :, cols] = partial(theirs, k).astype(BF16)
        half_copy(i).start()
        load(mine).wait()
        activate(mine)
        half_copy(i).wait_recv()
        for k in range(CELLS // CHUNK):
            cols = slice(CHUNK * k, CHUNK * (k + 1))
            both = partial(mine, k) + half_in[i, :, cols].astype(F32)
            pair_sc[i, :, cols] = both.astype(BF16)
        far_copy(i).start()
        return carry

    lax.fori_loop(0, 2 * quarter, forward, 0)

    chan_wait(1, same(wsp_in), wsp_sc)
    stacked = wsp_sc[...].reshape(4 * NEW_PAD, TAPS * NEW_PAD)
    n_own = wsg_ref.shape[0]
    lane, row = iota((MID_PAD, 4 * NEW_PAD), 1), iota((MID_PAD, 4 * NEW_PAD), 0)
    hit = None
    for b in range(4):
        inner = lane - NEW_PAD * b
        one = (inner >= 0) & (inner < n_own) & (row == inner + n_own * b)
        hit = one if hit is None else hit | one
    wb_sc[...] = dot(hit.astype(BF16), stacked).astype(BF16)
    taps_eye = iota((TAPS * NEW_PAD, TAPS * NEW_PAD), 0) == iota((TAPS * NEW_PAD, TAPS * NEW_PAD), 1)
    wf_sc[...] = dot_nt(taps_eye.astype(BF16), wb_sc[...]).astype(BF16)

    cell = iota((1, CELLS), 1)
    col_at, row_at = cell & (W - 1), cell >> 5

    def inside(values, row_step, col_step):
        ok = None
        if col_step != 0:
            ok = (col_at + col_step >= 0) & (col_at + col_step < W)
        if row_step != 0:
            on = (row_at + row_step >= 0) & (row_at + row_step < H)
            ok = on if ok is None else ok & on
        return values if ok is None else jnp.where(ok, values, 0.0)

    def at_offset(values, row_step, col_step):
        move = (-(W * row_step + col_step)) % CELLS
        rolled = values if move == 0 else pltpu.roll(values, move, 1)
        return inside(rolled, row_step, col_step)

    own_new.wait()
    chan_wait(2, dnew_of, dn_sc)

    def back_slot(i, carry):
        h = jnp.where(i < quarter, 1 - y, y)
        keep = i
        for b in range(4):
            dnf_sc[0 : dn_sc.shape[3], CHUNK * b : CHUNK * (b + 1)] = dn_sc[b, h, lax.rem(i, quarter)].astype(F32)
        grad = dnf_sc[...]
        for b in range(3):
            moved = at_offset(grad, 0, 1 - b)
            for a in range(3):
                t = 3 * a + b
                tap = at_offset(moved, 1 - a, 0)
                dcol_sc[keep, NEW_PAD * t : NEW_PAD * (t + 1), :] = tap.astype(BF16)
        for k in range(CELLS // CHUNK):
            cols = slice(CHUNK * k, CHUNK * (k + 1))
            d_sc[i, :, cols] = dot(wb_sc[...], dcol_sc[keep, :, cols])
        return carry

    lax.fori_loop(0, 2 * quarter, back_slot, 0)

    chan_wait(0, same(params_ref), par_sc)

    def gathered(at):
        total = None
        for b in range(4):
            piece = jnp.where(iota((8, 256), 1) < n_own, par_sc[b], 0.0)
            piece = piece if b == 0 else pltpu.roll(piece, n_own * b, 1)
            total = piece if total is None else total + piece
        return total[at : at + 1, :]

    row_to_cols(colm_sc.at[2], gathered(2))
    row_to_cols(colm_sc.at[3], gathered(3))

    def middle_sum(q, carry):
        far_copy(q).wait_recv()
        total = None
        for k in range(CELLS // CHUNK):
            cols = slice(CHUNK * k, CHUNK * (k + 1))
            part = pair_sc[quarter + q, :, cols].astype(F32) + far_sc[q, :, cols].astype(F32)
            mid_sc[q, :, cols] = part
            folded = lane_fold(part)
            total = folded if total is None else total + folded
        accm_sc[0] += total
        return carry

    lax.fori_loop(0, quarter, middle_sum, 0)
    local_mean = jnp.sum(accm_sc[0], axis=1, keepdims=True) / owned_count

    def middle_dev(q, carry):
        total = None
        for k in range(CELLS // CHUNK):
            part = mid_sc[q, :, CHUNK * k : CHUNK * (k + 1)] - local_mean
            folded = lane_fold(part * part)
            total = folded if total is None else total + folded
        accm_sc[1] += total
        return carry

    lax.fori_loop(0, quarter, middle_dev, 0)
    cmsg_sc[0] = jnp.zeros_like(cmsg_sc[0])
    cmsg_sc[0, 0:1, :] = cols_to_row(padm_sc, accm_sc[0]) / owned_count
    cmsg_sc[0, 1:2, :] = cols_to_row(padm_sc, accm_sc[1])
    accm_sc[...] = jnp.zeros_like(accm_sc)
    cstat_sc[0, ci] = cmsg_sc[0]
    chan_send(3, same(cmsg_sc.at[0]), cstat_sc.at[0])
    chan_wait(3, same(cmsg_sc.at[0]), cstat_sc.at[0])
    group_mean, group_dev = combine(cstat_sc[0], owned_count)
    msg_sc[0] = jnp.zeros_like(msg_sc[0])
    msg_sc[0, 0:1, :] = group_mean
    msg_sc[0, 1:2, :] = group_dev
    stat_sc[1, bi] = msg_sc[0]
    batch_send(1, same(msg_sc.at[0]), stat_sc.at[1])
    batch_wait(1, same(msg_sc.at[0]), stat_sc.at[1])
    meanm_row, devm_row = combine(stat_sc[1], local_count)
    rstdm_row = lax.rsqrt(devm_row / pixels + EPS)
    row_to_cols(colm_sc.at[0], meanm_row)
    row_to_cols(colm_sc.at[1], rstdm_row)

    def mid_point(values):
        mean, rstd = wide(colm_sc, 0), wide(colm_sc, 1)
        norm = (values - mean) * rstd
        pre = norm * wide(colm_sc, 2) + wide(colm_sc, 3)
        s = sigmoid(pre)
        act = pre * s
        return norm, act, s + act * (1.0 - s)

    def mid_own(q, carry):
        first, second = None, None
        for k in range(CELLS // CHUNK):
            cols = slice(CHUNK * k, CHUNK * (k + 1))
            norm, act, slope = mid_point(mid_sc[q, :, cols])
            actm_sc[q, :, cols] = act.astype(BF16)
            grad = d_sc[quarter + q, :, cols] * slope
            d_sc[quarter + q, :, cols] = grad
            mid_sc[q, :, cols] = norm
            one, two = lane_fold(grad), lane_fold(grad * norm)
            first = one if first is None else first + one
            second = two if second is None else second + two
        accm_sc[0] += first
        accm_sc[1] += second
        return carry

    lax.fori_loop(0, quarter, mid_own, 0)
    cmsg_sc[1] = jnp.zeros_like(cmsg_sc[1])
    cmsg_sc[1, 0:1, :] = cols_to_row(padm_sc, accm_sc[0])
    cmsg_sc[1, 1:2, :] = cols_to_row(padm_sc, accm_sc[1])
    cstat_sc[1, ci] = cmsg_sc[1]
    chan_send(4, same(cmsg_sc.at[1]), cstat_sc.at[1])
    chan_wait(4, same(cmsg_sc.at[1]), cstat_sc.at[1])
    msg_sc[1] = (cstat_sc[1, 0] + cstat_sc[1, 1]) + (cstat_sc[1, 2] + cstat_sc[1, 3])
    stat_sc[2, bi] = msg_sc[1]
    batch_send(2, same(msg_sc.at[1]), stat_sc.at[2])

    def spread(q, carry):
        for k in range(CELLS // CHUNK):
            cols = slice(CHUNK * k, CHUNK * (k + 1))
            t_sc[:, cols] = dot(wf_sc[...], actm_sc[q, :, cols])
        total = None
        for b in range(3):
            column = None
            for a in range(3):
                t = 3 * a + b
                tap = at_offset(t_sc[NEW_PAD * t : NEW_PAD * t + 40, :], a - 1, 0)
                column = tap if column is None else column + tap
            column = at_offset(column, 0, b - 1)
            total = column if total is None else total + column
        for b in range(4):
            newo_sc[b, q] = total[0 : newo_sc.shape[2], CHUNK * b : CHUNK * (b + 1)].astype(BF16)
        wsg_sc[...] += dot_nt(actm_sc[q], dcol_sc[quarter + q])
        return carry

    lax.fori_loop(0, quarter, spread, 0)
    new_of = lambda other: newo_sc.at[other]
    newi_sc[ci] = newo_sc[ci]
    chan_send(5, new_of, newi_sc)
    for b in range(4):
        wsgo_sc[b] = wsg_sc[n_own * b : n_own * b + 40, :]
    wsgi_sc[ci] = wsgo_sc[ci]
    wsg_of = lambda other: wsgo_sc.at[other]
    chan_send(6, wsg_of, wsgi_sc)

    batch_wait(2, same(msg_sc.at[1]), stat_sc.at[2])
    total = stat_sc[2, 0]
    for at in range(1, nb):
        total = total + stat_sc[2, at]
    row_to_cols(colm_sc.at[4], total[0:1, :] / pixels)
    row_to_cols(colm_sc.at[5], total[1:2, :] / pixels)
    mid_sums = total
    gain_row_mid = gathered(2)
    row_to_cols(colm_sc.at[6], gain_row_mid * rstdm_row)

    def dm_copy(i):
        return pltpu.make_async_remote_copy(
            src_ref=dm_out.at[i],
            dst_ref=dm_in.at[i],
            send_sem=dm_s.at[i],
            recv_sem=dm_r.at[i],
            device_id=mate,
            device_id_type=MESH,
        )

    def store(n):
        return pltpu.make_async_copy(slope_sc.at[n], dpre_hbm.at[n], store_sem.at[n])

    def back_view(n, dm_ref):
        mean, rstd = wide(col_sc, 0), wide(col_sc, 1)
        first, second = None, None
        for k in range(CELLS // CHUNK):
            cols = slice(CHUNK * k, CHUNK * (k + 1))
            grad = dot(wr_sc[...], dm_ref[:, cols]) * slope_sc[n, :, cols].astype(F32)
            slope_sc[n, :, cols] = grad.astype(BF16)
            norm = (x_sc[n, :, cols].astype(F32) - mean) * rstd
            one, two = lane_fold(grad), lane_fold(grad * norm)
            first = one if first is None else first + one
            second = two if second is None else second + two
        acc_sc[0] += first
        acc_sc[1] += second
        wg_sc[0:n_in, :] += dot_nt(act_sc[n], dm_ref[...])
        store(n).start()

    def dm_own(q, carry):
        i = quarter + q
        for k in range(CELLS // CHUNK):
            cols = slice(CHUNK * k, CHUNK * (k + 1))
            grad = d_sc[i, :, cols] - wide(colm_sc, 4) - mid_sc[q, :, cols] * wide(colm_sc, 5)
            dm_out[i, :, cols] = (grad * wide(colm_sc, 6)).astype(BF16)
        dm_copy(i).start()
        return carry

    lax.fori_loop(0, quarter, dm_own, 0)

    def back_own(q, carry):
        i = quarter + q
        back_view(slot_view(i, c), dm_out.at[i])
        dm_copy(i).wait_recv()
        back_view(slot_view(i, 1 - c), dm_in.at[i])
        return carry

    lax.fori_loop(0, quarter, back_own, 0)

    rs_rows = rs_out.shape[2]
    chan_wait(6, wsg_of, wsgi_sc)
    wsg_total = (wsgi_sc[0] + wsgi_sc[1]) + (wsgi_sc[2] + wsgi_sc[3])
    wsg_tiles = [
        (r, l, min(128, TAPS * NEW_PAD - 128 * l)) for r in range(5) for l in range(4)
    ]

    def put_tiles(slot, values, tiles):
        for at, (r, l, width) in enumerate(tiles):
            rs_out[slot, at // rs_rows, at % rs_rows, :, 0:width] = values[
                8 * r : 8 * r + 8, 128 * l : 128 * l + width
            ]

    def scatter(slot, kind):
        rs_in[slot, bi] = rs_out[slot, bi]
        batch_send(kind, lambda other: rs_out.at[slot, other], rs_in.at[slot])

    def reduce_gather(slot, kind):
        batch_wait(kind, lambda other: rs_out.at[slot, other], rs_in.at[slot])
        total = rs_in[slot, 0]
        for at in range(1, nb):
            total = total + rs_in[slot, at]
        rs_out[slot, bi] = total
        ag_sc[slot, bi] = total
        batch_send(kind + 1, same(rs_out.at[slot, bi]), ag_sc.at[slot])

    def gather_wait(slot, kind):
        batch_wait(kind + 1, same(rs_out.at[slot, bi]), ag_sc.at[slot])

    rs_out[...] = jnp.zeros_like(rs_out)
    put_tiles(0, wsg_total, wsg_tiles)
    scatter(0, 4)

    def back_far(q, carry):
        far_copy(quarter + q).wait_recv()
        for k in range(CELLS // CHUNK):
            cols = slice(CHUNK * k, CHUNK * (k + 1))
            part = pair_sc[q, :, cols].astype(F32) + far_sc[quarter + q, :, cols].astype(F32)
            norm, act, slope = mid_point(part)
            grad = d_sc[q, :, cols] * slope - wide(colm_sc, 4) - norm * wide(colm_sc, 5)
            dm_out[q, :, cols] = (grad * wide(colm_sc, 6)).astype(BF16)
        dm_copy(q).start()
        back_view(slot_view(q, c), dm_out.at[q])
        dm_copy(q).wait_recv()
        back_view(slot_view(q, 1 - c), dm_in.at[q])
        return carry

    lax.fori_loop(0, quarter, back_far, 0)

    msg_sc[2] = jnp.zeros_like(msg_sc[2])
    msg_sc[2, 0:1, :] = cols_to_row(padc_sc, acc_sc[0])
    msg_sc[2, 1:2, :] = cols_to_row(padc_sc, acc_sc[1])
    stat_sc[3, bi] = msg_sc[2]
    batch_send(3, same(msg_sc.at[2]), stat_sc.at[3])
    wrg_tiles = [(r, l, 128 if l == 0 else MID_PAD - 128) for r in range(20) for l in range(2)]
    put_tiles(1, wg_sc, wrg_tiles)
    scatter(1, 6)
    reduce_gather(0, 4)
    reduce_gather(1, 6)

    chan_wait(5, new_of, newi_sc)
    for b in range(4):
        for q in range(quarter):
            new_ref[quarter * b + q] = newi_sc[b, q]

    batch_wait(3, same(msg_sc.at[2]), stat_sc.at[3])
    total = stat_sc[3, 0]
    for at in range(1, nb):
        total = total + stat_sc[3, at]
    gain_scale = gain_row * rstd_row
    row_to_cols(col_sc.at[4], -gain_scale * rstd_row * (total[1:2, :] / pixels))
    row_to_cols(col_sc.at[5], -gain_scale * (total[0:1, :] / pixels))
    row_to_cols(col_sc.at[6], gain_scale)
    lane = iota(coef_ref.shape, 1)
    coef = jnp.where(lane == 0, col_sc[0], 0.0)
    coef = jnp.where(lane == 1, col_sc[4], coef)
    coef = jnp.where(lane == 2, col_sc[5], coef)
    coef_ref[...] = jnp.where(lane == 3, col_sc[6], coef)

    grads_ref[...] = jnp.zeros_like(grads_ref)
    grads_ref[0:1, :] = total[1:2, :]
    grads_ref[1:2, :] = total[0:1, :]
    own_sums = mid_sums
    for b in range(1, 4):
        own_sums = jnp.where(ci == b, pltpu.roll(mid_sums, 256 - n_own * b, 1), own_sums)
    grads_ref[2:3, :] = own_sums[1:2, :]
    grads_ref[3:4, :] = own_sums[0:1, :]

    gather_wait(0, 4)
    for at, (r, l, width) in enumerate(wsg_tiles):
        height = min(8, wsg_ref.shape[0] - 8 * r)
        wsg_ref[8 * r : 8 * r + height, 128 * l : 128 * l + width] = ag_sc[
            0, at // rs_rows, at % rs_rows, 0:height, 0:width
        ]
    gather_wait(1, 6)
    for at, (r, l, width) in enumerate(wrg_tiles):
        height = min(8, wrg_ref.shape[0] - 8 * r)
        width = min(width, wrg_ref.shape[1] - 128 * l)
        wrg_ref[8 * r : 8 * r + height, 128 * l : 128 * l + width] = ag_sc[
            1, at // rs_rows, at % rs_rows, 0:height, 0:width
        ]

    def finish(n, carry):
        store(n).wait()
        return carry

    lax.fori_loop(0, n_views, finish, 0)

    def sent(i, carry):
        half_copy(i).wait_send()
        far_copy(i).wait_send()
        dm_copy(i).wait_send()
        return carry

    lax.fori_loop(0, 2 * quarter, sent, 0)


def layer(nb, views, stats, params, w_reduce, w_spread, d_new):
    n_views, n_in, _ = views.shape
    n_mid = w_reduce.shape[1]
    n_own = n_mid // 4
    quarter = n_views // 4
    n_new = d_new.shape[3]
    rs_rows = -(-40 // nb)
    n_cols = TAPS * NEW_PAD
    vmem = pl.BlockSpec(memory_space=pltpu.VMEM)
    anywhere = pl.BlockSpec(memory_space=pl.ANY)
    dma = pltpu.SemaphoreType.DMA
    slots = 2 * quarter
    return pl.pallas_call(
        functools.partial(layer_kernel, nb),
        in_specs=[anywhere, vmem, vmem, vmem, vmem, anywhere],
        out_specs=[anywhere, vmem, vmem, vmem, vmem, vmem],
        out_shape=[
            jax.ShapeDtypeStruct((n_views, n_in, CELLS), BF16),
            jax.ShapeDtypeStruct((n_in, 128), F32),
            jax.ShapeDtypeStruct((n_views, n_new, CHUNK), BF16),
            jax.ShapeDtypeStruct((n_in, n_mid), F32),
            jax.ShapeDtypeStruct((n_own, n_cols), F32),
            jax.ShapeDtypeStruct((8, 256), F32),
        ],
        scratch_shapes=[
            pltpu.VMEM((n_views, n_in, CELLS), BF16),
            pltpu.VMEM((n_views, n_in, CELLS), BF16),
            pltpu.VMEM((n_views, n_in, CELLS), BF16),
            pltpu.VMEM((slots, MID_PAD, CELLS), BF16),
            pltpu.VMEM((slots, MID_PAD, CELLS), BF16),
            pltpu.VMEM((slots, MID_PAD, CELLS), BF16),
            pltpu.VMEM((slots, MID_PAD, CELLS), BF16),
            pltpu.VMEM((slots, MID_PAD, CELLS), F32),
            pltpu.VMEM((slots, n_cols, CELLS), BF16),
            pltpu.VMEM((quarter, MID_PAD, CELLS), F32),
            pltpu.VMEM((quarter, MID_PAD, CELLS), BF16),
            pltpu.VMEM((slots, MID_PAD, CELLS), BF16),
            pltpu.VMEM((slots, MID_PAD, CELLS), BF16),
            pltpu.VMEM((n_cols, CELLS), F32),
            pltpu.VMEM((4, 2, quarter, n_new, CHUNK), BF16),
            pltpu.VMEM((NEW_PAD, CELLS), F32),
            pltpu.VMEM((4, 8, 256), F32),
            pltpu.VMEM((4, NEW_PAD, n_cols), BF16),
            pltpu.VMEM((n_in, MID_PAD), BF16),
            pltpu.VMEM((MID_PAD, n_in), BF16),
            pltpu.VMEM((MID_PAD, n_cols), BF16),
            pltpu.VMEM((n_cols, MID_PAD), BF16),
            pltpu.VMEM((4, nb, 8, 256), F32),
            pltpu.VMEM((2, 4, 8, 256), F32),
            pltpu.VMEM((3, 8, 256), F32),
            pltpu.VMEM((2, 8, 256), F32),
            pltpu.VMEM((7, n_in, 128), F32),
            pltpu.VMEM((7, MID_PAD, 128), F32),
            pltpu.VMEM((256, 128), F32),
            pltpu.VMEM((256, 128), F32),
            pltpu.VMEM((2, n_in, 128), F32),
            pltpu.VMEM((2, MID_PAD, 128), F32),
            pltpu.VMEM((160, MID_PAD), F32),
            pltpu.VMEM((MID_PAD, n_cols), F32),
            pltpu.VMEM((4, 40, n_cols), F32),
            pltpu.VMEM((4, 40, n_cols), F32),
            pltpu.VMEM((2, nb, rs_rows, 8, 128), F32),
            pltpu.VMEM((2, nb, rs_rows, 8, 128), F32),
            pltpu.VMEM((2, nb, rs_rows, 8, 128), F32),
            pltpu.VMEM((4, quarter, n_new, CHUNK), BF16),
            pltpu.VMEM((4, quarter, n_new, CHUNK), BF16),
            dma((n_views,)),
            dma((n_views,)),
            dma((slots,)),
            dma((slots,)),
            dma((slots,)),
            dma((slots,)),
            dma((slots,)),
            dma((slots,)),
            dma((8, nb)),
            dma((8, nb)),
            dma((7, 4)),
            dma((7, 4)),
            dma,
        ],
        compiler_params=pltpu.CompilerParams(
            collective_id=0, has_side_effects=True, vmem_limit_bytes=VMEM_LIMIT
        ),
        name="layer",
    )(views, stats, params, w_reduce, w_spread, d_new)


def solution(mesh):
    nb = mesh.shape["batch"]

    def on_device(features, crops, flips, gain_in, shift_in, w_reduce, gain_mid, shift_mid, w_spread, d_passed, d_new):
        n_in, n_mid = w_reduce.shape
        n_own, n_new = w_spread.shape[0], w_spread.shape[3]
        n_views = d_new.shape[0]

        def as_row(v):
            return jnp.pad(v.astype(F32), (0, 256 - v.shape[0]))

        params = jnp.stack([as_row(v) for v in (gain_in, shift_in, gain_mid, shift_mid)])
        params = jnp.pad(params, ((0, 4), (0, 0)))
        w9 = w_spread.reshape(n_own, TAPS, n_new)
        w9 = jnp.pad(w9, ((0, NEW_PAD - n_own), (0, 0), (0, NEW_PAD - n_new)))
        w9 = w9.reshape(NEW_PAD, TAPS * NEW_PAD)
        grads = d_new.reshape(2, 2, n_views // 4, n_new, d_new.shape[2])
        views, stats = crop_views(features, crops, flips)
        dpre, coef, new_maps, wr_grad, ws_grad, sums = layer(nb, views, stats, params, w_reduce, w9, grads)
        features_grad = place_views(crops, flips, coef, views, dpre, d_passed)
        ws_grad = ws_grad.reshape(n_own, TAPS, NEW_PAD)[:, :, :n_new].reshape(w_spread.shape)
        return (
            views,
            new_maps,
            features_grad,
            wr_grad,
            ws_grad,
            sums[0, :n_in],
            sums[1, :n_in],
            sums[2, :n_own],
            sums[3, :n_own],
        )

    return jax.shard_map(
        on_device,
        mesh=mesh,
        in_specs=(
            P("batch", "chan", None),
            P("batch", None, None),
            P("batch", None),
            P("chan"),
            P("chan"),
            P("chan", None),
            P("chan"),
            P("chan"),
            P("chan", None, None, None),
            P("batch", "chan", None),
            P("batch", None, "chan"),
        ),
        out_specs=(
            P("batch", "chan", None),
            P("batch", None, "chan"),
            P("batch", "chan", None),
            P("chan", None),
            P("chan", None, None, None),
            P("chan"),
            P("chan"),
            P("chan"),
            P("chan"),
        ),
        check_vma=False,
    )
```

```python
import functools

import jax
import jax.numpy as jnp
from jax import lax
from jax.experimental import pallas as pl
from jax.experimental.pallas import tpu as pltpu
from jax.sharding import PartitionSpec as P

H = 32
W = 32
MARGIN = 8
GRID = H + 2 * MARGIN
CELLS = H * W
EPS = 1e-05
CHUNK = 256
SPAN = 512
STRIDE = 8 * GRID
TAPS = 9
MID_PAD = 144
NEW_PAD = 48
MAIN = 128
REST = 4
F32 = jnp.float32
BF16 = jnp.bfloat16
MESH = pl.DeviceIdType.MESH
VMEM_LIMIT = 63 * 2**20 + 800 * 2**10


def dot(a, b):
    return jnp.dot(a, b, preferred_element_type=F32)


def dot_nt(a, b):
    return lax.dot_general(a, b, (((1,), (1,)), ((), ())), preferred_element_type=F32)


def iota(shape, axis):
    return lax.broadcasted_iota(jnp.int32, shape, axis)


def lane_fold(values):
    total = values[:, 0:128]
    for at in range(128, values.shape[1], 128):
        total = total + values[:, at : at + 128]
    return total


def cols_to_row(pad_ref, values):
    if values is not None:
        pad_ref[0 : values.shape[0], :] = values
    halves = [
        jnp.sum(jnp.transpose(pad_ref[at : at + 128, :]), axis=0, keepdims=True)
        for at in (0, 128)
    ]
    return jnp.concatenate(halves, axis=0)


def two_rows(row):
    return jnp.concatenate([row[:, 0:128], row[:, 128:256]], axis=0)


def one_row(rows):
    return jnp.concatenate([rows[0:1, :], rows[1:2, :]], axis=1)


def row_to_cols(out_ref, row):
    rows = out_ref.shape[0]
    for h, at in enumerate((0, 128)):
        height = min(128, rows - at)
        square = jnp.broadcast_to(row[h : h + 1, :], (128, 128))
        out_ref[at : at + height, :] = jnp.transpose(square)[0:height, :]


def window_start(crops_ref, j, v):
    start = crops_ref[v, 0, j] * GRID + crops_ref[v, 1, j]
    base = jnp.minimum((start // 128) * 128, GRID * GRID - 3 * STRIDE - SPAN)
    return pl.multiple_of(base, 128), start - base


def chunk_target(offset, flip, cell):
    col = cell & (W - 1)
    row = cell >> 5
    return offset + row * GRID + jnp.where(flip > 0, W - 1 - col, col)


def crop_kernel(crops_ref, flips_ref, x_ref, views_ref, passed_ref, stats_ref, pick_sc, xf_sc, xi_sc, pf_sc, mean_sc, dev_sc):
    step = pl.program_id(0)
    rows, items, cells = x_ref.shape
    n_views = 2 * items

    @pl.when(step == 0)
    def _():
        def build(n, carry):
            j, v = n // 2, n % 2
            _, offset = window_start(crops_ref, j, v)
            target = chunk_target(offset, flips_ref[v, j], iota((1, CHUNK), 1))
            pick_sc[n] = (iota((SPAN, CHUNK), 0) == target).astype(BF16)
            return carry

        lax.fori_loop(0, n_views, build, 0)
        mean_sc[...] = jnp.zeros_like(mean_sc)
        dev_sc[...] = jnp.zeros_like(dev_sc)

    for l in range(cells // 128):
        at = slice(128 * l, 128 * (l + 1))
        wide_x = x_ref[:, :, at].astype(F32)
        for ch in range(rows):
            xf_sc[l, (items + 1) * ch : (items + 1) * ch + items, :] = wide_x[ch]

    total = jnp.zeros((rows, 128), F32)
    squares = jnp.zeros((rows, 128), F32)
    pivot = None
    for j in range(items):
        for l in range(cells // 128):
            xi_sc[j, :, 128 * l : 128 * (l + 1)] = xf_sc[l, pl.ds(j, rows, stride=items + 1), :].astype(BF16)
        for v in range(2):
            n = 2 * j + v
            base, _ = window_start(crops_ref, j, v)
            spans = [xi_sc[j, :, pl.ds(pl.multiple_of(base + STRIDE * k, 128), SPAN)] for k in range(CELLS // CHUNK)]
            parts = dot(jnp.concatenate(spans, axis=0), pick_sc[n])
            for k in range(CELLS // CHUNK):
                cols = slice(CHUNK * k, CHUNK * (k + 1))
                part = parts[rows * k : rows * (k + 1), :]
                views_ref[n, :, cols] = part.astype(BF16)
                for l in range(2):
                    pf_sc[2 * k + l, pl.ds(n, rows, stride=n_views + 1), :] = part[:, 128 * l : 128 * (l + 1)]
                if pivot is None:
                    pivot = jnp.sum(lane_fold(part), axis=1, keepdims=True) / CHUNK
                off = part - pivot
                total = total + lane_fold(off)
                squares = squares + lane_fold(off * off)
    for l in range(CELLS // 128):
        at = slice(128 * l, 128 * (l + 1))
        for ch in range(rows):
            first = (n_views + 1) * ch
            passed_ref[ch, :, at] = pf_sc[l, first : first + n_views, :].astype(BF16)
    count = n_views * CELLS
    shift = jnp.sum(total, axis=1, keepdims=True) / count
    mean = pivot + shift
    first = pl.multiple_of(step * rows, 8)
    lane = iota((rows, 128), 1)
    mean_sc[pl.ds(first, rows), :] = jnp.where(lane == 0, mean, 0.0)
    dev_sc[pl.ds(first, rows), :] = squares - jnp.where(lane == 0, shift * shift * count, 0.0)

    @pl.when(step == pl.num_programs(0) - 1)
    def _():
        stats_ref[...] = jnp.zeros_like(stats_ref)
        stats_ref[0:2, :] = cols_to_row(mean_sc, None)
        stats_ref[2:4, :] = cols_to_row(dev_sc, None)


def crop_views(features, crops, flips):
    channels, items, cells = features.shape
    rows = 80
    return pl.pallas_call(
        crop_kernel,
        grid=(-(-channels // rows),),
        in_specs=[
            pl.BlockSpec(memory_space=pltpu.SMEM),
            pl.BlockSpec(memory_space=pltpu.SMEM),
            pl.BlockSpec((rows, items, cells), lambda s: (s, 0, 0)),
        ],
        out_specs=[
            pl.BlockSpec((2 * items, rows, CELLS), lambda s: (0, s, 0)),
            pl.BlockSpec((rows, 2 * items, CELLS), lambda s: (s, 0, 0)),
            pl.BlockSpec((8, 128), lambda s: (0, 0)),
        ],
        out_shape=[
            jax.ShapeDtypeStruct((2 * items, channels, CELLS), BF16),
            jax.ShapeDtypeStruct((channels, 2 * items, CELLS), BF16),
            jax.ShapeDtypeStruct((8, 128), F32),
        ],
        scratch_shapes=[
            pltpu.VMEM((2 * items, SPAN, CHUNK), BF16),
            pltpu.VMEM((cells // 128, rows * (items + 1), 128), F32),
            pltpu.VMEM((items, rows, cells), BF16),
            pltpu.VMEM((CELLS // 128, rows * (2 * items + 1), 128), F32),
            pltpu.VMEM((256, 128), F32),
            pltpu.VMEM((256, 128), F32),
        ],
        compiler_params=pltpu.CompilerParams(vmem_limit_bytes=VMEM_LIMIT),
        name="crop_views",
    )(crops, flips, features)


def place_kernel(crops_ref, flips_ref, dv_ref, new_ref, wrg_ref, wsg_ref, sums_ref, out_ref, newo_ref, wrgo_ref, wsgo_ref, gi_ref, si_ref, gm_ref, sm_ref, pick_sc, sum_sc, flat_sc, new_sc):
    step = pl.program_id(0)
    rows, items, cells = out_ref.shape
    n_views = 2 * items

    @pl.when(step == 0)
    def _():
        def build(n, carry):
            j, v = n // 2, n % 2
            _, offset = window_start(crops_ref, j, v)
            target = chunk_target(offset, flips_ref[v, j], iota((CHUNK, 1), 0))
            pick_sc[n] = (iota((CHUNK, SPAN), 1) == target).astype(BF16)
            return carry

        lax.fori_loop(0, n_views, build, 0)
        n_new = new_ref.shape[1]
        for n in range(n_views):
            for l in range(2):
                piece = new_ref[n, :, 128 * l : 128 * (l + 1)]
                new_sc[l, pl.ds(n, n_new, stride=n_views), :] = piece.astype(F32)
        for l in range(2):
            newo_ref[:, :, 128 * l : 128 * (l + 1)] = new_sc[l].reshape(n_new, n_views, 128).astype(BF16)
        wrgo_ref[...] = wrg_ref[...]
        for t in range(TAPS):
            wsgo_ref[t] = wsg_ref[:, NEW_PAD * t : NEW_PAD * t + wsgo_ref.shape[2]]
        for at, ref in enumerate((gi_ref, si_ref, gm_ref, sm_ref)):
            ref[...] = sums_ref[at, 0 : ref.shape[0]]

    for j in range(items):
        sum_sc[j] = jnp.zeros_like(sum_sc[j])
        for v in range(2):
            n = 2 * j + v
            base, _ = window_start(crops_ref, j, v)
            parts = [dv_ref[n, :, CHUNK * k : CHUNK * (k + 1)] for k in range(CELLS // CHUNK)]
            spans = dot(jnp.concatenate(parts, axis=0), pick_sc[n])
            spans = [spans[rows * k : rows * (k + 1), :] for k in range(CELLS // CHUNK)]
            pieces = [spans[0][:, 0:STRIDE]]
            for k in range(1, CELLS // CHUNK):
                pieces.append(spans[k - 1][:, STRIDE:SPAN] + spans[k][:, 0 : SPAN - STRIDE])
                pieces.append(spans[k][:, SPAN - STRIDE : STRIDE])
            pieces.append(spans[-1][:, STRIDE:SPAN])
            window = jnp.concatenate(pieces, axis=1)
            span = pl.ds(base, window.shape[1])
            if v == 0:
                sum_sc[j, :, span] = window
            else:
                sum_sc[j, :, span] += window
        for l in range(cells // 128):
            flat_sc[l, pl.ds(j, rows, stride=items + 1), :] = sum_sc[j, :, 128 * l : 128 * (l + 1)]
    for l in range(cells // 128):
        for ch in range(rows):
            first = (items + 1) * ch
            out_ref[ch, :, 128 * l : 128 * (l + 1)] = flat_sc[l, first : first + items, :]


def place_views(crops, flips, dv, new_maps, wr_grad, ws_grad, sums):
    items = crops.shape[2]
    n_views, channels, _ = dv.shape
    n_new, n_own = new_maps.shape[1], ws_grad.shape[0]
    rows = 80
    whole = lambda shape: pl.BlockSpec(shape, lambda s: (0,) * len(shape))
    small = [
        ((n_new, n_views, CHUNK), BF16),
        (wr_grad.shape, F32),
        ((TAPS, n_own, n_new), F32),
        ((channels,), F32),
        ((channels,), F32),
        ((n_own,), F32),
        ((n_own,), F32),
    ]
    return pl.pallas_call(
        place_kernel,
        grid=(-(-channels // rows),),
        in_specs=[
            pl.BlockSpec(memory_space=pltpu.SMEM),
            pl.BlockSpec(memory_space=pltpu.SMEM),
            pl.BlockSpec((n_views, rows, CELLS), lambda s: (0, s, 0)),
        ]
        + [whole(v.shape) for v in (new_maps, wr_grad, ws_grad, sums)],
        out_specs=[pl.BlockSpec((rows, items, GRID * GRID), lambda s: (s, 0, 0))]
        + [whole(shape) for shape, _ in small],
        out_shape=[jax.ShapeDtypeStruct((channels, items, GRID * GRID), F32)]
        + [jax.ShapeDtypeStruct(shape, kind) for shape, kind in small],
        scratch_shapes=[
            pltpu.VMEM((n_views, CHUNK, SPAN), BF16),
            pltpu.VMEM((items, rows, GRID * GRID), F32),
            pltpu.VMEM((GRID * GRID // 128, rows * (items + 1), 128), F32),
            pltpu.VMEM((2, n_new * n_views, 128), F32),
        ],
        compiler_params=pltpu.CompilerParams(vmem_limit_bytes=VMEM_LIMIT),
        name="place_views",
    )(crops, flips, dv, new_maps, wr_grad, ws_grad, sums)


def sigmoid(v):
    return 0.5 * jnp.tanh(0.5 * v) + 0.5


def combine(parts, count):
    groups = parts.shape[0]
    mean = parts[0, 0:2, :]
    dev = parts[0, 2:4, :]
    for at in range(1, groups):
        mean = mean + parts[at, 0:2, :]
        dev = dev + parts[at, 2:4, :]
    mean = mean / groups
    spread = None
    for at in range(groups):
        off = parts[at, 0:2, :] - mean
        spread = off * off if spread is None else spread + off * off
    return mean, dev + spread * count


def layer_kernel(
    nb,
    views_hbm,
    stats_ref,
    gain_in_ref,
    shift_in_ref,
    gain_mid_ref,
    shift_mid_ref,
    wr_in,
    wsp_in,
    dnew_ref,
    dpass_hbm,
    dv_hbm,
    new_ref,
    wrg_ref,
    wsg_ref,
    sums_ref,
    x_sc,
    act_sc,
    slope_sc,
    dp_sc,
    half_out,
    half_in,
    pair_sc,
    far_sc,
    pair_rest,
    far_rest,
    pack_sc,
    ext_sc,
    d_sc,
    dcol_sc,
    mid_sc,
    actm_sc,
    dm_out,
    dm_in,
    dno_sc,
    dn_sc,
    dnf_sc,
    dpn_sc,
    flat_sc,
    own_par,
    par_sc,
    wsp_sc,
    wr_sc,
    wrt_sc,
    wb_sc,
    wf_sc,
    stat_sc,
    cstat_sc,
    msg_sc,
    cmsg_sc,
    col_sc,
    colm_sc,
    padc_sc,
    padm_sc,
    acc_sc,
    accm_sc,
    wg_sc,
    wsg_sc,
    wsgi_sc,
    ws_out,
    ws_in,
    ws_all,
    wr_out,
    wr_back,
    wr_all,
    newo_sc,
    newi_sc,
    load_sem,
    store_sem,
    half_s,
    half_r,
    far_s,
    far_r,
    rest_s,
    rest_r,
    dm_s,
    dm_r,
    bat_s,
    bat_r,
    chan_s,
    chan_r,
    dp_sem,
):
    bi, ci = lax.axis_index("batch"), lax.axis_index("chan")
    y, c = ci // 2, lax.rem(ci, 2)
    n_views, n_in = x_sc.shape[0], x_sc.shape[1]
    quarter = n_views // 4
    n_own, n_new = wsg_ref.shape[0], dnew_ref.shape[0]
    local_count = float(n_views * CELLS)
    owned_count = float(quarter * CELLS)
    pixels = float(nb) * local_count
    mate = (bi, 2 * y + (1 - c))
    across = (bi, 2 * (1 - y) + c)

    def batch_peer(k):
        return (lax.rem(bi + k, nb), ci)

    def chan_peer(k):
        return (bi, lax.rem(ci + k, 4))

    barrier = pltpu.get_barrier_semaphore()

    def greet(k, carry):
        pl.semaphore_signal(barrier, inc=1, device_id=batch_peer(k), device_id_type=MESH)
        return carry

    lax.fori_loop(1, nb, greet, 0)
    for k in range(1, 4):
        pl.semaphore_signal(barrier, inc=1, device_id=chan_peer(k), device_id_type=MESH)

    def load(n):
        return pltpu.make_async_copy(views_hbm.at[n], x_sc.at[n], load_sem.at[n])

    def load_step(i, carry):
        load(slot_view(i, 1 - c)).start()
        load(slot_view(i, c)).start()
        return carry

    def slot_view(i, core):
        h = jnp.where(i < quarter, 1 - y, y)
        return quarter * (2 * h + core) + lax.rem(i, quarter)

    lax.fori_loop(0, 2 * quarter, load_step, 0)
    pl.semaphore_wait(barrier, nb + 2)

    def batch_copy(kind, k, src, dst):
        return pltpu.make_async_remote_copy(
            src_ref=src,
            dst_ref=dst,
            send_sem=bat_s.at[kind, k],
            recv_sem=bat_r.at[kind, k],
            device_id=batch_peer(k),
            device_id_type=MESH,
        )

    def batch_send(kind, src_of, dst):
        def step(k, carry):
            batch_copy(kind, k, src_of(lax.rem(bi + k, nb)), dst.at[bi]).start()
            return carry

        lax.fori_loop(1, nb, step, 0)

    def batch_wait(kind, src_of, dst):
        def step(k, carry):
            other = lax.rem(bi + nb - k, nb)
            batch_copy(kind, k, src_of(lax.rem(bi + k, nb)), dst.at[other]).wait()
            return carry

        lax.fori_loop(1, nb, step, 0)

    def chan_copy(kind, k, src, dst):
        return pltpu.make_async_remote_copy(
            src_ref=src,
            dst_ref=dst,
            send_sem=chan_s.at[kind, k],
            recv_sem=chan_r.at[kind, k],
            device_id=chan_peer(k),
            device_id_type=MESH,
        )

    def chan_send(kind, src_of, dst):
        for k in range(1, 4):
            chan_copy(kind, k, src_of(lax.rem(ci + k, 4)), dst.at[ci]).start()

    def chan_wait(kind, src_of, dst):
        for k in range(1, 4):
            other = lax.rem(ci + 4 - k, 4)
            chan_copy(kind, k, src_of(lax.rem(ci + k, 4)), dst.at[other]).wait()

    def same(ref):
        return lambda other: ref

    stat_sc[0, bi] = stats_ref[...]
    batch_send(0, same(stats_ref), stat_sc.at[0])
    own_par[...] = jnp.zeros_like(own_par)
    for at, ref in enumerate((gain_in_ref, shift_in_ref, gain_mid_ref, shift_mid_ref)):
        own_par[at : at + 1, 0 : ref.shape[0]] = ref[...].astype(F32).reshape(1, ref.shape[0])
    par_sc[ci] = own_par[...]
    chan_send(0, same(own_par), par_sc)
    dnf_sc[...] = jnp.zeros_like(dnf_sc)
    for t in range(TAPS):
        dnf_sc[0:n_own, NEW_PAD * t : NEW_PAD * t + n_new] = wsp_in[t].astype(F32)
    wsp_sc[ci] = dnf_sc[:, 0 : TAPS * NEW_PAD].astype(BF16)
    wsp_own = same(wsp_sc.at[ci])
    chan_send(1, wsp_own, wsp_sc)

    for l in range(2):
        at = slice(128 * l, 128 * (l + 1))
        flat_sc[l, 0 : n_new * n_views, :] = dnew_ref[:, :, at].astype(F32).reshape(n_new * n_views, 128)
        for n in range(n_views):
            by_view = flat_sc[l, pl.ds(n, n_new, stride=n_views), :].astype(BF16)
            block, q = n // quarter, n % quarter
            dno_sc[block % 2, block // 2, q, :, at] = by_view
    dn_sc[0, ci] = dno_sc[c, y]
    dn_sc[1, ci] = dno_sc[c, 1 - y]
    dnew_of = lambda other: dno_sc.at[lax.rem(other, 2), other // 2]
    dfar_of = lambda other: dno_sc.at[lax.rem(other, 2), 1 - other // 2]
    chan_send(2, dnew_of, dn_sc.at[0])

    padc_sc[...] = jnp.zeros_like(padc_sc)
    padm_sc[...] = jnp.zeros_like(padm_sc)
    acc_sc[...] = jnp.zeros_like(acc_sc)
    accm_sc[...] = jnp.zeros_like(accm_sc)
    wg_sc[...] = jnp.zeros_like(wg_sc)
    wsg_sc[...] = jnp.zeros_like(wsg_sc)
    ext_sc[...] = jnp.zeros_like(ext_sc)
    ws_out[...] = jnp.zeros_like(ws_out)
    wr_out[...] = jnp.zeros_like(wr_out)
    wrt_sc[...] = jnp.zeros_like(wrt_sc)
    wrt_sc[0 : wr_in.shape[0], :] = wr_in[...]
    eye = (iota((n_in, n_in), 0) == iota((n_in, n_in), 1)).astype(BF16)
    wr_sc[...] = dot_nt(eye, wrt_sc[...]).astype(BF16)
    gain_row = two_rows(own_par[0:1, :])
    shift_row = two_rows(own_par[1:2, :])

    batch_wait(0, same(stats_ref), stat_sc.at[0])
    mean_row, dev_row = combine(stat_sc[0], local_count)
    rstd_row = lax.rsqrt(dev_row / pixels + EPS)
    row_to_cols(col_sc.at[0], mean_row)
    row_to_cols(col_sc.at[1], rstd_row)
    row_to_cols(col_sc.at[2], rstd_row * gain_row)
    row_to_cols(col_sc.at[3], shift_row)

    def wide(ref, at):
        col = ref[at]
        return jnp.concatenate([col, col], axis=1)

    def chunks(start=0, count=CELLS // CHUNK):
        if isinstance(start, int):
            return [slice(start + CHUNK * k, start + CHUNK * (k + 1)) for k in range(count)]
        return [pl.ds(pl.multiple_of(start + CHUNK * k, CHUNK), CHUNK) for k in range(count)]

    half = CELLS // 2

    def half_cols(h):
        return pl.ds(h * half if isinstance(h, int) else pl.multiple_of(h * half, half), half)

    def activate(n):
        mean, scale, shift = wide(col_sc, 0), wide(col_sc, 2), wide(col_sc, 3)
        for cols in chunks():
            pre = (x_sc[n, :, cols].astype(F32) - mean) * scale + shift
            s = sigmoid(pre)
            act = pre * s
            slope_sc[n, :, cols] = (s + act * (1.0 - s)).astype(BF16)
            act_sc[n, :, cols] = act.astype(BF16)

    def partial(n, cols):
        return dot(wrt_sc[...], act_sc[n, :, cols])

    def half_copy(i):
        return pltpu.make_async_remote_copy(
            src_ref=half_out.at[i],
            dst_ref=half_in.at[i],
            send_sem=half_s.at[i],
            recv_sem=half_r.at[i],
            device_id=mate,
            device_id_type=MESH,
        )

    def rest_copy(i):
        return pltpu.make_async_remote_copy(
            src_ref=pair_rest.at[i],
            dst_ref=far_rest.at[i],
            send_sem=rest_s.at[i],
            recv_sem=rest_r.at[i],
            device_id=across,
            device_id_type=MESH,
        )

    def unpack_rest(values):
        for k in range(CELLS // CHUNK):
            ext_sc[k, 0:REST, :] = values[REST * k : REST * (k + 1), :]

    def with_rest(main, k):
        return jnp.concatenate([main, ext_sc[k], jnp.zeros((8, CHUNK), F32)], axis=0)

    def far_start(i):
        rest_copy(i).start()
        far_copy(i, 0).start()
        far_copy(i, 1).start()

    def far_copy(i, h):
        return pltpu.make_async_remote_copy(
            src_ref=pair_sc.at[i, :, half_cols(h)],
            dst_ref=far_sc.at[i, :, half_cols(h)],
            send_sem=far_s.at[i, h],
            recv_sem=far_r.at[i, h],
            device_id=across,
            device_id_type=MESH,
        )

    def to_mate(i):
        theirs = slot_view(i, 1 - c)
        load(theirs).wait()
        activate(theirs)
        for cols in chunks():
            half_out[i, :, cols] = partial(theirs, cols)
        half_copy(i).start()

    def forward(i, carry):
        @pl.when(i < 2 * quarter - 1)
        def _():
            to_mate(i + 1)

        mine = slot_view(i, c)
        load(mine).wait()
        activate(mine)
        half_copy(i).wait_recv()
        for k, cols in enumerate(chunks()):
            both = partial(mine, cols) + half_in[i, :, cols]
            pair_sc[i, :, cols] = both[0:MAIN, :].astype(BF16)
            pack_sc[REST * k : REST * (k + 1), :] = both[MAIN : MAIN + REST, :]

            @pl.when(i >= quarter)
            def _():
                mid_sc[i - quarter, :, cols] = both

        pair_rest[i] = pack_sc[...].astype(BF16)

        @pl.when(i < quarter)
        def _():
            far_start(i)

        return carry

    to_mate(0)
    lax.fori_loop(0, 2 * quarter, forward, 0)

    chan_wait(1, wsp_own, wsp_sc)
    stacked = wsp_sc[...].reshape(4 * NEW_PAD, TAPS * NEW_PAD)
    lane, row = iota((MID_PAD, 4 * NEW_PAD), 1), iota((MID_PAD, 4 * NEW_PAD), 0)
    hit = None
    for b in range(4):
        inner = lane - NEW_PAD * b
        one = (inner >= 0) & (inner < n_own) & (row == inner + n_own * b)
        hit = one if hit is None else hit | one
    wb_sc[...] = dot(hit.astype(BF16), stacked).astype(BF16)
    taps_eye = iota((TAPS * NEW_PAD, TAPS * NEW_PAD), 0) == iota((TAPS * NEW_PAD, TAPS * NEW_PAD), 1)
    wf_sc[...] = dot_nt(taps_eye.astype(BF16), wb_sc[...]).astype(BF16)

    cell = iota((1, CELLS), 1)
    col_at, row_at = cell & (W - 1), cell >> 5

    def inside(values, row_step, col_step):
        ok = None
        if col_step != 0:
            ok = (col_at + col_step >= 0) & (col_at + col_step < W)
        if row_step != 0:
            on = (row_at + row_step >= 0) & (row_at + row_step < H)
            ok = on if ok is None else ok & on
        return values if ok is None else jnp.where(ok, values, 0.0)

    def at_offset(values, row_step, col_step):
        move = (-(W * row_step + col_step)) % CELLS
        rolled = values if move == 0 else pltpu.roll(values, move, 1)
        return inside(rolled, row_step, col_step)

    chan_wait(2, dnew_of, dn_sc.at[0])

    def back_slot(i, carry):
        far = jnp.where(i < quarter, 1, 0)
        keep = jnp.where(i < quarter, quarter, i - quarter)
        for b in range(4):
            dnf_sc[0:n_new, CHUNK * b : CHUNK * (b + 1)] = dn_sc[far, b, lax.rem(i, quarter)].astype(F32)
        grad = dnf_sc[...]
        for b in range(3):
            moved = at_offset(grad, 0, 1 - b)
            for a in range(3):
                t = 3 * a + b
                tap = at_offset(moved, 1 - a, 0)
                dcol_sc[keep, NEW_PAD * t : NEW_PAD * (t + 1), :] = tap.astype(BF16)
        for cols in chunks():
            d_sc[i, :, cols] = dot(wb_sc[...], dcol_sc[keep, :, cols])
        return carry

    lax.fori_loop(quarter, 2 * quarter, back_slot, 0)

    group = dpn_sc.shape[1]
    full = n_in // group

    def dp_load(k, rows):
        return pltpu.make_async_copy(
            dpass_hbm.at[pl.ds(k * group, rows)],
            dpn_sc.at[lax.rem(k, 2), pl.ds(0, rows)],
            dp_sem.at[lax.rem(k, 2)],
        )

    def dp_split(k, rows):
        first = k * group if isinstance(k, int) else pl.multiple_of(k * group, group)
        for l in range(CELLS // 128):
            at = slice(128 * l, 128 * (l + 1))
            native = dpn_sc[lax.rem(k, 2), 0:rows, :, at].astype(F32)
            for ch in range(rows):
                flat_sc[l, (n_views + 1) * ch : (n_views + 1) * ch + n_views, :] = native[ch]
            for n in range(n_views):
                by_view = flat_sc[l, pl.ds(n, rows, stride=n_views + 1), :]
                dp_sc[n, pl.ds(first, rows), at] = by_view.astype(BF16)

    left = n_in - full * group

    def dp_step(k, carry):
        @pl.when(k < full - 1)
        def _():
            dp_load(k + 1, group).start()

        dp_load(k, group).wait()
        dp_split(k, group)
        return carry

    dp_load(0, group).start()
    lax.fori_loop(0, full, dp_step, 0)
    if left > 0:
        dp_load(full, left).start()
        dp_load(full, left).wait()
        dp_split(full, left)

    chan_wait(0, same(own_par), par_sc)

    def gathered(at):
        total = None
        for b in range(4):
            piece = jnp.where(iota((8, 256), 1) < n_own, par_sc[b], 0.0)
            piece = piece if b == 0 else pltpu.roll(piece, n_own * b, 1)
            total = piece if total is None else total + piece
        return two_rows(total[at : at + 1, :])

    row_to_cols(colm_sc.at[2], gathered(2))
    row_to_cols(colm_sc.at[3], gathered(3))

    def middle_view(q):
        rest_copy(q).wait_recv()
        far_copy(q, 0).wait_recv()
        far_copy(q, 1).wait_recv()
        unpack_rest(far_rest[q].astype(F32))
        for k, cols in enumerate(chunks()):
            mid_sc[q, :, cols] = mid_sc[q, :, cols] + with_rest(far_sc[q, :, cols].astype(F32), k)

    def middle_sums(q, carry):
        @pl.when(q > 0)
        def _():
            middle_view(q)

        first, second = None, None
        for cols in chunks():
            part = mid_sc[q, :, cols] - wide(colm_sc, 7)
            one, two = lane_fold(part), lane_fold(part * part)
            first = one if first is None else first + one
            second = two if second is None else second + two
        accm_sc[0] += first
        accm_sc[1] += second
        return carry

    middle_view(0)
    pivot = sum(lane_fold(mid_sc[0, :, cols]) for cols in chunks())
    colm_sc[7] = jnp.broadcast_to(jnp.sum(pivot, axis=1, keepdims=True) / CELLS, colm_sc.shape[1:])
    pivot_row = cols_to_row(padm_sc, pivot) / CELLS
    lax.fori_loop(0, quarter, middle_sums, 0)
    off_row = cols_to_row(padm_sc, accm_sc[0]) / owned_count
    cmsg_sc[0] = jnp.zeros_like(cmsg_sc[0])
    cmsg_sc[0, 0:2, :] = pivot_row + off_row
    cmsg_sc[0, 2:4, :] = cols_to_row(padm_sc, accm_sc[1]) - off_row * off_row * owned_count
    accm_sc[...] = jnp.zeros_like(accm_sc)
    cstat_sc[0, ci] = cmsg_sc[0]
    chan_send(3, same(cmsg_sc.at[0]), cstat_sc.at[0])
    chan_send(7, dfar_of, dn_sc.at[1])
    far_start(quarter)
    chan_wait(3, same(cmsg_sc.at[0]), cstat_sc.at[0])
    group_mean, group_dev = combine(cstat_sc[0], owned_count)
    msg_sc[0] = jnp.zeros_like(msg_sc[0])
    msg_sc[0, 0:2, :] = group_mean
    msg_sc[0, 2:4, :] = group_dev
    stat_sc[1, bi] = msg_sc[0]
    batch_send(1, same(msg_sc.at[0]), stat_sc.at[1])
    chan_wait(7, dfar_of, dn_sc.at[1])
    lax.fori_loop(0, quarter, back_slot, 0)
    batch_wait(1, same(msg_sc.at[0]), stat_sc.at[1])
    meanm_row, devm_row = combine(stat_sc[1], local_count)
    rstdm_row = lax.rsqrt(devm_row / pixels + EPS)
    row_to_cols(colm_sc.at[0], meanm_row)
    row_to_cols(colm_sc.at[1], rstdm_row)

    def mid_point(values):
        mean, rstd = wide(colm_sc, 0), wide(colm_sc, 1)
        norm = (values - mean) * rstd
        pre = norm * wide(colm_sc, 2) + wide(colm_sc, 3)
        s = sigmoid(pre)
        act = pre * s
        return norm, act, s + act * (1.0 - s)

    def mid_own(q, carry):
        first, second = None, None
        for cols in chunks():
            norm, act, slope = mid_point(mid_sc[q, :, cols])
            actm_sc[q, :, cols] = act.astype(BF16)
            grad = d_sc[quarter + q, :, cols] * slope
            d_sc[quarter + q, :, cols] = grad
            mid_sc[q, :, cols] = norm
            one, two = lane_fold(grad), lane_fold(grad * norm)
            first = one if first is None else first + one
            second = two if second is None else second + two
        accm_sc[0] += first
        accm_sc[1] += second
        return carry

    lax.fori_loop(0, quarter, mid_own, 0)
    cmsg_sc[1] = jnp.zeros_like(cmsg_sc[1])
    cmsg_sc[1, 0:2, :] = cols_to_row(padm_sc, accm_sc[0])
    cmsg_sc[1, 2:4, :] = cols_to_row(padm_sc, accm_sc[1])
    cstat_sc[1, ci] = cmsg_sc[1]
    chan_send(4, same(cmsg_sc.at[1]), cstat_sc.at[1])
    for q in range(1, quarter):
        far_start(quarter + q)

    def tiles_of(ref):
        rows, cols = ref.shape
        return [(r, l, min(128, cols - 128 * l)) for r in range(rows // 16) for l in range(-(-cols // 128))]

    def scatter(refs, kind, values):
        out, back, _ = refs
        per = out.shape[1]
        for at, (r, l, width) in enumerate(tiles_of(values)):
            tile = values[16 * r : 16 * r + 16, 128 * l : 128 * l + width]
            out[at // per, at % per, :, 0:width] = tile.astype(BF16)
        back[bi] = out[bi]
        batch_send(kind, lambda other: out.at[other], back)

    def reduce_gather(refs, kind):
        out, back, whole = refs
        batch_wait(kind, lambda other: out.at[other], back)
        total = back[0].astype(F32)
        for at in range(1, nb):
            total = total + back[at].astype(F32)
        out[bi] = total.astype(BF16)
        whole[bi] = total.astype(BF16)
        batch_send(kind + 1, same(out.at[bi]), whole)

    def gather(refs, kind, ref):
        out, _, whole = refs
        per = out.shape[1]
        batch_wait(kind + 1, same(out.at[bi]), whole)
        for at, (r, l, width) in enumerate(tiles_of(ref)):
            tile = whole[at // per, at % per, :, 0:width]
            ref[16 * r : 16 * r + 16, 128 * l : 128 * l + width] = tile.astype(F32)

    spread_refs, reduce_refs = (ws_out, ws_in, ws_all), (wr_out, wr_back, wr_all)

    def spread_grad(q, carry):
        wsg_sc[...] += dot_nt(actm_sc[q], dcol_sc[q])
        return carry

    lax.fori_loop(0, quarter, spread_grad, 0)
    scatter(spread_refs, 4, wsg_sc)
    chan_wait(4, same(cmsg_sc.at[1]), cstat_sc.at[1])
    msg_sc[1] = (cstat_sc[1, 0] + cstat_sc[1, 1]) + (cstat_sc[1, 2] + cstat_sc[1, 3])
    stat_sc[2, bi] = msg_sc[1]
    batch_send(2, same(msg_sc.at[1]), stat_sc.at[2])
    def spread(q, carry):
        for k, cols in enumerate(chunks()):
            taps = dot(wf_sc[...], actm_sc[q, :, cols])
            for l in range(2):
                flat_sc[2 * k + l, 0 : TAPS * NEW_PAD, :] = taps[:, 128 * l : 128 * (l + 1)]
        total = None
        for b in range(3):
            column = None
            for a in range(3):
                t = 3 * a + b
                tap = [flat_sc[l, NEW_PAD * t : NEW_PAD * t + 40, :] for l in range(CELLS // 128)]
                tap = at_offset(jnp.concatenate(tap, axis=1), a - 1, 0)
                column = tap if column is None else column + tap
            column = at_offset(column, 0, b - 1)
            total = column if total is None else total + column
        for b in range(4):
            newo_sc[b, q] = total[0:n_new, CHUNK * b : CHUNK * (b + 1)].astype(BF16)
        return carry

    lax.fori_loop(0, quarter, spread, 0)
    new_of = lambda other: newo_sc.at[other]
    newi_sc[ci] = newo_sc[ci]
    reduce_gather(spread_refs, 4)
    batch_wait(2, same(msg_sc.at[1]), stat_sc.at[2])
    mid_sums = stat_sc[2, 0]
    for at in range(1, nb):
        mid_sums = mid_sums + stat_sc[2, at]
    row_to_cols(colm_sc.at[4], mid_sums[0:2, :] / pixels)
    row_to_cols(colm_sc.at[5], mid_sums[2:4, :] / pixels)
    row_to_cols(colm_sc.at[6], gathered(2) * rstdm_row)

    def dm_copy(i, h):
        return pltpu.make_async_remote_copy(
            src_ref=dm_out.at[i, :, half_cols(h)],
            dst_ref=dm_in.at[i, :, half_cols(h)],
            send_sem=dm_s.at[i, h],
            recv_sem=dm_r.at[i, h],
            device_id=mate,
            device_id_type=MESH,
        )

    def store(n):
        return pltpu.make_async_copy(slope_sc.at[n], dv_hbm.at[n], store_sem.at[n])

    def back_part(n, dm_ref, h):
        mean, rstd, scale = wide(col_sc, 0), wide(col_sc, 1), wide(col_sc, 2)
        first, second = None, None
        for cols in chunks(h * half, half // CHUNK):
            grad = dot(wr_sc[...], dm_ref[:, cols]) * slope_sc[n, :, cols].astype(F32)
            slope_sc[n, :, cols] = (grad * scale + dp_sc[n, :, cols].astype(F32)).astype(BF16)
            norm = (x_sc[n, :, cols].astype(F32) - mean) * rstd
            one, two = lane_fold(grad), lane_fold(grad * norm)
            first = one if first is None else first + one
            second = two if second is None else second + two
        acc_sc[0] += first
        acc_sc[1] += second
        cols = half_cols(h)
        wg_sc[:, 0:n_in] += dot_nt(dm_ref[:, cols], act_sc[n, :, cols])

    def dm_own(q, carry):
        i = quarter + q
        for cols in chunks():
            grad = d_sc[i, :, cols] - wide(colm_sc, 4) - mid_sc[q, :, cols] * wide(colm_sc, 5)
            dm_out[i, :, cols] = (grad * wide(colm_sc, 6)).astype(BF16)
        dm_copy(i, 0).start()
        dm_copy(i, 1).start()
        return carry

    lax.fori_loop(0, quarter, dm_own, 0)

    def back_mate(i, h):
        dm_copy(i, h).wait_recv()
        back_part(slot_view(i, 1 - c), dm_in.at[i], h)

    def back_own(t, carry):
        i, h = quarter + t // 2, lax.rem(t, 2)
        back_part(slot_view(i, c), dm_out.at[i], h)
        back_mate(i, h)
        return carry

    lax.fori_loop(0, 2 * quarter, back_own, 0)

    def back_far(t, carry):
        q, h = t // 2, lax.rem(t, 2)
        @pl.when(h == 0)
        def _():
            rest_copy(quarter + q).wait_recv()
            unpack_rest(pair_rest[q].astype(F32) + far_rest[quarter + q].astype(F32))

        far_copy(quarter + q, h).wait_recv()
        for k, cols in enumerate(chunks(h * half, half // CHUNK)):
            part = pair_sc[q, :, cols].astype(F32) + far_sc[quarter + q, :, cols].astype(F32)
            part = with_rest(part, half // CHUNK * h + k)
            norm, act, slope = mid_point(part)
            grad = d_sc[q, :, cols] * slope - wide(colm_sc, 4) - norm * wide(colm_sc, 5)
            dm_out[q, :, cols] = (grad * wide(colm_sc, 6)).astype(BF16)
        dm_copy(q, h).start()
        back_part(slot_view(q, c), dm_out.at[q], h)

        @pl.when(t > 0)
        def _():
            back_mate((t - 1) // 2, lax.rem(t + 1, 2))

        return carry

    lax.fori_loop(0, quarter, back_far, 0)
    gather(spread_refs, 4, wsg_sc)
    for b in range(4):
        wsp_sc[b, 0:40, :] = wsg_sc[n_own * b : n_own * b + 40, :].astype(BF16)
    wsgi_sc[ci] = wsp_sc[ci]
    wsg_of = lambda other: wsp_sc.at[other]
    chan_send(6, wsg_of, wsgi_sc)
    chan_send(5, new_of, newi_sc)
    lax.fori_loop(quarter, 2 * quarter, back_far, 0)
    back_mate(quarter - 1, 1)

    msg_sc[2] = jnp.zeros_like(msg_sc[2])
    msg_sc[2, 0:2, :] = cols_to_row(padc_sc, acc_sc[0])
    msg_sc[2, 2:4, :] = cols_to_row(padc_sc, acc_sc[1])
    stat_sc[3, bi] = msg_sc[2]
    batch_send(3, same(msg_sc.at[2]), stat_sc.at[3])
    scatter(reduce_refs, 6, wg_sc)
    batch_wait(3, same(msg_sc.at[2]), stat_sc.at[3])
    total = stat_sc[3, 0]
    for at in range(1, nb):
        total = total + stat_sc[3, at]
    gain_scale = gain_row * rstd_row
    row_to_cols(col_sc.at[4], -gain_scale * rstd_row * (total[2:4, :] / pixels))
    row_to_cols(col_sc.at[5], -gain_scale * (total[0:2, :] / pixels))
    reduce_gather(reduce_refs, 6)

    def finish(n, carry):
        mean, slant, level = wide(col_sc, 0), wide(col_sc, 4), wide(col_sc, 5)
        for cols in chunks():
            rest = (x_sc[n, :, cols].astype(F32) - mean) * slant + level
            slope_sc[n, :, cols] = (slope_sc[n, :, cols].astype(F32) + rest).astype(BF16)
        store(n).start()
        return carry

    lax.fori_loop(0, n_views, finish, 0)

    sums_ref[...] = jnp.zeros_like(sums_ref)
    sums_ref[0:1, :] = one_row(total[2:4, :])
    sums_ref[1:2, :] = one_row(total[0:2, :])
    all_sums = jnp.concatenate([one_row(mid_sums[2:4, :]), one_row(mid_sums[0:2, :]), jnp.zeros((6, 256), F32)], axis=0)
    own_sums = all_sums
    for b in range(1, 4):
        own_sums = jnp.where(ci == b, pltpu.roll(all_sums, 256 - n_own * b, 1), own_sums)
    sums_ref[2:4, :] = own_sums[0:2, :]

    chan_wait(5, new_of, newi_sc)
    for b in range(4):
        for q in range(quarter):
            new_ref[quarter * b + q] = newi_sc[b, q]
    chan_wait(6, wsg_of, wsgi_sc)
    wsg_total = (wsgi_sc[0].astype(F32) + wsgi_sc[1].astype(F32)) + (
        wsgi_sc[2].astype(F32) + wsgi_sc[3].astype(F32)
    )
    wsg_ref[...] = wsg_total[0:n_own, :]
    gather(reduce_refs, 6, wg_sc)
    wrg_ref[...] = wg_sc[0 : wrg_ref.shape[0], 0:n_in]

    def stored(n, carry):
        store(n).wait()
        return carry

    lax.fori_loop(0, n_views, stored, 0)

    def sent(i, carry):
        half_copy(i).wait_send()
        rest_copy(i).wait_send()
        for h in range(2):
            far_copy(i, h).wait_send()
            dm_copy(i, h).wait_send()
        return carry

    lax.fori_loop(0, 2 * quarter, sent, 0)


def layer(nb, views, stats, vectors, wr_t, w_spread, d_new, d_passed):
    n_views, n_in, _ = views.shape
    n_mid = wr_t.shape[0]
    n_own = n_mid // 4
    quarter = n_views // 4
    n_new = d_new.shape[0]
    n_cols = TAPS * NEW_PAD
    in_pad = -(-n_in // 16) * 16
    ws_tiles = -(-(MID_PAD // 16 * -(-n_cols // 128)) // nb)
    wr_tiles = -(-(MID_PAD // 16 * -(-in_pad // 128)) // nb)
    group = 16
    vmem = pl.BlockSpec(memory_space=pltpu.VMEM)
    anywhere = pl.BlockSpec(memory_space=pl.ANY)
    dma = pltpu.SemaphoreType.DMA
    slots = 2 * quarter
    return pl.pallas_call(
        functools.partial(layer_kernel, nb),
        in_specs=[anywhere] + [vmem] * 8 + [anywhere],
        out_specs=[anywhere, vmem, vmem, vmem, vmem],
        out_shape=[
            jax.ShapeDtypeStruct((n_views, n_in, CELLS), BF16),
            jax.ShapeDtypeStruct((n_views, n_new, CHUNK), BF16),
            jax.ShapeDtypeStruct((n_mid, n_in), F32),
            jax.ShapeDtypeStruct((n_own, n_cols), F32),
            jax.ShapeDtypeStruct((8, 256), F32),
        ],
        scratch_shapes=[
            pltpu.VMEM((n_views, n_in, CELLS), BF16),
            pltpu.VMEM((n_views, n_in, CELLS), BF16),
            pltpu.VMEM((n_views, n_in, CELLS), BF16),
            pltpu.VMEM((n_views, n_in, CELLS), BF16),
            pltpu.VMEM((slots, MID_PAD, CELLS), F32),
            pltpu.VMEM((slots, MID_PAD, CELLS), F32),
            pltpu.VMEM((slots, MAIN, CELLS), BF16),
            pltpu.VMEM((slots, MAIN, CELLS), BF16),
            pltpu.VMEM((slots, 16, CHUNK), BF16),
            pltpu.VMEM((slots, 16, CHUNK), BF16),
            pltpu.VMEM((16, CHUNK), F32),
            pltpu.VMEM((CELLS // CHUNK, 8, CHUNK), F32),
            pltpu.VMEM((slots, MID_PAD, CELLS), F32),
            pltpu.VMEM((quarter + 1, n_cols, CELLS), BF16),
            pltpu.VMEM((quarter, MID_PAD, CELLS), F32),
            pltpu.VMEM((quarter, MID_PAD, CELLS), BF16),
            pltpu.VMEM((slots, MID_PAD, CELLS), BF16),
            pltpu.VMEM((slots, MID_PAD, CELLS), BF16),
            pltpu.VMEM((2, 2, quarter, n_new, CHUNK), BF16),
            pltpu.VMEM((2, 4, quarter, n_new, CHUNK), BF16),
            pltpu.VMEM((NEW_PAD, CELLS), F32),
            pltpu.VMEM((2, group, n_views, CELLS), BF16),
            pltpu.VMEM((CELLS // 128, max(max(group, n_new) * n_views, n_cols), 128), F32),
            pltpu.VMEM((8, 256), F32),
            pltpu.VMEM((4, 8, 256), F32),
            pltpu.VMEM((4, NEW_PAD, n_cols), BF16),
            pltpu.VMEM((n_in, MID_PAD), BF16),
            pltpu.VMEM((MID_PAD, n_in), BF16),
            pltpu.VMEM((MID_PAD, n_cols), BF16),
            pltpu.VMEM((n_cols, MID_PAD), BF16),
            pltpu.VMEM((4, nb, 8, 128), F32),
            pltpu.VMEM((2, 4, 8, 128), F32),
            pltpu.VMEM((3, 8, 128), F32),
            pltpu.VMEM((2, 8, 128), F32),
            pltpu.VMEM((6, n_in, 128), F32),
            pltpu.VMEM((8, MID_PAD, 128), F32),
            pltpu.VMEM((256, 128), F32),
            pltpu.VMEM((256, 128), F32),
            pltpu.VMEM((2, n_in, 128), F32),
            pltpu.VMEM((2, MID_PAD, 128), F32),
            pltpu.VMEM((MID_PAD, in_pad), F32),
            pltpu.VMEM((MID_PAD, n_cols), F32),
            pltpu.VMEM((4, NEW_PAD, n_cols), BF16),
            pltpu.VMEM((nb, ws_tiles, 16, 128), BF16),
            pltpu.VMEM((nb, ws_tiles, 16, 128), BF16),
            pltpu.VMEM((nb, ws_tiles, 16, 128), BF16),
            pltpu.VMEM((nb, wr_tiles, 16, 128), BF16),
            pltpu.VMEM((nb, wr_tiles, 16, 128), BF16),
            pltpu.VMEM((nb, wr_tiles, 16, 128), BF16),
            pltpu.VMEM((4, quarter, n_new, CHUNK), BF16),
            pltpu.VMEM((4, quarter, n_new, CHUNK), BF16),
            dma((n_views,)),
            dma((n_views,)),
            dma((slots,)),
            dma((slots,)),
            dma((slots, 2)),
            dma((slots, 2)),
            dma((slots,)),
            dma((slots,)),
            dma((slots, 2)),
            dma((slots, 2)),
            dma((8, nb)),
            dma((8, nb)),
            dma((8, 4)),
            dma((8, 4)),
            dma((2,)),
        ],
        compiler_params=pltpu.CompilerParams(
            collective_id=0, has_side_effects=True, vmem_limit_bytes=VMEM_LIMIT
        ),
        name="layer",
    )(views, stats, *vectors, wr_t, w_spread, d_new, d_passed)


def solution(mesh):
    nb = mesh.shape["batch"]

    def on_device(features, crops, flips, gain_in, shift_in, w_reduce, gain_mid, shift_mid, w_spread, d_passed, d_new):
        n_own, n_new = w_spread.shape[0], w_spread.shape[3]

        w9 = jnp.transpose(w_spread, (1, 2, 0, 3)).reshape(TAPS, n_own, n_new)
        crops_t, flips_t = jnp.transpose(crops, (1, 2, 0)), jnp.transpose(flips)
        swap = lambda v: jnp.transpose(v, (1, 0, 2))
        views, passed, stats = crop_views(swap(features), crops_t, flips_t)
        dv, new_maps, wr_grad, ws_grad, sums = layer(
            nb, views, stats, (gain_in, shift_in, gain_mid, shift_mid), jnp.transpose(w_reduce), w9, swap(d_new), swap(d_passed)
        )
        features_grad, new_maps, wr_grad, ws_grad, *grads = place_views(
            crops_t, flips_t, dv, new_maps, wr_grad, ws_grad, sums
        )
        ws_grad = jnp.transpose(ws_grad.reshape(3, 3, n_own, n_new), (2, 0, 1, 3))
        return (swap(passed), swap(new_maps), swap(features_grad), jnp.transpose(wr_grad), ws_grad, *grads)

    return jax.shard_map(
        on_device,
        mesh=mesh,
        in_specs=(
            P("batch", "chan", None),
            P("batch", None, None),
            P("batch", None),
            P("chan"),
            P("chan"),
            P("chan", None),
            P("chan"),
            P("chan"),
            P("chan", None, None, None),
            P("batch", "chan", None),
            P("batch", None, "chan"),
        ),
        out_specs=(
            P("batch", "chan", None),
            P("batch", None, "chan"),
            P("batch", "chan", None),
            P("chan", None),
            P("chan", None, None, None),
            P("chan"),
            P("chan"),
            P("chan"),
            P("chan"),
        ),
        check_vma=False,
    )
```

```python
import functools

import jax
import jax.numpy as jnp
from jax import lax
from jax.experimental import pallas as pl
from jax.experimental.pallas import tpu as pltpu
from jax.sharding import PartitionSpec as P

H = 32
W = 32
MARGIN = 8
GRID = H + 2 * MARGIN
CELLS = H * W
EPS = 1e-05
CHUNK = 256
SPAN = 512
STRIDE = 8 * GRID
TAPS = 9
BLOCK = 80
MID_PAD = 144
NEW_PAD = 48
MAIN = 128
REST = 4
F32 = jnp.float32
BF16 = jnp.bfloat16
MESH = pl.DeviceIdType.MESH
VMEM_LIMIT = 63 * 2**20 + 800 * 2**10


def dot(a, b):
    return jnp.dot(a, b, preferred_element_type=F32)


def dot_nt(a, b):
    return lax.dot_general(a, b, (((1,), (1,)), ((), ())), preferred_element_type=F32)


def iota(shape, axis):
    return lax.broadcasted_iota(jnp.int32, shape, axis)


def lane_fold(values):
    total = values[:, 0:128]
    for at in range(128, values.shape[1], 128):
        total = total + values[:, at : at + 128]
    return total


def cols_to_row(pad_ref, values):
    if values is not None:
        pad_ref[0 : values.shape[0], :] = values
    halves = [
        jnp.sum(jnp.transpose(pad_ref[at : at + 128, :]), axis=0, keepdims=True)
        for at in (0, 128)
    ]
    return jnp.concatenate(halves, axis=0)


def two_rows(row):
    return jnp.concatenate([row[:, 0:128], row[:, 128:256]], axis=0)


def one_row(rows):
    return jnp.concatenate([rows[0:1, :], rows[1:2, :]], axis=1)


def row_to_cols(out_ref, row):
    rows = out_ref.shape[0]
    for h, at in enumerate((0, 128)):
        height = min(128, rows - at)
        square = jnp.broadcast_to(row[h : h + 1, :], (128, 128))
        out_ref[at : at + height, :] = jnp.transpose(square)[0:height, :]


def window_start(crops_ref, j, v):
    start = crops_ref[v, 0, j] * GRID + crops_ref[v, 1, j]
    base = jnp.minimum((start // 128) * 128, GRID * GRID - 3 * STRIDE - SPAN)
    return pl.multiple_of(base, 128), start - base


def chunk_target(offset, flip, cell):
    col = cell & (W - 1)
    row = cell >> 5
    return offset + row * GRID + jnp.where(flip > 0, W - 1 - col, col)


def blocks_of(channels):
    return [(at, min(BLOCK, channels - at)) for at in range(0, channels, BLOCK)]


def crop_kernel(crops_ref, flips_ref, x_hbm, views_hbm, passed_hbm, stats_ref, pick_sc, xn_sc, xf_sc, xi_sc, vw_sc, pf_sc, pn_sc, mean_sc, dev_sc, x_sem, vw_sem, pn_sem):
    channels, items, cells = x_hbm.shape
    n_views, rows, part_rows = 2 * items, BLOCK, 16
    blocks = blocks_of(channels)

    def load(at):
        first, size = blocks[at]
        return pltpu.make_async_copy(x_hbm.at[pl.ds(first, size)], xn_sc.at[at, pl.ds(0, size)], x_sem.at[at])

    def view_out(at, n):
        first = pl.multiple_of(at * rows, rows)
        return pltpu.make_async_copy(vw_sc.at[at, n], views_hbm.at[n, pl.ds(first, rows)], vw_sem.at[at, n])

    def passed_out(at, u):
        first, size = blocks[at]
        size = min(part_rows, size - part_rows * u)
        return pltpu.make_async_copy(
            pn_sc.at[at, pl.ds(part_rows * u, size)],
            passed_hbm.at[pl.ds(first + part_rows * u, size)],
            pn_sem.at[at, u],
        )

    for at in range(len(blocks)):
        load(at).start()

    def build(n, carry):
        j, v = n // 2, n % 2
        _, offset = window_start(crops_ref, j, v)
        target = chunk_target(offset, flips_ref[v, j], iota((1, CHUNK), 1))
        pick_sc[n] = (iota((SPAN, CHUNK), 0) == target).astype(BF16)
        return carry

    lax.fori_loop(0, n_views, build, 0)
    mean_sc[...] = jnp.zeros_like(mean_sc)
    dev_sc[...] = jnp.zeros_like(dev_sc)

    def block(b, carry):
        for at in range(len(blocks)):

            @pl.when(b == at)
            def _(at=at):
                load(at).wait()

        for l in range(cells // 128):
            at = slice(128 * l, 128 * (l + 1))
            wide_x = xn_sc[b, :, :, at].astype(F32)
            for ch in range(rows):
                xf_sc[l, (items + 1) * ch : (items + 1) * ch + items, :] = wide_x[ch]

        total = jnp.zeros((rows, 128), F32)
        squares = jnp.zeros((rows, 128), F32)
        pivot = None
        for j in range(items):
            for l in range(cells // 128):
                xi_sc[j, :, 128 * l : 128 * (l + 1)] = xf_sc[l, pl.ds(j, rows, stride=items + 1), :].astype(BF16)
            for v in range(2):
                n = 2 * j + v
                base, _ = window_start(crops_ref, j, v)
                spans = [xi_sc[j, :, pl.ds(pl.multiple_of(base + STRIDE * k, 128), SPAN)] for k in range(CELLS // CHUNK)]
                parts = dot(jnp.concatenate(spans, axis=0), pick_sc[n])
                for k in range(CELLS // CHUNK):
                    part = parts[rows * k : rows * (k + 1), :]
                    vw_sc[b, n, :, CHUNK * k : CHUNK * (k + 1)] = part.astype(BF16)
                    for l in range(2):
                        pf_sc[2 * k + l, pl.ds(n, rows, stride=n_views + 1), :] = part[:, 128 * l : 128 * (l + 1)]
                    if pivot is None:
                        pivot = jnp.sum(lane_fold(part), axis=1, keepdims=True) / CHUNK
                    off = part - pivot
                    total = total + lane_fold(off)
                    squares = squares + lane_fold(off * off)
                view_out(b, n).start()
        for u in range(rows // part_rows):
            for l in range(CELLS // 128):
                at = slice(128 * l, 128 * (l + 1))
                for ch in range(part_rows * u, part_rows * (u + 1)):
                    first = (n_views + 1) * ch
                    pn_sc[b, ch, :, at] = pf_sc[l, first : first + n_views, :].astype(BF16)
            for at in range(len(blocks)):

                @pl.when(b == at)
                def _(at=at):
                    passed_out(at, u).start()

        count = n_views * CELLS
        shift = jnp.sum(total, axis=1, keepdims=True) / count
        first = pl.multiple_of(b * rows, 8)
        lane = iota((rows, 128), 1)
        mean_sc[pl.ds(first, rows), :] = jnp.where(lane == 0, pivot + shift, 0.0)
        dev_sc[pl.ds(first, rows), :] = squares - jnp.where(lane == 0, shift * shift * count, 0.0)
        return carry

    lax.fori_loop(0, len(blocks), block, 0)
    stats_ref[...] = jnp.zeros_like(stats_ref)
    stats_ref[0:2, :] = cols_to_row(mean_sc, None)
    stats_ref[2:4, :] = cols_to_row(dev_sc, None)
    for at in range(len(blocks)):
        for n in range(n_views):
            view_out(at, n).wait()
        for u in range(rows // part_rows):
            passed_out(at, u).wait()


def crop_views(features, crops, flips):
    channels, items, cells = features.shape
    n_blocks = len(blocks_of(channels))
    anywhere = pl.BlockSpec(memory_space=pl.ANY)
    smem = pl.BlockSpec(memory_space=pltpu.SMEM)
    dma = pltpu.SemaphoreType.DMA
    return pl.pallas_call(
        crop_kernel,
        in_specs=[smem, smem, anywhere],
        out_specs=[anywhere, anywhere, pl.BlockSpec(memory_space=pltpu.VMEM)],
        out_shape=[
            jax.ShapeDtypeStruct((2 * items, n_blocks * BLOCK, CELLS), BF16),
            jax.ShapeDtypeStruct((channels, 2 * items, CELLS), BF16),
            jax.ShapeDtypeStruct((8, 128), F32),
        ],
        scratch_shapes=[
            pltpu.VMEM((2 * items, SPAN, CHUNK), BF16),
            pltpu.VMEM((n_blocks, BLOCK, items, cells), BF16),
            pltpu.VMEM((cells // 128, BLOCK * (items + 1), 128), F32),
            pltpu.VMEM((items, BLOCK, cells), BF16),
            pltpu.VMEM((n_blocks, 2 * items, BLOCK, CELLS), BF16),
            pltpu.VMEM((CELLS // 128, BLOCK * (2 * items + 1), 128), F32),
            pltpu.VMEM((n_blocks, BLOCK, 2 * items, CELLS), BF16),
            pltpu.VMEM((256, 128), F32),
            pltpu.VMEM((256, 128), F32),
            dma((n_blocks,)),
            dma((n_blocks, 2 * items)),
            dma((n_blocks, BLOCK // 16)),
        ],
        compiler_params=pltpu.CompilerParams(vmem_limit_bytes=VMEM_LIMIT),
        name="crop_views",
    )(crops, flips, features)


def place_kernel(crops_ref, flips_ref, dv_hbm, new_ref, wrg_ref, wsg_ref, sums_ref, out_hbm, newo_ref, wrgo_ref, wsgo_ref, gi_ref, si_ref, gm_ref, sm_ref, pick_sc, dv_sc, flat_sc, out_sc, new_sc, dv_sem, out_sem):
    channels, items, cells = out_hbm.shape
    n_views, rows, part_rows = 2 * items, BLOCK, 16
    blocks = blocks_of(channels)

    def load(at):
        first = at * rows if isinstance(at, int) else pl.multiple_of(at * rows, rows)
        return pltpu.make_async_copy(dv_hbm.at[:, pl.ds(first, rows)], dv_sc.at[at], dv_sem.at[at])

    def out(at, u):
        first, size = blocks[at]
        size = min(part_rows, size - part_rows * u)
        return pltpu.make_async_copy(
            out_sc.at[at, pl.ds(part_rows * u, size)],
            out_hbm.at[pl.ds(first + part_rows * u, size)],
            out_sem.at[at, u],
        )

    for at in range(len(blocks)):
        load(at).start()

    def build(n, carry):
        j, v = n // 2, n % 2
        _, offset = window_start(crops_ref, j, v)
        target = chunk_target(offset, flips_ref[v, j], iota((CHUNK, 1), 0))
        pick_sc[n] = (iota((CHUNK, SPAN), 1) == target).astype(BF16)
        return carry

    lax.fori_loop(0, n_views, build, 0)

    def block(b, carry):
        load(b).wait()
        flat_sc[...] = jnp.zeros_like(flat_sc)

        def place_item(j):
            for v in range(2):
                n = 2 * j + v
                base, _ = window_start(crops_ref, j, v)
                tile = base // 128
                parts = [dv_sc[b, n, :, CHUNK * k : CHUNK * (k + 1)] for k in range(CELLS // CHUNK)]
                spans = dot(jnp.concatenate(parts, axis=0), pick_sc[n])
                spans = [spans[rows * k : rows * (k + 1), :] for k in range(CELLS // CHUNK)]
                pieces = [spans[0][:, 0:STRIDE]]
                for k in range(1, CELLS // CHUNK):
                    pieces.append(spans[k - 1][:, STRIDE:SPAN] + spans[k][:, 0 : SPAN - STRIDE])
                    pieces.append(spans[k][:, SPAN - STRIDE : STRIDE])
                pieces.append(spans[-1][:, STRIDE:SPAN])
                window = jnp.concatenate(pieces, axis=1)
                of_item = pl.ds(j, rows, stride=items + 1)
                for t in range(window.shape[1] // 128):
                    piece = window[:, 128 * t : 128 * (t + 1)]
                    if v == 1:
                        piece = piece + flat_sc[tile + t, of_item, :]
                    flat_sc[tile + t, of_item, :] = piece

        def place_some(group, carry):
            for inner in range(4):
                place_item(4 * group + inner)
            return carry

        lax.fori_loop(0, items // 4, place_some, 0)
        for u in range(rows // part_rows):
            for l in range(cells // 128):
                for ch in range(part_rows * u, part_rows * (u + 1)):
                    first = (items + 1) * ch
                    out_sc[b, ch, :, 128 * l : 128 * (l + 1)] = flat_sc[l, first : first + items, :]
            for at in range(len(blocks)):

                @pl.when(b == at)
                def _(at=at):
                    out(at, u).start()

        return carry

    lax.fori_loop(0, len(blocks), block, 0)

    n_new = new_ref.shape[1]
    for n in range(n_views):
        for l in range(2):
            piece = new_ref[n, :, 128 * l : 128 * (l + 1)]
            new_sc[l, pl.ds(n, n_new, stride=n_views), :] = piece.astype(F32)
    for l in range(2):
        newo_ref[:, :, 128 * l : 128 * (l + 1)] = new_sc[l].reshape(n_new, n_views, 128).astype(BF16)
    wrgo_ref[...] = wrg_ref[...]
    for t in range(TAPS):
        wsgo_ref[t] = wsg_ref[:, NEW_PAD * t : NEW_PAD * t + wsgo_ref.shape[2]]
    for at, ref in enumerate((gi_ref, si_ref, gm_ref, sm_ref)):
        ref[...] = sums_ref[at, 0 : ref.shape[0]]
    for at in range(len(blocks)):
        for u in range(rows // part_rows):
            out(at, u).wait()


def place_views(crops, flips, dv, new_maps, wr_grad, ws_grad, sums):
    items, channels = crops.shape[2], wr_grad.shape[1]
    n_views, n_blocks = dv.shape[0], dv.shape[1] // BLOCK
    n_new, n_own = new_maps.shape[1], ws_grad.shape[0]
    cells = GRID * GRID
    anywhere = pl.BlockSpec(memory_space=pl.ANY)
    vmem = pl.BlockSpec(memory_space=pltpu.VMEM)
    smem = pl.BlockSpec(memory_space=pltpu.SMEM)
    dma = pltpu.SemaphoreType.DMA
    small = [
        ((n_new, n_views, CHUNK), BF16),
        (wr_grad.shape, F32),
        ((TAPS, n_own, n_new), F32),
        ((channels,), F32),
        ((channels,), F32),
        ((n_own,), F32),
        ((n_own,), F32),
    ]
    return pl.pallas_call(
        place_kernel,
        in_specs=[smem, smem, anywhere] + [vmem] * 4,
        out_specs=[anywhere] + [vmem] * len(small),
        out_shape=[jax.ShapeDtypeStruct((channels, items, cells), F32)]
        + [jax.ShapeDtypeStruct(shape, kind) for shape, kind in small],
        scratch_shapes=[
            pltpu.VMEM((n_views, CHUNK, SPAN), BF16),
            pltpu.VMEM((n_blocks, n_views, BLOCK, CELLS), BF16),
            pltpu.VMEM((cells // 128, BLOCK * (items + 1), 128), F32),
            pltpu.VMEM((n_blocks, BLOCK, items, cells), F32),
            pltpu.VMEM((2, n_new * n_views, 128), F32),
            dma((n_blocks,)),
            dma((n_blocks, BLOCK // 16)),
        ],
        compiler_params=pltpu.CompilerParams(vmem_limit_bytes=VMEM_LIMIT),
        name="place_views",
    )(crops, flips, dv, new_maps, wr_grad, ws_grad, sums)


def sigmoid(v):
    return 0.5 * jnp.tanh(0.5 * v) + 0.5


def combine(parts, count):
    groups = parts.shape[0]
    mean = parts[0, 0:2, :]
    dev = parts[0, 2:4, :]
    for at in range(1, groups):
        mean = mean + parts[at, 0:2, :]
        dev = dev + parts[at, 2:4, :]
    mean = mean / groups
    spread = None
    for at in range(groups):
        off = parts[at, 0:2, :] - mean
        spread = off * off if spread is None else spread + off * off
    return mean, dev + spread * count


def layer_kernel(
    nb,
    crops_ref,
    flips_ref,
    views_hbm,
    stats_ref,
    gain_in_ref,
    shift_in_ref,
    gain_mid_ref,
    shift_mid_ref,
    wr_in,
    wsp_in,
    dnew_ref,
    dpass_hbm,
    dv_hbm,
    new_ref,
    wrg_ref,
    wsg_ref,
    sums_ref,
    x_sc,
    act_sc,
    slope_sc,
    dp_sc,
    half_out,
    half_in,
    pair_sc,
    far_sc,
    pair_rest,
    far_rest,
    pack_sc,
    ext_sc,
    packed_sc,
    find_sc,
    join_sc,
    d_sc,
    dcol_sc,
    mid_sc,
    actm_sc,
    dm_out,
    dm_in,
    dno_sc,
    dn_sc,
    pack_dn,
    dnf_sc,
    dpn_sc,
    flat_sc,
    own_par,
    par_sc,
    wsp_sc,
    wr_sc,
    wrt_sc,
    wb_sc,
    wf_sc,
    stat_sc,
    cstat_sc,
    msg_sc,
    cmsg_sc,
    col_sc,
    colm_sc,
    padc_sc,
    padm_sc,
    acc_sc,
    accm_sc,
    wg_sc,
    wsg_sc,
    wsgi_sc,
    ws_out,
    ws_in,
    ws_all,
    wr_out,
    wr_back,
    wr_all,
    newo_sc,
    newi_sc,
    load_sem,
    store_sem,
    half_s,
    half_r,
    far_s,
    far_r,
    rest_s,
    rest_r,
    dm_s,
    dm_r,
    bat_s,
    bat_r,
    chan_s,
    chan_r,
    dp_sem,
):
    bi, ci = lax.axis_index("batch"), lax.axis_index("chan")
    y, c = ci // 2, lax.rem(ci, 2)
    n_views, n_in = x_sc.shape[0], act_sc.shape[1]
    quarter = n_views // 4
    n_own, n_new = wsg_ref.shape[0], dnew_ref.shape[0]
    local_count = float(n_views * CELLS)
    owned_count = float(quarter * CELLS)
    pixels = float(nb) * local_count
    mate = (bi, 2 * y + (1 - c))
    across = (bi, 2 * (1 - y) + c)

    def batch_peer(k):
        return (lax.rem(bi + k, nb), ci)

    def chan_peer(k):
        return (bi, lax.rem(ci + k, 4))

    barrier = pltpu.get_barrier_semaphore()

    def greet(k, carry):
        pl.semaphore_signal(barrier, inc=1, device_id=batch_peer(k), device_id_type=MESH)
        return carry

    lax.fori_loop(1, nb, greet, 0)
    for k in range(1, 4):
        pl.semaphore_signal(barrier, inc=1, device_id=chan_peer(k), device_id_type=MESH)

    def load(n):
        return pltpu.make_async_copy(views_hbm.at[n], x_sc.at[n], load_sem.at[n])

    def load_step(i, carry):
        load(slot_view(i, 1 - c)).start()
        load(slot_view(i, c)).start()
        return carry

    def slot_view(i, core):
        h = jnp.where(i < quarter, 1 - y, y)
        return quarter * (2 * h + core) + lax.rem(i, quarter)

    lax.fori_loop(0, 2 * quarter, load_step, 0)
    pl.semaphore_wait(barrier, nb + 2)

    def batch_copy(kind, k, src, dst):
        return pltpu.make_async_remote_copy(
            src_ref=src,
            dst_ref=dst,
            send_sem=bat_s.at[kind, k],
            recv_sem=bat_r.at[kind, k],
            device_id=batch_peer(k),
            device_id_type=MESH,
        )

    def batch_send(kind, src_of, dst):
        def step(k, carry):
            batch_copy(kind, k, src_of(lax.rem(bi + k, nb)), dst.at[bi]).start()
            return carry

        lax.fori_loop(1, nb, step, 0)

    def batch_wait(kind, src_of, dst):
        def step(k, carry):
            other = lax.rem(bi + nb - k, nb)
            batch_copy(kind, k, src_of(lax.rem(bi + k, nb)), dst.at[other]).wait()
            return carry

        lax.fori_loop(1, nb, step, 0)

    def chan_copy(kind, k, src, dst):
        return pltpu.make_async_remote_copy(
            src_ref=src,
            dst_ref=dst,
            send_sem=chan_s.at[kind, k],
            recv_sem=chan_r.at[kind, k],
            device_id=chan_peer(k),
            device_id_type=MESH,
        )

    def chan_send(kind, src_of, dst):
        for k in range(1, 4):
            chan_copy(kind, k, src_of(lax.rem(ci + k, 4)), dst.at[ci]).start()

    def chan_wait(kind, src_of, dst):
        for k in range(1, 4):
            other = lax.rem(ci + 4 - k, 4)
            chan_copy(kind, k, src_of(lax.rem(ci + k, 4)), dst.at[other]).wait()

    def wide(ref, at):
        col = ref[at]
        return jnp.concatenate([col, col], axis=1)

    def same(ref):
        return lambda other: ref

    stat_sc[0, bi] = stats_ref[...]
    batch_send(0, same(stats_ref), stat_sc.at[0])
    own_par[...] = jnp.zeros_like(own_par)
    for at, ref in enumerate((gain_in_ref, shift_in_ref, gain_mid_ref, shift_mid_ref)):
        own_par[at : at + 1, 0 : ref.shape[0]] = ref[...].astype(F32).reshape(1, ref.shape[0])
    par_sc[ci] = own_par[...]
    chan_send(0, same(own_par), par_sc)
    dnf_sc[...] = jnp.zeros_like(dnf_sc)
    for t in range(TAPS):
        dnf_sc[0:n_own, NEW_PAD * t : NEW_PAD * t + n_new] = wsp_in[t].astype(F32)
    wsp_sc[ci] = dnf_sc[:, 0 : TAPS * NEW_PAD].astype(BF16)
    wsp_own = same(wsp_sc.at[ci])
    chan_send(1, wsp_own, wsp_sc)

    pack_dn[...] = jnp.zeros_like(pack_dn)
    for l in range(2):
        at = slice(128 * l, 128 * (l + 1))
        native = dnew_ref[:, :, at].astype(F32)
        for ch in range(n_new):
            flat_sc[l, (n_views + 1) * ch : (n_views + 1) * ch + n_views, :] = native[ch]
        for block in range(4):
            for q in range(quarter):
                by_view = flat_sc[l, pl.ds(quarter * block + q, n_new, stride=n_views + 1), :]
                pack_dn[n_new * q : n_new * (q + 1), :] = by_view
            dno_sc[block % 2, block // 2, :, at] = pack_dn[...].astype(BF16)
    dn_sc[0, ci] = dno_sc[c, y]
    dn_sc[1, ci] = dno_sc[c, 1 - y]
    dnew_of = lambda other: dno_sc.at[lax.rem(other, 2), other // 2]
    dfar_of = lambda other: dno_sc.at[lax.rem(other, 2), 1 - other // 2]
    chan_send(2, dnew_of, dn_sc.at[0])

    padc_sc[...] = jnp.zeros_like(padc_sc)
    padm_sc[...] = jnp.zeros_like(padm_sc)
    acc_sc[...] = jnp.zeros_like(acc_sc)
    accm_sc[...] = jnp.zeros_like(accm_sc)
    wg_sc[...] = jnp.zeros_like(wg_sc)
    wsg_sc[...] = jnp.zeros_like(wsg_sc)
    ext_sc[...] = jnp.zeros_like(ext_sc)
    piece, place = iota((CELLS // 2, CELLS // 2), 0), iota((CELLS // 2, CELLS // 2), 1)
    joined_at = ((piece & 255) >> 4) * W + (piece >> 8) * 16 + (piece & 15)
    join_sc[...] = (joined_at == place).astype(BF16)
    ws_out[...] = jnp.zeros_like(ws_out)
    wr_out[...] = jnp.zeros_like(wr_out)
    wrt_sc[...] = jnp.zeros_like(wrt_sc)
    wrt_sc[0 : wr_in.shape[0], :] = wr_in[...]
    eye = (iota((n_in, n_in), 0) == iota((n_in, n_in), 1)).astype(BF16)
    wr_sc[...] = dot_nt(eye, wrt_sc[...]).astype(BF16)
    gain_row = two_rows(own_par[0:1, :])
    shift_row = two_rows(own_par[1:2, :])

    gain_col, shift_col = (jnp.transpose(jnp.broadcast_to(one_row(v), (256, 256)))[0:n_in, 0:128] for v in (gain_row, shift_row))
    guess = None
    for weight, offset in ((2 / 3, 0.0), (1 / 6, 3.0**0.5), (1 / 6, -(3.0**0.5))):
        pre = shift_col + offset * gain_col
        part = weight * pre * sigmoid(pre)
        guess = part if guess is None else guess + part
    colm_sc[7] = dot(wrt_sc[...], guess.astype(BF16))

    batch_wait(0, same(stats_ref), stat_sc.at[0])
    mean_row, dev_row = combine(stat_sc[0], local_count)
    rstd_row = lax.rsqrt(dev_row / pixels + EPS)
    row_to_cols(col_sc.at[0], mean_row)
    row_to_cols(col_sc.at[1], rstd_row)
    row_to_cols(col_sc.at[2], rstd_row * gain_row)
    row_to_cols(col_sc.at[3], shift_row)

    def chunks(start=0, count=CELLS // CHUNK):
        if isinstance(start, int):
            return [slice(start + CHUNK * k, start + CHUNK * (k + 1)) for k in range(count)]
        return [pl.ds(pl.multiple_of(start + CHUNK * k, CHUNK), CHUNK) for k in range(count)]

    half = CELLS // 2

    def half_cols(h):
        return pl.ds(h * half if isinstance(h, int) else pl.multiple_of(h * half, half), half)

    def activate(n):
        mean, scale, shift = wide(col_sc, 0), wide(col_sc, 2), wide(col_sc, 3)
        for cols in chunks():
            pre = (x_sc[n, 0:n_in, cols].astype(F32) - mean) * scale + shift
            s = sigmoid(pre)
            act = pre * s
            slope_sc[n, 0:n_in, cols] = (s + act * (1.0 - s)).astype(BF16)
            act_sc[n, :, cols] = act.astype(BF16)

    def partial(n, cols):
        return dot(wrt_sc[...], act_sc[n, :, cols]) - wide(colm_sc, 7)

    def half_copy(i):
        return pltpu.make_async_remote_copy(
            src_ref=half_out.at[i],
            dst_ref=half_in.at[i],
            send_sem=half_s.at[i],
            recv_sem=half_r.at[i],
            device_id=mate,
            device_id_type=MESH,
        )

    def rest_copy(i):
        return pltpu.make_async_remote_copy(
            src_ref=pair_rest.at[i],
            dst_ref=far_rest.at[i],
            send_sem=rest_s.at[i],
            recv_sem=rest_r.at[i],
            device_id=across,
            device_id_type=MESH,
        )

    def unpack_rest(values):
        for k in range(CELLS // CHUNK):
            ext_sc[k, 0:REST, :] = values[REST * k : REST * (k + 1), :]

    def with_rest(main, k):
        return jnp.concatenate([main, ext_sc[k], jnp.zeros((8, CHUNK), F32)], axis=0)

    def quarter_of(i):
        j = slot_view(i, c) // 2
        row_half = jnp.where(crops_ref[1, 0, j] >= crops_ref[0, 0, j], 0, 1)
        col_half = jnp.where(crops_ref[1, 1, j] >= crops_ref[0, 1, j], 0, 1)
        return j, row_half, jnp.where(flips_ref[1, j] > 0, 1 - col_half, col_half)

    def arriving(m):
        return lax.rem(2 * m + quarter, 2 * quarter)

    def find_quarter(m, carry):
        j, row_half, col_half = quarter_of(arriving(m))
        cell = iota((1, CHUNK), 1)
        row, col = (cell >> 4) + 16 * row_half, (cell & 15) + 16 * col_half
        col = jnp.where(flips_ref[1, j] > 0, W - 1 - col, col)
        row = row + crops_ref[1, 0, j] - crops_ref[0, 0, j]
        col = col + crops_ref[1, 1, j] - crops_ref[0, 1, j]
        col = jnp.where(flips_ref[0, j] > 0, W - 1 - col, col)
        find_sc[m] = (iota((CELLS, CHUNK), 0) == row * W + col).astype(BF16)
        return carry

    def pack_second(m):
        _, row_half, col_half = quarter_of(2 * m)
        low, high = pair_sc[2 * m + 1, :, 0:half], pair_sc[2 * m + 1, :, half:CELLS]
        columns = dot_nt(jnp.where(row_half == 0, low, high), join_sc[...])
        kept = jnp.where(col_half == 0, columns[:, CHUNK:half], columns[:, 0:CHUNK])
        packed_sc[m, :, 0:half] = jnp.where(row_half == 0, high, low)
        packed_sc[m, :, half : half + CHUNK] = kept.astype(BF16)

    def unpack_second(m):
        far_copy(m, 1, 0).wait_recv()
        far_copy(m, 1, 1).wait_recv()
        _, row_half, col_half = quarter_of(arriving(m))
        whole = far_sc[2 * m + 1, :, 0:half]
        kept = far_sc[2 * m + 1, :, half : half + CHUNK]
        found = dot(far_sc[2 * m], find_sc[m]).astype(BF16)
        left, right = jnp.where(col_half == 0, found, kept), jnp.where(col_half == 0, kept, found)
        joined = dot(jnp.concatenate([left, right], axis=1), join_sc[...]).astype(BF16)
        far_sc[2 * m + 1, :, 0:half] = jnp.where(row_half == 0, joined, whole)
        far_sc[2 * m + 1, :, half:CELLS] = jnp.where(row_half == 0, whole, joined)

    def far_start(m, v):
        rest_copy(2 * m + v).start()
        far_copy(m, v, 0).start()
        far_copy(m, v, 1).start()

    def far_copy(m, v, h):
        i = 2 * m + v
        if v == 0:
            cols = half_cols(h)
            src = pair_sc.at[i, :, cols]
        else:
            cols = pl.ds(half * h, half if h == 0 else CHUNK)
            src = packed_sc.at[m, :, cols]
        return pltpu.make_async_remote_copy(
            src_ref=src,
            dst_ref=far_sc.at[i, :, cols],
            send_sem=far_s.at[i, h],
            recv_sem=far_r.at[i, h],
            device_id=across,
            device_id_type=MESH,
        )

    def to_mate(i):
        theirs = slot_view(i, 1 - c)
        load(theirs).wait()
        activate(theirs)
        for cols in chunks():
            half_out[i, :, cols] = partial(theirs, cols).astype(BF16)
        half_copy(i).start()

    def forward(m, carry):
        for v in range(2):
            i = 2 * m + v

            @pl.when(i < 2 * quarter - 1)
            def _():
                to_mate(i + 1)

            mine = slot_view(i, c)
            load(mine).wait()
            activate(mine)
            half_copy(i).wait_recv()
            for k, cols in enumerate(chunks()):
                both = partial(mine, cols) + half_in[i, :, cols].astype(F32)
                pair_sc[i, :, cols] = both[0:MAIN, :].astype(BF16)
                pack_sc[REST * k : REST * (k + 1), :] = both[MAIN : MAIN + REST, :]

                @pl.when(i >= quarter)
                def _():
                    mid_sc[i - quarter, :, cols] = both

            pair_rest[i] = pack_sc[...].astype(BF16)
            if v == 1:
                pack_second(m)

            @pl.when(i < quarter)
            def _():
                far_start(m, v)

        return carry

    to_mate(0)
    lax.fori_loop(0, quarter, forward, 0)
    lax.fori_loop(0, quarter, find_quarter, 0)

    chan_wait(1, wsp_own, wsp_sc)
    stacked = wsp_sc[...].reshape(4 * NEW_PAD, TAPS * NEW_PAD)
    lane, row = iota((MID_PAD, 4 * NEW_PAD), 1), iota((MID_PAD, 4 * NEW_PAD), 0)
    hit = None
    for b in range(4):
        inner = lane - NEW_PAD * b
        one = (inner >= 0) & (inner < n_own) & (row == inner + n_own * b)
        hit = one if hit is None else hit | one
    wb_sc[...] = dot(hit.astype(BF16), stacked).astype(BF16)
    taps_eye = iota((TAPS * NEW_PAD, TAPS * NEW_PAD), 0) == iota((TAPS * NEW_PAD, TAPS * NEW_PAD), 1)
    wf_sc[...] = dot_nt(taps_eye.astype(BF16), wb_sc[...]).astype(BF16)

    cell = iota((1, CELLS), 1)
    col_at, row_at = cell & (W - 1), cell >> 5

    def inside(values, row_step, col_step):
        ok = None
        if col_step != 0:
            ok = (col_at + col_step >= 0) & (col_at + col_step < W)
        if row_step != 0:
            on = (row_at + row_step >= 0) & (row_at + row_step < H)
            ok = on if ok is None else ok & on
        return values if ok is None else jnp.where(ok, values, 0.0)

    def at_offset(values, row_step, col_step):
        move = (-(W * row_step + col_step)) % CELLS
        rolled = values if move == 0 else pltpu.roll(values, move, 1)
        return inside(rolled, row_step, col_step)

    chan_wait(2, dnew_of, dn_sc.at[0])

    def back_slot(i, carry):
        far = jnp.where(i < quarter, 1, 0)
        keep = jnp.where(i < quarter, quarter, i - quarter)
        for b in range(4):
            for l in range(2):
                pack_dn[...] = dn_sc[far, b, :, 128 * l : 128 * (l + 1)].astype(F32)
                at = CHUNK * b + 128 * l
                dnf_sc[0:n_new, at : at + 128] = pack_dn[pl.ds(n_new * lax.rem(i, quarter), n_new), :]
        grad = dnf_sc[...]
        for b in range(3):
            moved = at_offset(grad, 0, 1 - b)
            for a in range(3):
                t = 3 * a + b
                tap = at_offset(moved, 1 - a, 0)
                dcol_sc[keep, NEW_PAD * t : NEW_PAD * (t + 1), :] = tap.astype(BF16)
        for cols in chunks():
            d_sc[i, :, cols] = dot(wb_sc[...], dcol_sc[keep, :, cols])
        return carry

    lax.fori_loop(quarter, 2 * quarter, back_slot, 0)

    group = dpn_sc.shape[1]
    full = n_in // group

    def dp_load(k, rows):
        return pltpu.make_async_copy(
            dpass_hbm.at[pl.ds(k * group, rows)],
            dpn_sc.at[lax.rem(k, 2), pl.ds(0, rows)],
            dp_sem.at[lax.rem(k, 2)],
        )

    def dp_split(k, rows):
        first = k * group if isinstance(k, int) else pl.multiple_of(k * group, group)
        for l in range(CELLS // 128):
            at = slice(128 * l, 128 * (l + 1))
            native = dpn_sc[lax.rem(k, 2), 0:rows, :, at].astype(F32)
            for ch in range(rows):
                flat_sc[l, (n_views + 1) * ch : (n_views + 1) * ch + n_views, :] = native[ch]
            for n in range(n_views):
                by_view = flat_sc[l, pl.ds(n, rows, stride=n_views + 1), :]
                dp_sc[n, pl.ds(first, rows), at] = by_view.astype(BF16)

    left = n_in - full * group

    def dp_step(k, carry):
        @pl.when(k < full - 1)
        def _():
            dp_load(k + 1, group).start()

        dp_load(k, group).wait()
        dp_split(k, group)
        return carry

    def dp_some(first, last):
        lax.fori_loop(first, last, dp_step, 0)

    early = full - 2
    dp_load(0, group).start()
    dp_some(0, early)

    chan_wait(0, same(own_par), par_sc)

    def gathered(at):
        total = None
        for b in range(4):
            piece = jnp.where(iota((8, 256), 1) < n_own, par_sc[b], 0.0)
            piece = piece if b == 0 else pltpu.roll(piece, n_own * b, 1)
            total = piece if total is None else total + piece
        return two_rows(total[at : at + 1, :])

    row_to_cols(colm_sc.at[2], gathered(2))
    row_to_cols(colm_sc.at[3], gathered(3))

    def middle_view(q, first):
        rest_copy(q).wait_recv()

        def arrive_first():
            far_copy(q // 2, 0, 0).wait_recv()
            far_copy(q // 2, 0, 1).wait_recv()

        if first:
            arrive_first()
        else:
            pl.when(lax.rem(q, 2) == 0)(arrive_first)

            @pl.when(lax.rem(q, 2) == 1)
            def _():
                unpack_second(q // 2)

        unpack_rest(far_rest[q].astype(F32))
        for k, cols in enumerate(chunks()):
            mid_sc[q, :, cols] = mid_sc[q, :, cols] + with_rest(far_sc[q, :, cols].astype(F32), k)

    def middle_sums(q, carry):
        @pl.when(q > 0)
        def _():
            middle_view(q, False)

        first, second = None, None
        for cols in chunks():
            part = mid_sc[q, :, cols] - wide(colm_sc, 8)
            one, two = lane_fold(part), lane_fold(part * part)
            first = one if first is None else first + one
            second = two if second is None else second + two
        accm_sc[0] += first
        accm_sc[1] += second
        return carry

    middle_view(0, True)
    pivot = sum(lane_fold(mid_sc[0, :, cols]) for cols in chunks())
    colm_sc[8] = jnp.broadcast_to(jnp.sum(pivot, axis=1, keepdims=True) / CELLS, colm_sc.shape[1:])
    pivot_row = cols_to_row(padm_sc, pivot) / CELLS
    lax.fori_loop(0, quarter, middle_sums, 0)
    off_row = cols_to_row(padm_sc, accm_sc[0]) / owned_count
    cmsg_sc[0] = jnp.zeros_like(cmsg_sc[0])
    cmsg_sc[0, 0:2, :] = pivot_row + off_row
    cmsg_sc[0, 2:4, :] = cols_to_row(padm_sc, accm_sc[1]) - off_row * off_row * owned_count
    accm_sc[...] = jnp.zeros_like(accm_sc)
    cstat_sc[0, ci] = cmsg_sc[0]
    chan_send(3, same(cmsg_sc.at[0]), cstat_sc.at[0])
    chan_send(7, dfar_of, dn_sc.at[1])
    far_start(quarter // 2, 0)
    dp_some(early, full)
    if left > 0:
        dp_load(full, left).start()
        dp_load(full, left).wait()
        dp_split(full, left)
    chan_wait(3, same(cmsg_sc.at[0]), cstat_sc.at[0])
    group_mean, group_dev = combine(cstat_sc[0], owned_count)
    msg_sc[0] = jnp.zeros_like(msg_sc[0])
    msg_sc[0, 0:2, :] = group_mean
    msg_sc[0, 2:4, :] = group_dev
    stat_sc[1, bi] = msg_sc[0]
    batch_send(1, same(msg_sc.at[0]), stat_sc.at[1])
    chan_wait(7, dfar_of, dn_sc.at[1])
    lax.fori_loop(0, quarter, back_slot, 0)
    batch_wait(1, same(msg_sc.at[0]), stat_sc.at[1])
    meanm_row, devm_row = combine(stat_sc[1], local_count)
    rstdm_row = lax.rsqrt(devm_row / pixels + EPS)
    row_to_cols(colm_sc.at[0], meanm_row)
    row_to_cols(colm_sc.at[1], rstdm_row)

    def mid_point(values):
        mean, rstd = wide(colm_sc, 0), wide(colm_sc, 1)
        norm = (values - mean) * rstd
        pre = norm * wide(colm_sc, 2) + wide(colm_sc, 3)
        s = sigmoid(pre)
        act = pre * s
        return norm, act, s + act * (1.0 - s)

    def mid_own(q, carry):
        first, second = None, None
        for cols in chunks():
            norm, act, slope = mid_point(mid_sc[q, :, cols])
            actm_sc[q, :, cols] = act.astype(BF16)
            grad = d_sc[quarter + q, :, cols] * slope
            d_sc[quarter + q, :, cols] = grad
            mid_sc[q, :, cols] = norm
            one, two = lane_fold(grad), lane_fold(grad * norm)
            first = one if first is None else first + one
            second = two if second is None else second + two
        accm_sc[0] += first
        accm_sc[1] += second
        return carry

    lax.fori_loop(0, quarter, mid_own, 0)
    cmsg_sc[1] = jnp.zeros_like(cmsg_sc[1])
    cmsg_sc[1, 0:2, :] = cols_to_row(padm_sc, accm_sc[0])
    cmsg_sc[1, 2:4, :] = cols_to_row(padm_sc, accm_sc[1])
    cstat_sc[1, ci] = cmsg_sc[1]
    chan_send(4, same(cmsg_sc.at[1]), cstat_sc.at[1])
    for q in range(1, quarter):
        far_start((quarter + q) // 2, q % 2)

    def tiles_of(ref):
        rows, cols = ref.shape
        return [(r, l, min(128, cols - 128 * l)) for r in range(rows // 16) for l in range(-(-cols // 128))]

    def scatter(refs, kind, values):
        out, back, _ = refs
        per = out.shape[1]
        for at, (r, l, width) in enumerate(tiles_of(values)):
            tile = values[16 * r : 16 * r + 16, 128 * l : 128 * l + width]
            out[at // per, at % per, :, 0:width] = tile.astype(BF16)
        back[bi] = out[bi]
        batch_send(kind, lambda other: out.at[other], back)

    def reduce_gather(refs, kind):
        out, back, whole = refs
        batch_wait(kind, lambda other: out.at[other], back)
        total = back[0].astype(F32)
        for at in range(1, nb):
            total = total + back[at].astype(F32)
        out[bi] = total.astype(BF16)
        whole[bi] = total.astype(BF16)
        batch_send(kind + 1, same(out.at[bi]), whole)

    def gather(refs, kind, ref):
        out, _, whole = refs
        per = out.shape[1]
        batch_wait(kind + 1, same(out.at[bi]), whole)
        for at, (r, l, width) in enumerate(tiles_of(ref)):
            tile = whole[at // per, at % per, :, 0:width]
            ref[16 * r : 16 * r + 16, 128 * l : 128 * l + width] = tile.astype(F32)

    spread_refs, reduce_refs = (ws_out, ws_in, ws_all), (wr_out, wr_back, wr_all)

    def spread_grad(q, carry):
        wsg_sc[...] += dot_nt(actm_sc[q], dcol_sc[q])
        return carry

    lax.fori_loop(0, quarter, spread_grad, 0)
    scatter(spread_refs, 4, wsg_sc)
    chan_wait(4, same(cmsg_sc.at[1]), cstat_sc.at[1])
    msg_sc[1] = (cstat_sc[1, 0] + cstat_sc[1, 1]) + (cstat_sc[1, 2] + cstat_sc[1, 3])
    stat_sc[2, bi] = msg_sc[1]
    batch_send(2, same(msg_sc.at[1]), stat_sc.at[2])
    def spread(q, carry):
        for k, cols in enumerate(chunks()):
            taps = dot(wf_sc[...], actm_sc[q, :, cols])
            for l in range(2):
                flat_sc[2 * k + l, 0 : TAPS * NEW_PAD, :] = taps[:, 128 * l : 128 * (l + 1)]
        total = None
        for b in range(3):
            column = None
            for a in range(3):
                t = 3 * a + b
                tap = [flat_sc[l, NEW_PAD * t : NEW_PAD * t + 40, :] for l in range(CELLS // 128)]
                tap = at_offset(jnp.concatenate(tap, axis=1), a - 1, 0)
                column = tap if column is None else column + tap
            column = at_offset(column, 0, b - 1)
            total = column if total is None else total + column
        for b in range(4):
            newo_sc[b, q] = total[0:n_new, CHUNK * b : CHUNK * (b + 1)].astype(BF16)
        return carry

    lax.fori_loop(0, quarter, spread, 0)
    new_of = lambda other: newo_sc.at[other]
    newi_sc[ci] = newo_sc[ci]
    reduce_gather(spread_refs, 4)
    batch_wait(2, same(msg_sc.at[1]), stat_sc.at[2])
    mid_sums = stat_sc[2, 0]
    for at in range(1, nb):
        mid_sums = mid_sums + stat_sc[2, at]
    row_to_cols(colm_sc.at[4], mid_sums[0:2, :] / pixels)
    row_to_cols(colm_sc.at[5], mid_sums[2:4, :] / pixels)
    row_to_cols(colm_sc.at[6], gathered(2) * rstdm_row)

    def dm_copy(i, h):
        return pltpu.make_async_remote_copy(
            src_ref=dm_out.at[i, :, half_cols(h)],
            dst_ref=dm_in.at[i, :, half_cols(h)],
            send_sem=dm_s.at[i, h],
            recv_sem=dm_r.at[i, h],
            device_id=mate,
            device_id_type=MESH,
        )

    def store(n):
        return pltpu.make_async_copy(slope_sc.at[n], dv_hbm.at[n], store_sem.at[n])

    def back_view(n, dm_ref):
        mean, rstd, scale = wide(col_sc, 0), wide(col_sc, 1), wide(col_sc, 2)
        first, second = None, None
        for cols in chunks():
            grad = dot(wr_sc[...], dm_ref[:, cols]) * slope_sc[n, 0:n_in, cols].astype(F32)
            slope_sc[n, 0:n_in, cols] = (grad * scale + dp_sc[n, :, cols].astype(F32)).astype(BF16)
            norm = (x_sc[n, 0:n_in, cols].astype(F32) - mean) * rstd
            one, two = lane_fold(grad), lane_fold(grad * norm)
            first = one if first is None else first + one
            second = two if second is None else second + two
        acc_sc[0] += first
        acc_sc[1] += second
        wg_sc[:, 0:n_in] += dot_nt(dm_ref[...], act_sc[n])

    def dm_own(q, carry):
        i = quarter + q
        for cols in chunks():
            grad = d_sc[i, :, cols] - wide(colm_sc, 4) - mid_sc[q, :, cols] * wide(colm_sc, 5)
            dm_out[i, :, cols] = (grad * wide(colm_sc, 6)).astype(BF16)
        dm_copy(i, 0).start()
        dm_copy(i, 1).start()
        return carry

    lax.fori_loop(0, quarter, dm_own, 0)

    def back_mate(i):
        dm_copy(i, 0).wait_recv()
        dm_copy(i, 1).wait_recv()
        back_view(slot_view(i, 1 - c), dm_in.at[i])

    def back_own(q, carry):
        back_view(slot_view(quarter + q, c), dm_out.at[quarter + q])

        @pl.when(q > 0)
        def _():
            back_mate(quarter + q - 1)

        return carry

    lax.fori_loop(0, quarter, back_own, 0)
    back_mate(2 * quarter - 1)

    def back_far(q, carry):
        m = quarter // 2 + q // 2
        rest_copy(quarter + q).wait_recv()
        unpack_rest(pair_rest[q].astype(F32) + far_rest[quarter + q].astype(F32))

        @pl.when(lax.rem(q, 2) == 0)
        def _():
            far_copy(m, 0, 0).wait_recv()
            far_copy(m, 0, 1).wait_recv()

        @pl.when(lax.rem(q, 2) == 1)
        def _():
            unpack_second(m)

        for k, cols in enumerate(chunks()):
            part = pair_sc[q, :, cols].astype(F32) + far_sc[quarter + q, :, cols].astype(F32)
            norm, act, slope = mid_point(with_rest(part, k))
            grad = d_sc[q, :, cols] * slope - wide(colm_sc, 4) - norm * wide(colm_sc, 5)
            dm_out[q, :, cols] = (grad * wide(colm_sc, 6)).astype(BF16)
            if k % 2 == 1:
                dm_copy(q, k // 2).start()
        back_view(slot_view(q, c), dm_out.at[q])

        @pl.when(q > 0)
        def _():
            back_mate(q - 1)

        return carry

    lax.fori_loop(0, quarter // 2, back_far, 0)
    gather(spread_refs, 4, wsg_sc)
    for b in range(4):
        wsp_sc[b, 0:40, :] = wsg_sc[n_own * b : n_own * b + 40, :].astype(BF16)
    wsgi_sc[ci] = wsp_sc[ci]
    wsg_of = lambda other: wsp_sc.at[other]
    chan_send(6, wsg_of, wsgi_sc)
    chan_send(5, new_of, newi_sc)
    lax.fori_loop(quarter // 2, quarter, back_far, 0)
    back_mate(quarter - 1)

    scatter(reduce_refs, 6, wg_sc)
    msg_sc[2] = jnp.zeros_like(msg_sc[2])
    msg_sc[2, 0:2, :] = cols_to_row(padc_sc, acc_sc[0])
    msg_sc[2, 2:4, :] = cols_to_row(padc_sc, acc_sc[1])
    stat_sc[3, bi] = msg_sc[2]
    batch_send(3, same(msg_sc.at[2]), stat_sc.at[3])
    batch_wait(3, same(msg_sc.at[2]), stat_sc.at[3])
    total = stat_sc[3, 0]
    for at in range(1, nb):
        total = total + stat_sc[3, at]
    gain_scale = gain_row * rstd_row
    row_to_cols(col_sc.at[4], -gain_scale * rstd_row * (total[2:4, :] / pixels))
    row_to_cols(col_sc.at[5], -gain_scale * (total[0:2, :] / pixels))
    reduce_gather(reduce_refs, 6)

    def finish(n, carry):
        mean, slant, level = wide(col_sc, 0), wide(col_sc, 4), wide(col_sc, 5)
        for cols in chunks():
            rest = (x_sc[n, 0:n_in, cols].astype(F32) - mean) * slant + level
            slope_sc[n, 0:n_in, cols] = (slope_sc[n, 0:n_in, cols].astype(F32) + rest).astype(BF16)
        store(n).start()
        return carry

    lax.fori_loop(0, n_views, finish, 0)

    sums_ref[...] = jnp.zeros_like(sums_ref)
    sums_ref[0:1, :] = one_row(total[2:4, :])
    sums_ref[1:2, :] = one_row(total[0:2, :])
    all_sums = jnp.concatenate([one_row(mid_sums[2:4, :]), one_row(mid_sums[0:2, :]), jnp.zeros((6, 256), F32)], axis=0)
    own_sums = all_sums
    for b in range(1, 4):
        own_sums = jnp.where(ci == b, pltpu.roll(all_sums, 256 - n_own * b, 1), own_sums)
    sums_ref[2:4, :] = own_sums[0:2, :]

    chan_wait(5, new_of, newi_sc)
    for b in range(4):
        for q in range(quarter):
            new_ref[quarter * b + q] = newi_sc[b, q]
    chan_wait(6, wsg_of, wsgi_sc)
    wsg_total = (wsgi_sc[0].astype(F32) + wsgi_sc[1].astype(F32)) + (
        wsgi_sc[2].astype(F32) + wsgi_sc[3].astype(F32)
    )
    wsg_ref[...] = wsg_total[0:n_own, :]
    gather(reduce_refs, 6, wg_sc)
    wrg_ref[...] = wg_sc[0 : wrg_ref.shape[0], 0:n_in]

    def stored(n, carry):
        store(n).wait()
        return carry

    lax.fori_loop(0, n_views, stored, 0)

    def sent(i, carry):
        half_copy(i).wait_send()
        rest_copy(i).wait_send()
        for h in range(2):
            dm_copy(i, h).wait_send()
        return carry

    lax.fori_loop(0, 2 * quarter, sent, 0)

    def sent_far(m, carry):
        for v in range(2):
            for h in range(2):
                far_copy(m, v, h).wait_send()
        return carry

    lax.fori_loop(0, quarter, sent_far, 0)


def layer(nb, crops, flips, views, stats, vectors, wr_t, w_spread, d_new, d_passed):
    n_views, n_rows, _ = views.shape
    n_mid, n_in = wr_t.shape
    n_own = n_mid // 4
    quarter = n_views // 4
    n_new = d_new.shape[0]
    n_cols = TAPS * NEW_PAD
    together = -(-quarter * n_new // 16) * 16
    in_pad = -(-n_in // 16) * 16
    ws_tiles = -(-(MID_PAD // 16 * -(-n_cols // 128)) // nb)
    wr_tiles = -(-(MID_PAD // 16 * -(-in_pad // 128)) // nb)
    group = 16
    vmem = pl.BlockSpec(memory_space=pltpu.VMEM)
    anywhere = pl.BlockSpec(memory_space=pl.ANY)
    smem = pl.BlockSpec(memory_space=pltpu.SMEM)
    dma = pltpu.SemaphoreType.DMA
    slots = 2 * quarter
    return pl.pallas_call(
        functools.partial(layer_kernel, nb),
        in_specs=[smem, smem, anywhere] + [vmem] * 8 + [anywhere],
        out_specs=[anywhere, vmem, vmem, vmem, vmem],
        out_shape=[
            jax.ShapeDtypeStruct((n_views, n_rows, CELLS), BF16),
            jax.ShapeDtypeStruct((n_views, n_new, CHUNK), BF16),
            jax.ShapeDtypeStruct((n_mid, n_in), F32),
            jax.ShapeDtypeStruct((n_own, n_cols), F32),
            jax.ShapeDtypeStruct((8, 256), F32),
        ],
        scratch_shapes=[
            pltpu.VMEM((n_views, n_rows, CELLS), BF16),
            pltpu.VMEM((n_views, n_in, CELLS), BF16),
            pltpu.VMEM((n_views, n_rows, CELLS), BF16),
            pltpu.VMEM((n_views, n_in, CELLS), BF16),
            pltpu.VMEM((slots, MID_PAD, CELLS), BF16),
            pltpu.VMEM((slots, MID_PAD, CELLS), BF16),
            pltpu.VMEM((slots, MAIN, CELLS), BF16),
            pltpu.VMEM((slots, MAIN, CELLS), BF16),
            pltpu.VMEM((slots, 16, CHUNK), BF16),
            pltpu.VMEM((slots, 16, CHUNK), BF16),
            pltpu.VMEM((16, CHUNK), F32),
            pltpu.VMEM((CELLS // CHUNK, 8, CHUNK), F32),
            pltpu.VMEM((quarter, MAIN, CELLS // 2 + CHUNK), BF16),
            pltpu.VMEM((quarter, CELLS, CHUNK), BF16),
            pltpu.VMEM((CELLS // 2, CELLS // 2), BF16),
            pltpu.VMEM((slots, MID_PAD, CELLS), F32),
            pltpu.VMEM((quarter + 1, n_cols, CELLS), BF16),
            pltpu.VMEM((quarter, MID_PAD, CELLS), F32),
            pltpu.VMEM((quarter, MID_PAD, CELLS), BF16),
            pltpu.VMEM((slots, MID_PAD, CELLS), BF16),
            pltpu.VMEM((slots, MID_PAD, CELLS), BF16),
            pltpu.VMEM((2, 2, together, CHUNK), BF16),
            pltpu.VMEM((2, 4, together, CHUNK), BF16),
            pltpu.VMEM((together, 128), F32),
            pltpu.VMEM((NEW_PAD, CELLS), F32),
            pltpu.VMEM((2, group, n_views, CELLS), BF16),
            pltpu.VMEM((CELLS // 128, max(max(group, n_new) * (n_views + 1), n_cols), 128), F32),
            pltpu.VMEM((8, 256), F32),
            pltpu.VMEM((4, 8, 256), F32),
            pltpu.VMEM((4, NEW_PAD, n_cols), BF16),
            pltpu.VMEM((n_in, MID_PAD), BF16),
            pltpu.VMEM((MID_PAD, n_in), BF16),
            pltpu.VMEM((MID_PAD, n_cols), BF16),
            pltpu.VMEM((n_cols, MID_PAD), BF16),
            pltpu.VMEM((4, nb, 8, 128), F32),
            pltpu.VMEM((2, 4, 8, 128), F32),
            pltpu.VMEM((3, 8, 128), F32),
            pltpu.VMEM((2, 8, 128), F32),
            pltpu.VMEM((6, n_in, 128), F32),
            pltpu.VMEM((9, MID_PAD, 128), F32),
            pltpu.VMEM((256, 128), F32),
            pltpu.VMEM((256, 128), F32),
            pltpu.VMEM((2, n_in, 128), F32),
            pltpu.VMEM((2, MID_PAD, 128), F32),
            pltpu.VMEM((MID_PAD, in_pad), F32),
            pltpu.VMEM((MID_PAD, n_cols), F32),
            pltpu.VMEM((4, NEW_PAD, n_cols), BF16),
            pltpu.VMEM((nb, ws_tiles, 16, 128), BF16),
            pltpu.VMEM((nb, ws_tiles, 16, 128), BF16),
            pltpu.VMEM((nb, ws_tiles, 16, 128), BF16),
            pltpu.VMEM((nb, wr_tiles, 16, 128), BF16),
            pltpu.VMEM((nb, wr_tiles, 16, 128), BF16),
            pltpu.VMEM((nb, wr_tiles, 16, 128), BF16),
            pltpu.VMEM((4, quarter, n_new, CHUNK), BF16),
            pltpu.VMEM((4, quarter, n_new, CHUNK), BF16),
            dma((n_views,)),
            dma((n_views,)),
            dma((slots,)),
            dma((slots,)),
            dma((slots, 2)),
            dma((slots, 2)),
            dma((slots,)),
            dma((slots,)),
            dma((slots, 2)),
            dma((slots, 2)),
            dma((8, nb)),
            dma((8, nb)),
            dma((8, 4)),
            dma((8, 4)),
            dma((2,)),
        ],
        compiler_params=pltpu.CompilerParams(
            collective_id=0, has_side_effects=True, vmem_limit_bytes=VMEM_LIMIT
        ),
        name="layer",
    )(crops, flips, views, stats, *vectors, wr_t, w_spread, d_new, d_passed)


def solution(mesh):
    nb = mesh.shape["batch"]

    def on_device(features, crops, flips, gain_in, shift_in, w_reduce, gain_mid, shift_mid, w_spread, d_passed, d_new):
        n_own, n_new = w_spread.shape[0], w_spread.shape[3]

        w9 = jnp.transpose(w_spread, (1, 2, 0, 3)).reshape(TAPS, n_own, n_new)
        crops_t, flips_t = jnp.transpose(crops, (1, 2, 0)), jnp.transpose(flips)
        swap = lambda v: jnp.transpose(v, (1, 0, 2))
        views, passed, stats = crop_views(swap(features), crops_t, flips_t)
        dv, new_maps, wr_grad, ws_grad, sums = layer(
            nb, crops_t, flips_t, views, stats, (gain_in, shift_in, gain_mid, shift_mid), jnp.transpose(w_reduce), w9, swap(d_new), swap(d_passed)
        )
        features_grad, new_maps, wr_grad, ws_grad, *grads = place_views(
            crops_t, flips_t, dv, new_maps, wr_grad, ws_grad, sums
        )
        ws_grad = jnp.transpose(ws_grad.reshape(3, 3, n_own, n_new), (2, 0, 1, 3))
        return (swap(passed), swap(new_maps), swap(features_grad), jnp.transpose(wr_grad), ws_grad, *grads)

    return jax.shard_map(
        on_device,
        mesh=mesh,
        in_specs=(
            P("batch", "chan", None),
            P("batch", None, None),
            P("batch", None),
            P("chan"),
            P("chan"),
            P("chan", None),
            P("chan"),
            P("chan"),
            P("chan", None, None, None),
            P("batch", "chan", None),
            P("batch", None, "chan"),
        ),
        out_specs=(
            P("batch", "chan", None),
            P("batch", None, "chan"),
            P("batch", "chan", None),
            P("chan", None),
            P("chan", None, None, None),
            P("chan"),
            P("chan"),
            P("chan"),
            P("chan"),
        ),
        check_vma=False,
    )
```

```python
import functools

import jax
import jax.numpy as jnp
from jax import lax
from jax.experimental import pallas as pl
from jax.experimental.pallas import tpu as pltpu
from jax.sharding import PartitionSpec as P

H = 32
W = 32
MARGIN = 8
GRID = H + 2 * MARGIN
CELLS = H * W
EPS = 1e-05
CHUNK = 256
SPAN = 512
STRIDE = 8 * GRID
TAPS = 9
BLOCK = 80
MID_PAD = 144
NEW_PAD = 48
MAIN = 128
REST = 4
F32 = jnp.float32
BF16 = jnp.bfloat16
MESH = pl.DeviceIdType.MESH
VMEM_LIMIT = 63 * 2**20 + 800 * 2**10


def dot(a, b):
    return jnp.dot(a, b, preferred_element_type=F32)


def dot_nt(a, b):
    return lax.dot_general(a, b, (((1,), (1,)), ((), ())), preferred_element_type=F32)


def iota(shape, axis):
    return lax.broadcasted_iota(jnp.int32, shape, axis)


def lane_fold(values):
    total = values[:, 0:128]
    for at in range(128, values.shape[1], 128):
        total = total + values[:, at : at + 128]
    return total


def cols_to_row(pad_ref, values):
    if values is not None:
        pad_ref[0 : values.shape[0], :] = values
    halves = [
        jnp.sum(jnp.transpose(pad_ref[at : at + 128, :]), axis=0, keepdims=True)
        for at in (0, 128)
    ]
    return jnp.concatenate(halves, axis=0)


def two_rows(row):
    return jnp.concatenate([row[:, 0:128], row[:, 128:256]], axis=0)


def one_row(rows):
    return jnp.concatenate([rows[0:1, :], rows[1:2, :]], axis=1)


def row_to_cols(out_ref, row):
    rows = out_ref.shape[0]
    for h, at in enumerate((0, 128)):
        height = min(128, rows - at)
        square = jnp.broadcast_to(row[h : h + 1, :], (128, 128))
        out_ref[at : at + height, :] = jnp.transpose(square)[0:height, :]


def window_start(crops_ref, j, v):
    start = crops_ref[v, 0, j] * GRID + crops_ref[v, 1, j]
    base = jnp.minimum((start // 128) * 128, GRID * GRID - 3 * STRIDE - SPAN)
    return pl.multiple_of(base, 128), start - base


def chunk_target(offset, flip, cell):
    col = cell & (W - 1)
    row = cell >> 5
    return offset + row * GRID + jnp.where(flip > 0, W - 1 - col, col)


def blocks_of(channels):
    return [(at, min(BLOCK, channels - at)) for at in range(0, channels, BLOCK)]


def crop_kernel(crops_ref, flips_ref, x_hbm, views_hbm, passed_hbm, stats_ref, pick_sc, xn_sc, xf_sc, xi_sc, vw_sc, pf_sc, pn_sc, mean_sc, dev_sc, x_sem, vw_sem, pn_sem):
    channels, items, cells = x_hbm.shape
    n_views, rows, part_rows = 2 * items, BLOCK, 16
    blocks = blocks_of(channels)

    def load(at):
        first, size = blocks[at]
        return pltpu.make_async_copy(x_hbm.at[pl.ds(first, size)], xn_sc.at[at, pl.ds(0, size)], x_sem.at[at])

    def view_out(at, n):
        first = pl.multiple_of(at * rows, rows)
        return pltpu.make_async_copy(vw_sc.at[at, n], views_hbm.at[n, pl.ds(first, rows)], vw_sem.at[at, n])

    def passed_out(at, u):
        first, size = blocks[at]
        size = min(part_rows, size - part_rows * u)
        return pltpu.make_async_copy(
            pn_sc.at[at, pl.ds(part_rows * u, size)],
            passed_hbm.at[pl.ds(first + part_rows * u, size)],
            pn_sem.at[at, u],
        )

    for at in range(len(blocks)):
        load(at).start()

    def build(n, carry):
        j, v = n // 2, n % 2
        _, offset = window_start(crops_ref, j, v)
        target = chunk_target(offset, flips_ref[v, j], iota((1, CHUNK), 1))
        pick_sc[n] = (iota((SPAN, CHUNK), 0) == target).astype(BF16)
        return carry

    lax.fori_loop(0, n_views, build, 0)
    mean_sc[...] = jnp.zeros_like(mean_sc)
    dev_sc[...] = jnp.zeros_like(dev_sc)

    def block(b, carry):
        for at in range(len(blocks)):

            @pl.when(b == at)
            def _(at=at):
                load(at).wait()

        for l in range(cells // 128):
            at = slice(128 * l, 128 * (l + 1))
            wide_x = xn_sc[b, :, :, at].astype(F32)
            for ch in range(rows):
                xf_sc[l, (items + 1) * ch : (items + 1) * ch + items, :] = wide_x[ch]

        total = jnp.zeros((rows, 128), F32)
        squares = jnp.zeros((rows, 128), F32)
        pivot = None
        for j in range(items):
            for l in range(cells // 128):
                xi_sc[j, :, 128 * l : 128 * (l + 1)] = xf_sc[l, pl.ds(j, rows, stride=items + 1), :].astype(BF16)
            for v in range(2):
                n = 2 * j + v
                base, _ = window_start(crops_ref, j, v)
                spans = [xi_sc[j, :, pl.ds(pl.multiple_of(base + STRIDE * k, 128), SPAN)] for k in range(CELLS // CHUNK)]
                parts = dot(jnp.concatenate(spans, axis=0), pick_sc[n])
                for k in range(CELLS // CHUNK):
                    part = parts[rows * k : rows * (k + 1), :]
                    vw_sc[b, n, :, CHUNK * k : CHUNK * (k + 1)] = part.astype(BF16)
                    for l in range(2):
                        pf_sc[2 * k + l, pl.ds(n, rows, stride=n_views + 1), :] = part[:, 128 * l : 128 * (l + 1)]
                    if pivot is None:
                        pivot = jnp.sum(lane_fold(part), axis=1, keepdims=True) / CHUNK
                    off = part - pivot
                    total = total + lane_fold(off)
                    squares = squares + lane_fold(off * off)
                view_out(b, n).start()
        for u in range(rows // part_rows):
            for l in range(CELLS // 128):
                at = slice(128 * l, 128 * (l + 1))
                for ch in range(part_rows * u, part_rows * (u + 1)):
                    first = (n_views + 1) * ch
                    pn_sc[b, ch, :, at] = pf_sc[l, first : first + n_views, :].astype(BF16)
            for at in range(len(blocks)):

                @pl.when(b == at)
                def _(at=at):
                    passed_out(at, u).start()

        count = n_views * CELLS
        shift = jnp.sum(total, axis=1, keepdims=True) / count
        first = pl.multiple_of(b * rows, 8)
        lane = iota((rows, 128), 1)
        mean_sc[pl.ds(first, rows), :] = jnp.where(lane == 0, pivot + shift, 0.0)
        dev_sc[pl.ds(first, rows), :] = squares - jnp.where(lane == 0, shift * shift * count, 0.0)
        return carry

    lax.fori_loop(0, len(blocks), block, 0)
    stats_ref[...] = jnp.zeros_like(stats_ref)
    stats_ref[0:2, :] = cols_to_row(mean_sc, None)
    stats_ref[2:4, :] = cols_to_row(dev_sc, None)
    for at in range(len(blocks)):
        for n in range(n_views):
            view_out(at, n).wait()
        for u in range(rows // part_rows):
            passed_out(at, u).wait()


def crop_views(features, crops, flips):
    channels, items, cells = features.shape
    n_blocks = len(blocks_of(channels))
    anywhere = pl.BlockSpec(memory_space=pl.ANY)
    smem = pl.BlockSpec(memory_space=pltpu.SMEM)
    dma = pltpu.SemaphoreType.DMA
    return pl.pallas_call(
        crop_kernel,
        in_specs=[smem, smem, anywhere],
        out_specs=[anywhere, anywhere, pl.BlockSpec(memory_space=pltpu.VMEM)],
        out_shape=[
            jax.ShapeDtypeStruct((2 * items, n_blocks * BLOCK, CELLS), BF16),
            jax.ShapeDtypeStruct((channels, 2 * items, CELLS), BF16),
            jax.ShapeDtypeStruct((8, 128), F32),
        ],
        scratch_shapes=[
            pltpu.VMEM((2 * items, SPAN, CHUNK), BF16),
            pltpu.VMEM((n_blocks, BLOCK, items, cells), BF16),
            pltpu.VMEM((cells // 128, BLOCK * (items + 1), 128), F32),
            pltpu.VMEM((items, BLOCK, cells), BF16),
            pltpu.VMEM((n_blocks, 2 * items, BLOCK, CELLS), BF16),
            pltpu.VMEM((CELLS // 128, BLOCK * (2 * items + 1), 128), F32),
            pltpu.VMEM((n_blocks, BLOCK, 2 * items, CELLS), BF16),
            pltpu.VMEM((256, 128), F32),
            pltpu.VMEM((256, 128), F32),
            dma((n_blocks,)),
            dma((n_blocks, 2 * items)),
            dma((n_blocks, BLOCK // 16)),
        ],
        compiler_params=pltpu.CompilerParams(vmem_limit_bytes=VMEM_LIMIT),
        name="crop_views",
    )(crops, flips, features)


def place_kernel(crops_ref, flips_ref, dv_hbm, new_ref, wrg_ref, wsg_ref, sums_ref, out_hbm, newo_ref, wrgo_ref, wsgo_ref, gi_ref, si_ref, gm_ref, sm_ref, pick_sc, dv_sc, flat_sc, out_sc, new_sc, dv_sem, out_sem):
    channels, items, cells = out_hbm.shape
    n_views, rows, part_rows = 2 * items, BLOCK, 16
    blocks = blocks_of(channels)

    def load(at):
        first = at * rows if isinstance(at, int) else pl.multiple_of(at * rows, rows)
        return pltpu.make_async_copy(dv_hbm.at[:, pl.ds(first, rows)], dv_sc.at[at], dv_sem.at[at])

    def out(at, u):
        first, size = blocks[at]
        size = min(part_rows, size - part_rows * u)
        return pltpu.make_async_copy(
            out_sc.at[at, pl.ds(part_rows * u, size)],
            out_hbm.at[pl.ds(first + part_rows * u, size)],
            out_sem.at[at, u],
        )

    for at in range(len(blocks)):
        load(at).start()

    def build(n, carry):
        j, v = n // 2, n % 2
        _, offset = window_start(crops_ref, j, v)
        target = chunk_target(offset, flips_ref[v, j], iota((CHUNK, 1), 0))
        pick_sc[n] = (iota((CHUNK, SPAN), 1) == target).astype(BF16)
        return carry

    lax.fori_loop(0, n_views, build, 0)

    def block(b, carry):
        load(b).wait()
        flat_sc[...] = jnp.zeros_like(flat_sc)

        def place_item(j):
            for v in range(2):
                n = 2 * j + v
                base, _ = window_start(crops_ref, j, v)
                tile = base // 128
                parts = [dv_sc[b, n, :, CHUNK * k : CHUNK * (k + 1)] for k in range(CELLS // CHUNK)]
                spans = dot(jnp.concatenate(parts, axis=0), pick_sc[n])
                spans = [spans[rows * k : rows * (k + 1), :] for k in range(CELLS // CHUNK)]
                pieces = [spans[0][:, 0:STRIDE]]
                for k in range(1, CELLS // CHUNK):
                    pieces.append(spans[k - 1][:, STRIDE:SPAN] + spans[k][:, 0 : SPAN - STRIDE])
                    pieces.append(spans[k][:, SPAN - STRIDE : STRIDE])
                pieces.append(spans[-1][:, STRIDE:SPAN])
                window = jnp.concatenate(pieces, axis=1)
                of_item = pl.ds(j, rows, stride=items + 1)
                for t in range(window.shape[1] // 128):
                    piece = window[:, 128 * t : 128 * (t + 1)]
                    if v == 1:
                        piece = piece + flat_sc[tile + t, of_item, :]
                    flat_sc[tile + t, of_item, :] = piece

        def place_some(group, carry):
            for inner in range(4):
                place_item(4 * group + inner)
            return carry

        lax.fori_loop(0, items // 4, place_some, 0)
        for u in range(rows // part_rows):
            for l in range(cells // 128):
                for ch in range(part_rows * u, part_rows * (u + 1)):
                    first = (items + 1) * ch
                    out_sc[b, ch, :, 128 * l : 128 * (l + 1)] = flat_sc[l, first : first + items, :]
            for at in range(len(blocks)):

                @pl.when(b == at)
                def _(at=at):
                    out(at, u).start()

        return carry

    lax.fori_loop(0, len(blocks), block, 0)

    n_new = new_ref.shape[1]
    for n in range(n_views):
        for l in range(2):
            piece = new_ref[n, :, 128 * l : 128 * (l + 1)]
            new_sc[l, pl.ds(n, n_new, stride=n_views), :] = piece.astype(F32)
    for l in range(2):
        newo_ref[:, :, 128 * l : 128 * (l + 1)] = new_sc[l].reshape(n_new, n_views, 128).astype(BF16)
    wrgo_ref[...] = wrg_ref[...]
    for t in range(TAPS):
        wsgo_ref[t] = wsg_ref[:, NEW_PAD * t : NEW_PAD * t + wsgo_ref.shape[2]]
    for at, ref in enumerate((gi_ref, si_ref, gm_ref, sm_ref)):
        ref[...] = sums_ref[at, 0 : ref.shape[0]]
    for at in range(len(blocks)):
        for u in range(rows // part_rows):
            out(at, u).wait()


def place_views(crops, flips, dv, new_maps, wr_grad, ws_grad, sums):
    items, channels = crops.shape[2], wr_grad.shape[1]
    n_views, n_blocks = dv.shape[0], dv.shape[1] // BLOCK
    n_new, n_own = new_maps.shape[1], ws_grad.shape[0]
    cells = GRID * GRID
    anywhere = pl.BlockSpec(memory_space=pl.ANY)
    vmem = pl.BlockSpec(memory_space=pltpu.VMEM)
    smem = pl.BlockSpec(memory_space=pltpu.SMEM)
    dma = pltpu.SemaphoreType.DMA
    small = [
        ((n_new, n_views, CHUNK), BF16),
        (wr_grad.shape, F32),
        ((TAPS, n_own, n_new), F32),
        ((channels,), F32),
        ((channels,), F32),
        ((n_own,), F32),
        ((n_own,), F32),
    ]
    return pl.pallas_call(
        place_kernel,
        in_specs=[smem, smem, anywhere] + [vmem] * 4,
        out_specs=[anywhere] + [vmem] * len(small),
        out_shape=[jax.ShapeDtypeStruct((channels, items, cells), F32)]
        + [jax.ShapeDtypeStruct(shape, kind) for shape, kind in small],
        scratch_shapes=[
            pltpu.VMEM((n_views, CHUNK, SPAN), BF16),
            pltpu.VMEM((n_blocks, n_views, BLOCK, CELLS), BF16),
            pltpu.VMEM((cells // 128, BLOCK * (items + 1), 128), F32),
            pltpu.VMEM((n_blocks, BLOCK, items, cells), F32),
            pltpu.VMEM((2, n_new * n_views, 128), F32),
            dma((n_blocks,)),
            dma((n_blocks, BLOCK // 16)),
        ],
        compiler_params=pltpu.CompilerParams(vmem_limit_bytes=VMEM_LIMIT),
        name="place_views",
    )(crops, flips, dv, new_maps, wr_grad, ws_grad, sums)


def sigmoid(v):
    return 0.5 * jnp.tanh(0.5 * v) + 0.5


def combine(parts, count):
    groups = parts.shape[0]
    mean = parts[0, 0:2, :]
    dev = parts[0, 2:4, :]
    for at in range(1, groups):
        mean = mean + parts[at, 0:2, :]
        dev = dev + parts[at, 2:4, :]
    mean = mean / groups
    spread = None
    for at in range(groups):
        off = parts[at, 0:2, :] - mean
        spread = off * off if spread is None else spread + off * off
    return mean, dev + spread * count


def layer_kernel(
    nb,
    crops_ref,
    flips_ref,
    views_hbm,
    stats_ref,
    gain_in_ref,
    shift_in_ref,
    gain_mid_ref,
    shift_mid_ref,
    wr_in,
    wsp_in,
    dnew_ref,
    dpass_hbm,
    dv_hbm,
    new_ref,
    wrg_ref,
    wsg_ref,
    sums_ref,
    x_sc,
    act_sc,
    slope_sc,
    dp_sc,
    half_out,
    half_in,
    pair_sc,
    far_sc,
    pair_rest,
    far_rest,
    pack_sc,
    ext_sc,
    packed_sc,
    find_sc,
    join_sc,
    d_sc,
    dcol_sc,
    mid_sc,
    actm_sc,
    dm_out,
    dm_in,
    dno_sc,
    dn_sc,
    pack_dn,
    dnf_sc,
    dpn_sc,
    flat_sc,
    own_par,
    par_sc,
    wsp_sc,
    wr_sc,
    wrt_sc,
    wb_sc,
    wf_sc,
    stat_sc,
    cstat_sc,
    msg_sc,
    cmsg_sc,
    col_sc,
    colm_sc,
    padc_sc,
    padm_sc,
    acc_sc,
    accm_sc,
    wg_sc,
    wsg_sc,
    wsgi_sc,
    ws_out,
    ws_in,
    ws_all,
    wr_out,
    wr_back,
    wr_all,
    newo_sc,
    newi_sc,
    load_sem,
    store_sem,
    half_s,
    half_r,
    far_s,
    far_r,
    rest_s,
    rest_r,
    dm_s,
    dm_r,
    bat_s,
    bat_r,
    chan_s,
    chan_r,
    dp_sem,
):
    bi, ci = lax.axis_index("batch"), lax.axis_index("chan")
    y, c = ci // 2, lax.rem(ci, 2)
    n_views, n_in = x_sc.shape[0], act_sc.shape[1]
    quarter = n_views // 4
    n_own, n_new = wsg_ref.shape[0], dnew_ref.shape[0]
    local_count = float(n_views * CELLS)
    owned_count = float(quarter * CELLS)
    pixels = float(nb) * local_count
    mate = (bi, 2 * y + (1 - c))
    across = (bi, 2 * (1 - y) + c)

    def batch_peer(k):
        return (lax.rem(bi + k, nb), ci)

    def chan_peer(k):
        return (bi, lax.rem(ci + k, 4))

    barrier = pltpu.get_barrier_semaphore()

    def greet(k, carry):
        pl.semaphore_signal(barrier, inc=1, device_id=batch_peer(k), device_id_type=MESH)
        return carry

    lax.fori_loop(1, nb, greet, 0)
    for k in range(1, 4):
        pl.semaphore_signal(barrier, inc=1, device_id=chan_peer(k), device_id_type=MESH)

    def load(n):
        return pltpu.make_async_copy(views_hbm.at[n], x_sc.at[n], load_sem.at[n])

    def load_step(i, carry):
        load(slot_view(i, 1 - c)).start()
        load(slot_view(i, c)).start()
        return carry

    def slot_view(i, core):
        h = jnp.where(i < quarter, 1 - y, y)
        return quarter * (2 * h + core) + lax.rem(i, quarter)

    lax.fori_loop(0, 2 * quarter, load_step, 0)
    pl.semaphore_wait(barrier, nb + 2)

    def batch_copy(kind, k, src, dst):
        return pltpu.make_async_remote_copy(
            src_ref=src,
            dst_ref=dst,
            send_sem=bat_s.at[kind, k],
            recv_sem=bat_r.at[kind, k],
            device_id=batch_peer(k),
            device_id_type=MESH,
        )

    def batch_send(kind, src_of, dst):
        def step(k, carry):
            batch_copy(kind, k, src_of(lax.rem(bi + k, nb)), dst.at[bi]).start()
            return carry

        lax.fori_loop(1, nb, step, 0)

    def batch_wait(kind, src_of, dst):
        def step(k, carry):
            other = lax.rem(bi + nb - k, nb)
            batch_copy(kind, k, src_of(lax.rem(bi + k, nb)), dst.at[other]).wait()
            return carry

        lax.fori_loop(1, nb, step, 0)

    def chan_copy(kind, k, src, dst):
        return pltpu.make_async_remote_copy(
            src_ref=src,
            dst_ref=dst,
            send_sem=chan_s.at[kind, k],
            recv_sem=chan_r.at[kind, k],
            device_id=chan_peer(k),
            device_id_type=MESH,
        )

    def chan_send(kind, src_of, dst):
        for k in range(1, 4):
            chan_copy(kind, k, src_of(lax.rem(ci + k, 4)), dst.at[ci]).start()

    def chan_wait(kind, src_of, dst):
        for k in range(1, 4):
            other = lax.rem(ci + 4 - k, 4)
            chan_copy(kind, k, src_of(lax.rem(ci + k, 4)), dst.at[other]).wait()

    def wide(ref, at):
        col = ref[at]
        return jnp.concatenate([col, col], axis=1)

    def same(ref):
        return lambda other: ref

    stat_sc[0, bi] = stats_ref[...]
    batch_send(0, same(stats_ref), stat_sc.at[0])
    own_par[...] = jnp.zeros_like(own_par)
    for at, ref in enumerate((gain_in_ref, shift_in_ref, gain_mid_ref, shift_mid_ref)):
        own_par[at : at + 1, 0 : ref.shape[0]] = ref[...].astype(F32).reshape(1, ref.shape[0])
    par_sc[ci] = own_par[...]
    chan_send(0, same(own_par), par_sc)
    dnf_sc[...] = jnp.zeros_like(dnf_sc)
    for t in range(TAPS):
        dnf_sc[0:n_own, NEW_PAD * t : NEW_PAD * t + n_new] = wsp_in[t].astype(F32)
    wsp_sc[ci] = dnf_sc[:, 0 : TAPS * NEW_PAD].astype(BF16)
    wsp_own = same(wsp_sc.at[ci])

    pack_dn[...] = jnp.zeros_like(pack_dn)
    for l in range(2):
        at = slice(128 * l, 128 * (l + 1))
        native = dnew_ref[:, :, at].astype(F32)
        for ch in range(n_new):
            flat_sc[l, (n_views + 1) * ch : (n_views + 1) * ch + n_views, :] = native[ch]
        for block in range(4):
            for q in range(quarter):
                by_view = flat_sc[l, pl.ds(quarter * block + q, n_new, stride=n_views + 1), :]
                pack_dn[n_new * q : n_new * (q + 1), :] = by_view
            dno_sc[block % 2, block // 2, :, at] = pack_dn[...].astype(BF16)
    dn_sc[0, ci] = dno_sc[c, y]
    dn_sc[1, ci] = dno_sc[c, 1 - y]
    dnew_of = lambda other: dno_sc.at[lax.rem(other, 2), other // 2]
    dfar_of = lambda other: dno_sc.at[lax.rem(other, 2), 1 - other // 2]
    chan_send(2, dnew_of, dn_sc.at[0])
    chan_send(1, wsp_own, wsp_sc)

    padc_sc[...] = jnp.zeros_like(padc_sc)
    padm_sc[...] = jnp.zeros_like(padm_sc)
    acc_sc[...] = jnp.zeros_like(acc_sc)
    accm_sc[...] = jnp.zeros_like(accm_sc)
    wg_sc[...] = jnp.zeros_like(wg_sc)
    wsg_sc[...] = jnp.zeros_like(wsg_sc)
    ext_sc[...] = jnp.zeros_like(ext_sc)
    piece, place = iota((CELLS // 2, CELLS // 2), 0), iota((CELLS // 2, CELLS // 2), 1)
    joined_at = ((piece & 255) >> 4) * W + (piece >> 8) * 16 + (piece & 15)
    join_sc[...] = (joined_at == place).astype(BF16)
    ws_out[...] = jnp.zeros_like(ws_out)
    wr_out[...] = jnp.zeros_like(wr_out)
    wrt_sc[...] = jnp.zeros_like(wrt_sc)
    wrt_sc[0 : wr_in.shape[0], :] = wr_in[...]
    eye = (iota((n_in, n_in), 0) == iota((n_in, n_in), 1)).astype(BF16)
    wr_sc[...] = dot_nt(eye, wrt_sc[...]).astype(BF16)
    gain_row = two_rows(own_par[0:1, :])
    shift_row = two_rows(own_par[1:2, :])

    gain_col, shift_col = (jnp.transpose(jnp.broadcast_to(one_row(v), (256, 256)))[0:n_in, 0:128] for v in (gain_row, shift_row))
    guess = None
    for weight, offset in ((2 / 3, 0.0), (1 / 6, 3.0**0.5), (1 / 6, -(3.0**0.5))):
        pre = shift_col + offset * gain_col
        part = weight * pre * sigmoid(pre)
        guess = part if guess is None else guess + part
    colm_sc[7] = dot(wrt_sc[...], guess.astype(BF16))

    batch_wait(0, same(stats_ref), stat_sc.at[0])
    mean_row, dev_row = combine(stat_sc[0], local_count)
    rstd_row = lax.rsqrt(dev_row / pixels + EPS)
    row_to_cols(col_sc.at[0], mean_row)
    row_to_cols(col_sc.at[1], rstd_row)
    row_to_cols(col_sc.at[2], rstd_row * gain_row)
    row_to_cols(col_sc.at[3], shift_row)

    def chunks(start=0, count=CELLS // CHUNK):
        if isinstance(start, int):
            return [slice(start + CHUNK * k, start + CHUNK * (k + 1)) for k in range(count)]
        return [pl.ds(pl.multiple_of(start + CHUNK * k, CHUNK), CHUNK) for k in range(count)]

    half = CELLS // 2

    def half_cols(h):
        return pl.ds(h * half if isinstance(h, int) else pl.multiple_of(h * half, half), half)

    def activate(n):
        mean, scale, shift = wide(col_sc, 0), wide(col_sc, 2), wide(col_sc, 3)
        for cols in chunks():
            pre = (x_sc[n, 0:n_in, cols].astype(F32) - mean) * scale + shift
            s = sigmoid(pre)
            act = pre * s
            slope_sc[n, 0:n_in, cols] = (s + act * (1.0 - s)).astype(BF16)
            act_sc[n, :, cols] = act.astype(BF16)

    def partial(n, cols):
        return dot(wrt_sc[...], act_sc[n, :, cols]) - wide(colm_sc, 7)

    def half_copy(i, h):
        return pltpu.make_async_remote_copy(
            src_ref=half_out.at[i, :, half_cols(h)],
            dst_ref=half_in.at[i, :, half_cols(h)],
            send_sem=half_s.at[i, h],
            recv_sem=half_r.at[i, h],
            device_id=mate,
            device_id_type=MESH,
        )

    def rest_copy(i):
        return pltpu.make_async_remote_copy(
            src_ref=pair_rest.at[i],
            dst_ref=far_rest.at[i],
            send_sem=rest_s.at[i],
            recv_sem=rest_r.at[i],
            device_id=across,
            device_id_type=MESH,
        )

    def unpack_rest(values):
        for k in range(CELLS // CHUNK):
            ext_sc[k, 0:REST, :] = values[REST * k : REST * (k + 1), :]

    def with_rest(main, k):
        return jnp.concatenate([main, ext_sc[k], jnp.zeros((8, CHUNK), F32)], axis=0)

    def quarter_of(i):
        j = slot_view(i, c) // 2
        row_half = jnp.where(crops_ref[1, 0, j] >= crops_ref[0, 0, j], 0, 1)
        col_half = jnp.where(crops_ref[1, 1, j] >= crops_ref[0, 1, j], 0, 1)
        return j, row_half, jnp.where(flips_ref[1, j] > 0, 1 - col_half, col_half)

    def arriving(m):
        return lax.rem(2 * m + quarter, 2 * quarter)

    def find_quarter(m, carry):
        j, row_half, col_half = quarter_of(arriving(m))
        cell = iota((1, CHUNK), 1)
        row, col = (cell >> 4) + 16 * row_half, (cell & 15) + 16 * col_half
        col = jnp.where(flips_ref[1, j] > 0, W - 1 - col, col)
        row = row + crops_ref[1, 0, j] - crops_ref[0, 0, j]
        col = col + crops_ref[1, 1, j] - crops_ref[0, 1, j]
        col = jnp.where(flips_ref[0, j] > 0, W - 1 - col, col)
        find_sc[m] = (iota((CELLS, CHUNK), 0) == row * W + col).astype(BF16)
        return carry

    def pack_second(m):
        _, row_half, col_half = quarter_of(2 * m)
        low, high = pair_sc[2 * m + 1, :, 0:half], pair_sc[2 * m + 1, :, half:CELLS]
        columns = dot_nt(jnp.where(row_half == 0, low, high), join_sc[...])
        kept = jnp.where(col_half == 0, columns[:, CHUNK:half], columns[:, 0:CHUNK])
        packed_sc[m, :, 0:half] = jnp.where(row_half == 0, high, low)
        packed_sc[m, :, half : half + CHUNK] = kept.astype(BF16)

    def unpack_second(m):
        far_copy(m, 1, 0).wait_recv()
        far_copy(m, 1, 1).wait_recv()
        _, row_half, col_half = quarter_of(arriving(m))
        whole = far_sc[2 * m + 1, :, 0:half]
        kept = far_sc[2 * m + 1, :, half : half + CHUNK]
        found = dot(far_sc[2 * m], find_sc[m]).astype(BF16)
        left, right = jnp.where(col_half == 0, found, kept), jnp.where(col_half == 0, kept, found)
        joined = dot(jnp.concatenate([left, right], axis=1), join_sc[...]).astype(BF16)
        far_sc[2 * m + 1, :, 0:half] = jnp.where(row_half == 0, joined, whole)
        far_sc[2 * m + 1, :, half:CELLS] = jnp.where(row_half == 0, whole, joined)

    def far_start(m, v):
        rest_copy(2 * m + v).start()
        far_copy(m, v, 0).start()
        far_copy(m, v, 1).start()

    def far_copy(m, v, h):
        i = 2 * m + v
        if v == 0:
            cols = half_cols(h)
            src = pair_sc.at[i, :, cols]
        else:
            cols = pl.ds(half * h, half if h == 0 else CHUNK)
            src = packed_sc.at[m, :, cols]
        return pltpu.make_async_remote_copy(
            src_ref=src,
            dst_ref=far_sc.at[i, :, cols],
            send_sem=far_s.at[i, h],
            recv_sem=far_r.at[i, h],
            device_id=across,
            device_id_type=MESH,
        )

    def to_mate(i):
        theirs = slot_view(i, 1 - c)
        load(theirs).wait()
        activate(theirs)
        for k, cols in enumerate(chunks()):
            half_out[i, :, cols] = partial(theirs, cols).astype(BF16)
            if k % 2 == 1:
                half_copy(i, k // 2).start()

    def forward(m, carry):
        for v in range(2):
            i = 2 * m + v

            @pl.when(i < 2 * quarter - 1)
            def _():
                to_mate(i + 1)

            mine = slot_view(i, c)
            load(mine).wait()
            activate(mine)
            for k, cols in enumerate(chunks()):
                if k % 2 == 0:
                    half_copy(i, k // 2).wait_recv()
                both = partial(mine, cols) + half_in[i, :, cols].astype(F32)
                pair_sc[i, :, cols] = both[0:MAIN, :].astype(BF16)
                pack_sc[REST * k : REST * (k + 1), :] = both[MAIN : MAIN + REST, :]

                @pl.when(i >= quarter)
                def _():
                    mid_sc[i - quarter, :, cols] = both

                if v == 0 and k % 2 == 1:

                    @pl.when(i < quarter)
                    def _(h=k // 2):
                        far_copy(m, 0, h).start()

            pair_rest[i] = pack_sc[...].astype(BF16)
            if v == 1:
                pack_second(m)

            @pl.when(i < quarter)
            def _():
                rest_copy(i).start()
                if v == 1:
                    far_copy(m, 1, 0).start()
                    far_copy(m, 1, 1).start()

        return carry

    to_mate(0)
    lax.fori_loop(0, quarter, forward, 0)
    lax.fori_loop(0, quarter, find_quarter, 0)

    chan_send(7, dfar_of, dn_sc.at[1])

    chan_wait(1, wsp_own, wsp_sc)
    stacked = wsp_sc[...].reshape(4 * NEW_PAD, TAPS * NEW_PAD)
    lane, row = iota((MID_PAD, 4 * NEW_PAD), 1), iota((MID_PAD, 4 * NEW_PAD), 0)
    hit = None
    for b in range(4):
        inner = lane - NEW_PAD * b
        one = (inner >= 0) & (inner < n_own) & (row == inner + n_own * b)
        hit = one if hit is None else hit | one
    wb_sc[...] = dot(hit.astype(BF16), stacked).astype(BF16)
    taps_eye = iota((TAPS * NEW_PAD, TAPS * NEW_PAD), 0) == iota((TAPS * NEW_PAD, TAPS * NEW_PAD), 1)
    wf_sc[...] = dot_nt(taps_eye.astype(BF16), wb_sc[...]).astype(BF16)

    cell = iota((1, CELLS), 1)
    col_at, row_at = cell & (W - 1), cell >> 5

    def inside(values, row_step, col_step):
        ok = None
        if col_step != 0:
            ok = (col_at + col_step >= 0) & (col_at + col_step < W)
        if row_step != 0:
            on = (row_at + row_step >= 0) & (row_at + row_step < H)
            ok = on if ok is None else ok & on
        return values if ok is None else jnp.where(ok, values, 0.0)

    def at_offset(values, row_step, col_step):
        move = (-(W * row_step + col_step)) % CELLS
        rolled = values if move == 0 else pltpu.roll(values, move, 1)
        return inside(rolled, row_step, col_step)

    chan_wait(2, dnew_of, dn_sc.at[0])

    def back_slot(i, carry):
        far = jnp.where(i < quarter, 1, 0)
        keep = jnp.where(i < quarter, quarter, i - quarter)
        for b in range(4):
            for l in range(2):
                pack_dn[...] = dn_sc[far, b, :, 128 * l : 128 * (l + 1)].astype(F32)
                at = CHUNK * b + 128 * l
                dnf_sc[0:n_new, at : at + 128] = pack_dn[pl.ds(n_new * lax.rem(i, quarter), n_new), :]
        grad = dnf_sc[...]
        for b in range(3):
            moved = at_offset(grad, 0, 1 - b)
            for a in range(3):
                t = 3 * a + b
                tap = at_offset(moved, 1 - a, 0)
                dcol_sc[keep, NEW_PAD * t : NEW_PAD * (t + 1), :] = tap.astype(BF16)
        for cols in chunks():
            d_sc[i, :, cols] = dot(wb_sc[...], dcol_sc[keep, :, cols])
        return carry

    lax.fori_loop(quarter, 2 * quarter, back_slot, 0)

    group = dpn_sc.shape[1]
    full = n_in // group

    def dp_load(k, rows):
        return pltpu.make_async_copy(
            dpass_hbm.at[pl.ds(k * group, rows)],
            dpn_sc.at[lax.rem(k, 2), pl.ds(0, rows)],
            dp_sem.at[lax.rem(k, 2)],
        )

    def dp_split(k, rows):
        first = k * group if isinstance(k, int) else pl.multiple_of(k * group, group)
        for l in range(CELLS // 128):
            at = slice(128 * l, 128 * (l + 1))
            native = dpn_sc[lax.rem(k, 2), 0:rows, :, at].astype(F32)
            for ch in range(rows):
                flat_sc[l, (n_views + 1) * ch : (n_views + 1) * ch + n_views, :] = native[ch]
            for n in range(n_views):
                by_view = flat_sc[l, pl.ds(n, rows, stride=n_views + 1), :]
                dp_sc[n, pl.ds(first, rows), at] = by_view.astype(BF16)

    left = n_in - full * group

    def dp_step(k, carry):
        @pl.when(k < full - 1)
        def _():
            dp_load(k + 1, group).start()

        dp_load(k, group).wait()
        dp_split(k, group)
        return carry

    def dp_some(first, last):
        lax.fori_loop(first, last, dp_step, 0)

    early = full - 2
    dp_load(0, group).start()
    dp_some(0, early)

    chan_wait(0, same(own_par), par_sc)

    def gathered(at):
        total = None
        for b in range(4):
            piece = jnp.where(iota((8, 256), 1) < n_own, par_sc[b], 0.0)
            piece = piece if b == 0 else pltpu.roll(piece, n_own * b, 1)
            total = piece if total is None else total + piece
        return two_rows(total[at : at + 1, :])

    row_to_cols(colm_sc.at[2], gathered(2))
    row_to_cols(colm_sc.at[3], gathered(3))

    def middle_view(q, first):
        rest_copy(q).wait_recv()

        def arrive_first():
            far_copy(q // 2, 0, 0).wait_recv()
            far_copy(q // 2, 0, 1).wait_recv()

        if first:
            arrive_first()
        else:
            pl.when(lax.rem(q, 2) == 0)(arrive_first)

            @pl.when(lax.rem(q, 2) == 1)
            def _():
                unpack_second(q // 2)

        unpack_rest(far_rest[q].astype(F32))
        for k, cols in enumerate(chunks()):
            mid_sc[q, :, cols] = mid_sc[q, :, cols] + with_rest(far_sc[q, :, cols].astype(F32), k)

    def middle_sums(q, carry):
        @pl.when(q > 0)
        def _():
            middle_view(q, False)

        first, second = None, None
        for cols in chunks():
            part = mid_sc[q, :, cols] - wide(colm_sc, 8)
            one, two = lane_fold(part), lane_fold(part * part)
            first = one if first is None else first + one
            second = two if second is None else second + two
        accm_sc[0] += first
        accm_sc[1] += second
        return carry

    middle_view(0, True)
    pivot = sum(lane_fold(mid_sc[0, :, cols]) for cols in chunks())
    colm_sc[8] = jnp.broadcast_to(jnp.sum(pivot, axis=1, keepdims=True) / CELLS, colm_sc.shape[1:])
    pivot_row = cols_to_row(padm_sc, pivot) / CELLS
    lax.fori_loop(0, quarter, middle_sums, 0)
    off_row = cols_to_row(padm_sc, accm_sc[0]) / owned_count
    cmsg_sc[0] = jnp.zeros_like(cmsg_sc[0])
    cmsg_sc[0, 0:2, :] = pivot_row + off_row
    cmsg_sc[0, 2:4, :] = cols_to_row(padm_sc, accm_sc[1]) - off_row * off_row * owned_count
    accm_sc[...] = jnp.zeros_like(accm_sc)
    cstat_sc[0, ci] = cmsg_sc[0]
    chan_send(3, same(cmsg_sc.at[0]), cstat_sc.at[0])
    far_start(quarter // 2, 0)
    far_start(quarter // 2, 1)
    dp_some(early, full)
    if left > 0:
        dp_load(full, left).start()
        dp_load(full, left).wait()
        dp_split(full, left)
    chan_wait(3, same(cmsg_sc.at[0]), cstat_sc.at[0])
    group_mean, group_dev = combine(cstat_sc[0], owned_count)
    msg_sc[0] = jnp.zeros_like(msg_sc[0])
    msg_sc[0, 0:2, :] = group_mean
    msg_sc[0, 2:4, :] = group_dev
    stat_sc[1, bi] = msg_sc[0]
    batch_send(1, same(msg_sc.at[0]), stat_sc.at[1])
    chan_wait(7, dfar_of, dn_sc.at[1])
    lax.fori_loop(0, quarter, back_slot, 0)
    batch_wait(1, same(msg_sc.at[0]), stat_sc.at[1])
    meanm_row, devm_row = combine(stat_sc[1], local_count)
    rstdm_row = lax.rsqrt(devm_row / pixels + EPS)
    row_to_cols(colm_sc.at[0], meanm_row)
    row_to_cols(colm_sc.at[1], rstdm_row)

    def mid_point(values):
        mean, rstd = wide(colm_sc, 0), wide(colm_sc, 1)
        norm = (values - mean) * rstd
        pre = norm * wide(colm_sc, 2) + wide(colm_sc, 3)
        s = sigmoid(pre)
        act = pre * s
        return norm, act, s + act * (1.0 - s)

    def mid_own(q, carry):
        first, second = None, None
        for cols in chunks():
            norm, act, slope = mid_point(mid_sc[q, :, cols])
            actm_sc[q, :, cols] = act.astype(BF16)
            grad = d_sc[quarter + q, :, cols] * slope
            d_sc[quarter + q, :, cols] = grad
            mid_sc[q, :, cols] = norm
            one, two = lane_fold(grad), lane_fold(grad * norm)
            first = one if first is None else first + one
            second = two if second is None else second + two
        accm_sc[0] += first
        accm_sc[1] += second
        return carry

    lax.fori_loop(0, quarter, mid_own, 0)
    cmsg_sc[1] = jnp.zeros_like(cmsg_sc[1])
    cmsg_sc[1, 0:2, :] = cols_to_row(padm_sc, accm_sc[0])
    cmsg_sc[1, 2:4, :] = cols_to_row(padm_sc, accm_sc[1])
    cstat_sc[1, ci] = cmsg_sc[1]
    chan_send(4, same(cmsg_sc.at[1]), cstat_sc.at[1])
    for q in range(2, quarter):
        far_start((quarter + q) // 2, q % 2)

    def tiles_of(ref):
        rows, cols = ref.shape
        return [(r, l, min(128, cols - 128 * l)) for r in range(rows // 16) for l in range(-(-cols // 128))]

    def scatter(refs, kind, values):
        out, back, _ = refs
        per = out.shape[1]
        for at, (r, l, width) in enumerate(tiles_of(values)):
            tile = values[16 * r : 16 * r + 16, 128 * l : 128 * l + width]
            out[at // per, at % per, :, 0:width] = tile.astype(BF16)
        back[bi] = out[bi]
        batch_send(kind, lambda other: out.at[other], back)

    def reduce_gather(refs, kind):
        out, back, whole = refs
        batch_wait(kind, lambda other: out.at[other], back)
        total = back[0].astype(F32)
        for at in range(1, nb):
            total = total + back[at].astype(F32)
        out[bi] = total.astype(BF16)
        whole[bi] = total.astype(BF16)
        batch_send(kind + 1, same(out.at[bi]), whole)

    def gather(refs, kind, ref):
        out, _, whole = refs
        per = out.shape[1]
        batch_wait(kind + 1, same(out.at[bi]), whole)
        for at, (r, l, width) in enumerate(tiles_of(ref)):
            tile = whole[at // per, at % per, :, 0:width]
            ref[16 * r : 16 * r + 16, 128 * l : 128 * l + width] = tile.astype(F32)

    spread_refs, reduce_refs = (ws_out, ws_in, ws_all), (wr_out, wr_back, wr_all)

    def spread_grad(q, carry):
        wsg_sc[...] += dot_nt(actm_sc[q], dcol_sc[q])
        return carry

    lax.fori_loop(0, quarter, spread_grad, 0)
    scatter(spread_refs, 4, wsg_sc)
    chan_wait(4, same(cmsg_sc.at[1]), cstat_sc.at[1])
    msg_sc[1] = (cstat_sc[1, 0] + cstat_sc[1, 1]) + (cstat_sc[1, 2] + cstat_sc[1, 3])
    stat_sc[2, bi] = msg_sc[1]
    batch_send(2, same(msg_sc.at[1]), stat_sc.at[2])
    def spread(q, carry):
        for k, cols in enumerate(chunks()):
            taps = dot(wf_sc[...], actm_sc[q, :, cols])
            for l in range(2):
                flat_sc[2 * k + l, 0 : TAPS * NEW_PAD, :] = taps[:, 128 * l : 128 * (l + 1)]
        total = None
        for b in range(3):
            column = None
            for a in range(3):
                t = 3 * a + b
                tap = [flat_sc[l, NEW_PAD * t : NEW_PAD * t + 40, :] for l in range(CELLS // 128)]
                tap = at_offset(jnp.concatenate(tap, axis=1), a - 1, 0)
                column = tap if column is None else column + tap
            column = at_offset(column, 0, b - 1)
            total = column if total is None else total + column
        for b in range(4):
            newo_sc[b, q] = total[0:n_new, CHUNK * b : CHUNK * (b + 1)].astype(BF16)
        return carry

    lax.fori_loop(0, quarter, spread, 0)
    new_of = lambda other: newo_sc.at[other]
    newi_sc[ci] = newo_sc[ci]
    reduce_gather(spread_refs, 4)
    batch_wait(2, same(msg_sc.at[1]), stat_sc.at[2])
    mid_sums = stat_sc[2, 0]
    for at in range(1, nb):
        mid_sums = mid_sums + stat_sc[2, at]
    row_to_cols(colm_sc.at[4], mid_sums[0:2, :] / pixels)
    row_to_cols(colm_sc.at[5], mid_sums[2:4, :] / pixels)
    row_to_cols(colm_sc.at[6], gathered(2) * rstdm_row)

    def dm_copy(i, h):
        return pltpu.make_async_remote_copy(
            src_ref=dm_out.at[i, :, half_cols(h)],
            dst_ref=dm_in.at[i, :, half_cols(h)],
            send_sem=dm_s.at[i, h],
            recv_sem=dm_r.at[i, h],
            device_id=mate,
            device_id_type=MESH,
        )

    def store(n):
        return pltpu.make_async_copy(slope_sc.at[n], dv_hbm.at[n], store_sem.at[n])

    def back_view(n, dm_ref):
        mean, scale = wide(col_sc, 0), wide(col_sc, 2)
        first, second = None, None
        for cols in chunks():
            grad = dot(wr_sc[...], dm_ref[:, cols]) * slope_sc[n, 0:n_in, cols].astype(F32)
            slope_sc[n, 0:n_in, cols] = (grad * scale + dp_sc[n, :, cols].astype(F32)).astype(BF16)
            off = x_sc[n, 0:n_in, cols].astype(F32) - mean
            one, two = lane_fold(grad), lane_fold(grad * off)
            first = one if first is None else first + one
            second = two if second is None else second + two
        acc_sc[0] += first
        acc_sc[1] += second
        wg_sc[:, 0:n_in] += dot_nt(dm_ref[...], act_sc[n])

    def dm_own(q, carry):
        i = quarter + q
        for cols in chunks():
            grad = d_sc[i, :, cols] - wide(colm_sc, 4) - mid_sc[q, :, cols] * wide(colm_sc, 5)
            dm_out[i, :, cols] = (grad * wide(colm_sc, 6)).astype(BF16)
        dm_copy(i, 0).start()
        dm_copy(i, 1).start()
        return carry

    lax.fori_loop(0, quarter, dm_own, 0)

    def back_mate(i):
        dm_copy(i, 0).wait_recv()
        dm_copy(i, 1).wait_recv()
        back_view(slot_view(i, 1 - c), dm_in.at[i])

    def back_own(q, carry):
        back_view(slot_view(quarter + q, c), dm_out.at[quarter + q])

        @pl.when(q > 0)
        def _():
            back_mate(quarter + q - 1)

        return carry

    lax.fori_loop(0, quarter, back_own, 0)
    back_mate(2 * quarter - 1)

    def back_far(q, carry):
        m = quarter // 2 + q // 2
        rest_copy(quarter + q).wait_recv()
        unpack_rest(pair_rest[q].astype(F32) + far_rest[quarter + q].astype(F32))

        @pl.when(lax.rem(q, 2) == 0)
        def _():
            far_copy(m, 0, 0).wait_recv()
            far_copy(m, 0, 1).wait_recv()

        @pl.when(lax.rem(q, 2) == 1)
        def _():
            unpack_second(m)

        for k, cols in enumerate(chunks()):
            part = pair_sc[q, :, cols].astype(F32) + far_sc[quarter + q, :, cols].astype(F32)
            norm, act, slope = mid_point(with_rest(part, k))
            grad = d_sc[q, :, cols] * slope - wide(colm_sc, 4) - norm * wide(colm_sc, 5)
            dm_out[q, :, cols] = (grad * wide(colm_sc, 6)).astype(BF16)
            if k % 2 == 1:
                dm_copy(q, k // 2).start()
        back_view(slot_view(q, c), dm_out.at[q])

        @pl.when(q > 0)
        def _():
            back_mate(q - 1)

        return carry

    lax.fori_loop(0, quarter // 2, back_far, 0)
    gather(spread_refs, 4, wsg_sc)
    for b in range(4):
        wsp_sc[b, 0:40, :] = wsg_sc[n_own * b : n_own * b + 40, :].astype(BF16)
    wsgi_sc[ci] = wsp_sc[ci]
    wsg_of = lambda other: wsp_sc.at[other]
    chan_send(6, wsg_of, wsgi_sc)
    chan_send(5, new_of, newi_sc)
    lax.fori_loop(quarter // 2, quarter, back_far, 0)
    back_mate(quarter - 1)

    scatter(reduce_refs, 6, wg_sc)
    msg_sc[2] = jnp.zeros_like(msg_sc[2])
    msg_sc[2, 0:2, :] = cols_to_row(padc_sc, acc_sc[0])
    msg_sc[2, 2:4, :] = cols_to_row(padc_sc, acc_sc[1]) * rstd_row
    stat_sc[3, bi] = msg_sc[2]
    batch_send(3, same(msg_sc.at[2]), stat_sc.at[3])
    reduce_gather(reduce_refs, 6)
    batch_wait(3, same(msg_sc.at[2]), stat_sc.at[3])
    total = stat_sc[3, 0]
    for at in range(1, nb):
        total = total + stat_sc[3, at]
    gain_scale = gain_row * rstd_row
    row_to_cols(col_sc.at[4], -gain_scale * rstd_row * (total[2:4, :] / pixels))
    row_to_cols(col_sc.at[5], -gain_scale * (total[0:2, :] / pixels))

    def finish(n, carry):
        mean, slant, level = wide(col_sc, 0), wide(col_sc, 4), wide(col_sc, 5)
        for cols in chunks():
            rest = (x_sc[n, 0:n_in, cols].astype(F32) - mean) * slant + level
            slope_sc[n, 0:n_in, cols] = (slope_sc[n, 0:n_in, cols].astype(F32) + rest).astype(BF16)
        store(n).start()
        return carry

    lax.fori_loop(0, n_views, finish, 0)

    sums_ref[...] = jnp.zeros_like(sums_ref)
    sums_ref[0:1, :] = one_row(total[2:4, :])
    sums_ref[1:2, :] = one_row(total[0:2, :])
    all_sums = jnp.concatenate([one_row(mid_sums[2:4, :]), one_row(mid_sums[0:2, :]), jnp.zeros((6, 256), F32)], axis=0)
    own_sums = all_sums
    for b in range(1, 4):
        own_sums = jnp.where(ci == b, pltpu.roll(all_sums, 256 - n_own * b, 1), own_sums)
    sums_ref[2:4, :] = own_sums[0:2, :]

    chan_wait(5, new_of, newi_sc)
    for b in range(4):
        for q in range(quarter):
            new_ref[quarter * b + q] = newi_sc[b, q]
    chan_wait(6, wsg_of, wsgi_sc)
    wsg_total = (wsgi_sc[0].astype(F32) + wsgi_sc[1].astype(F32)) + (
        wsgi_sc[2].astype(F32) + wsgi_sc[3].astype(F32)
    )
    wsg_ref[...] = wsg_total[0:n_own, :]
    gather(reduce_refs, 6, wg_sc)
    wrg_ref[...] = wg_sc[0 : wrg_ref.shape[0], 0:n_in]

    def stored(n, carry):
        store(n).wait()
        return carry

    lax.fori_loop(0, n_views, stored, 0)

    def sent(i, carry):
        rest_copy(i).wait_send()
        for h in range(2):
            half_copy(i, h).wait_send()
            dm_copy(i, h).wait_send()
        return carry

    lax.fori_loop(0, 2 * quarter, sent, 0)

    def sent_far(m, carry):
        for v in range(2):
            for h in range(2):
                far_copy(m, v, h).wait_send()
        return carry

    lax.fori_loop(0, quarter, sent_far, 0)


def layer(nb, crops, flips, views, stats, vectors, wr_t, w_spread, d_new, d_passed):
    n_views, n_rows, _ = views.shape
    n_mid, n_in = wr_t.shape
    n_own = n_mid // 4
    quarter = n_views // 4
    n_new = d_new.shape[0]
    n_cols = TAPS * NEW_PAD
    together = -(-quarter * n_new // 16) * 16
    in_pad = -(-n_in // 16) * 16
    ws_tiles = -(-(MID_PAD // 16 * -(-n_cols // 128)) // nb)
    wr_tiles = -(-(MID_PAD // 16 * -(-in_pad // 128)) // nb)
    group = 16
    vmem = pl.BlockSpec(memory_space=pltpu.VMEM)
    anywhere = pl.BlockSpec(memory_space=pl.ANY)
    smem = pl.BlockSpec(memory_space=pltpu.SMEM)
    dma = pltpu.SemaphoreType.DMA
    slots = 2 * quarter
    return pl.pallas_call(
        functools.partial(layer_kernel, nb),
        in_specs=[smem, smem, anywhere] + [vmem] * 8 + [anywhere],
        out_specs=[anywhere, vmem, vmem, vmem, vmem],
        out_shape=[
            jax.ShapeDtypeStruct((n_views, n_rows, CELLS), BF16),
            jax.ShapeDtypeStruct((n_views, n_new, CHUNK), BF16),
            jax.ShapeDtypeStruct((n_mid, n_in), F32),
            jax.ShapeDtypeStruct((n_own, n_cols), F32),
            jax.ShapeDtypeStruct((8, 256), F32),
        ],
        scratch_shapes=[
            pltpu.VMEM((n_views, n_rows, CELLS), BF16),
            pltpu.VMEM((n_views, n_in, CELLS), BF16),
            pltpu.VMEM((n_views, n_rows, CELLS), BF16),
            pltpu.VMEM((n_views, n_in, CELLS), BF16),
            pltpu.VMEM((slots, MID_PAD, CELLS), BF16),
            pltpu.VMEM((slots, MID_PAD, CELLS), BF16),
            pltpu.VMEM((slots, MAIN, CELLS), BF16),
            pltpu.VMEM((slots, MAIN, CELLS), BF16),
            pltpu.VMEM((slots, 16, CHUNK), BF16),
            pltpu.VMEM((slots, 16, CHUNK), BF16),
            pltpu.VMEM((16, CHUNK), F32),
            pltpu.VMEM((CELLS // CHUNK, 8, CHUNK), F32),
            pltpu.VMEM((quarter, MAIN, CELLS // 2 + CHUNK), BF16),
            pltpu.VMEM((quarter, CELLS, CHUNK), BF16),
            pltpu.VMEM((CELLS // 2, CELLS // 2), BF16),
            pltpu.VMEM((slots, MID_PAD, CELLS), F32),
            pltpu.VMEM((quarter + 1, n_cols, CELLS), BF16),
            pltpu.VMEM((quarter, MID_PAD, CELLS), F32),
            pltpu.VMEM((quarter, MID_PAD, CELLS), BF16),
            pltpu.VMEM((slots, MID_PAD, CELLS), BF16),
            pltpu.VMEM((slots, MID_PAD, CELLS), BF16),
            pltpu.VMEM((2, 2, together, CHUNK), BF16),
            pltpu.VMEM((2, 4, together, CHUNK), BF16),
            pltpu.VMEM((together, 128), F32),
            pltpu.VMEM((NEW_PAD, CELLS), F32),
            pltpu.VMEM((2, group, n_views, CELLS), BF16),
            pltpu.VMEM((CELLS // 128, max(max(group, n_new) * (n_views + 1), n_cols), 128), F32),
            pltpu.VMEM((8, 256), F32),
            pltpu.VMEM((4, 8, 256), F32),
            pltpu.VMEM((4, NEW_PAD, n_cols), BF16),
            pltpu.VMEM((n_in, MID_PAD), BF16),
            pltpu.VMEM((MID_PAD, n_in), BF16),
            pltpu.VMEM((MID_PAD, n_cols), BF16),
            pltpu.VMEM((n_cols, MID_PAD), BF16),
            pltpu.VMEM((4, nb, 8, 128), F32),
            pltpu.VMEM((2, 4, 8, 128), F32),
            pltpu.VMEM((3, 8, 128), F32),
            pltpu.VMEM((2, 8, 128), F32),
            pltpu.VMEM((6, n_in, 128), F32),
            pltpu.VMEM((9, MID_PAD, 128), F32),
            pltpu.VMEM((256, 128), F32),
            pltpu.VMEM((256, 128), F32),
            pltpu.VMEM((2, n_in, 128), F32),
            pltpu.VMEM((2, MID_PAD, 128), F32),
            pltpu.VMEM((MID_PAD, in_pad), F32),
            pltpu.VMEM((MID_PAD, n_cols), F32),
            pltpu.VMEM((4, NEW_PAD, n_cols), BF16),
            pltpu.VMEM((nb, ws_tiles, 16, 128), BF16),
            pltpu.VMEM((nb, ws_tiles, 16, 128), BF16),
            pltpu.VMEM((nb, ws_tiles, 16, 128), BF16),
            pltpu.VMEM((nb, wr_tiles, 16, 128), BF16),
            pltpu.VMEM((nb, wr_tiles, 16, 128), BF16),
            pltpu.VMEM((nb, wr_tiles, 16, 128), BF16),
            pltpu.VMEM((4, quarter, n_new, CHUNK), BF16),
            pltpu.VMEM((4, quarter, n_new, CHUNK), BF16),
            dma((n_views,)),
            dma((n_views,)),
            dma((slots, 2)),
            dma((slots, 2)),
            dma((slots, 2)),
            dma((slots, 2)),
            dma((slots,)),
            dma((slots,)),
            dma((slots, 2)),
            dma((slots, 2)),
            dma((8, nb)),
            dma((8, nb)),
            dma((8, 4)),
            dma((8, 4)),
            dma((2,)),
        ],
        compiler_params=pltpu.CompilerParams(
            collective_id=0, has_side_effects=True, vmem_limit_bytes=VMEM_LIMIT
        ),
        name="layer",
    )(crops, flips, views, stats, *vectors, wr_t, w_spread, d_new, d_passed)


def solution(mesh):
    nb = mesh.shape["batch"]

    def on_device(features, crops, flips, gain_in, shift_in, w_reduce, gain_mid, shift_mid, w_spread, d_passed, d_new):
        n_own, n_new = w_spread.shape[0], w_spread.shape[3]

        w9 = jnp.transpose(w_spread, (1, 2, 0, 3)).reshape(TAPS, n_own, n_new)
        crops_t, flips_t = jnp.transpose(crops, (1, 2, 0)), jnp.transpose(flips)
        swap = lambda v: jnp.transpose(v, (1, 0, 2))
        views, passed, stats = crop_views(swap(features), crops_t, flips_t)
        dv, new_maps, wr_grad, ws_grad, sums = layer(
            nb, crops_t, flips_t, views, stats, (gain_in, shift_in, gain_mid, shift_mid), jnp.transpose(w_reduce), w9, swap(d_new), swap(d_passed)
        )
        features_grad, new_maps, wr_grad, ws_grad, *grads = place_views(
            crops_t, flips_t, dv, new_maps, wr_grad, ws_grad, sums
        )
        ws_grad = jnp.transpose(ws_grad.reshape(3, 3, n_own, n_new), (2, 0, 1, 3))
        return (swap(passed), swap(new_maps), swap(features_grad), jnp.transpose(wr_grad), ws_grad, *grads)

    return jax.shard_map(
        on_device,
        mesh=mesh,
        in_specs=(
            P("batch", "chan", None),
            P("batch", None, None),
            P("batch", None),
            P("chan"),
            P("chan"),
            P("chan", None),
            P("chan"),
            P("chan"),
            P("chan", None, None, None),
            P("batch", "chan", None),
            P("batch", None, "chan"),
        ),
        out_specs=(
            P("batch", "chan", None),
            P("batch", None, "chan"),
            P("batch", "chan", None),
            P("chan", None),
            P("chan", None, None, None),
            P("chan"),
            P("chan"),
            P("chan"),
            P("chan"),
        ),
        check_vma=False,
    )
```

```python
import functools

import jax
import jax.numpy as jnp
from jax import lax
from jax.experimental import pallas as pl
from jax.experimental.pallas import tpu as pltpu
from jax.sharding import PartitionSpec as P

H = 32
W = 32
MARGIN = 8
GRID = H + 2 * MARGIN
CELLS = H * W
EPS = 1e-05
CHUNK = 256
SPAN = 512
STRIDE = 8 * GRID
TAPS = 9
BLOCK = 80
MID_PAD = 144
NEW_PAD = 48
MAIN = 128
REST = 4
F32 = jnp.float32
BF16 = jnp.bfloat16
MESH = pl.DeviceIdType.MESH
VMEM_LIMIT = 63 * 2**20 + 800 * 2**10


def dot(a, b):
    return jnp.dot(a, b, preferred_element_type=F32)


def dot_nt(a, b):
    return lax.dot_general(a, b, (((1,), (1,)), ((), ())), preferred_element_type=F32)


def iota(shape, axis):
    return lax.broadcasted_iota(jnp.int32, shape, axis)


def lane_fold(values):
    total = values[:, 0:128]
    for at in range(128, values.shape[1], 128):
        total = total + values[:, at : at + 128]
    return total


def cols_to_row(pad_ref, values):
    if values is not None:
        pad_ref[0 : values.shape[0], :] = values
    halves = [
        jnp.sum(jnp.transpose(pad_ref[at : at + 128, :]), axis=0, keepdims=True)
        for at in (0, 128)
    ]
    return jnp.concatenate(halves, axis=0)


def two_rows(row):
    return jnp.concatenate([row[:, 0:128], row[:, 128:256]], axis=0)


def one_row(rows):
    return jnp.concatenate([rows[0:1, :], rows[1:2, :]], axis=1)


def row_to_cols(out_ref, row):
    rows = out_ref.shape[0]
    for h, at in enumerate((0, 128)):
        height = min(128, rows - at)
        square = jnp.broadcast_to(row[h : h + 1, :], (128, 128))
        out_ref[at : at + height, :] = jnp.transpose(square)[0:height, :]


def window_start(crops_ref, j, v):
    start = crops_ref[v, 0, j] * GRID + crops_ref[v, 1, j]
    base = jnp.minimum((start // 128) * 128, GRID * GRID - 3 * STRIDE - SPAN)
    return pl.multiple_of(base, 128), start - base


def chunk_target(offset, flip, cell):
    col = cell & (W - 1)
    row = cell >> 5
    return offset + row * GRID + jnp.where(flip > 0, W - 1 - col, col)


def blocks_of(channels):
    return [(at, min(BLOCK, channels - at)) for at in range(0, channels, BLOCK)]


def crop_kernel(crops_ref, flips_ref, x_hbm, views_hbm, passed_hbm, stats_ref, pick_sc, xn_sc, xf_sc, xi_sc, vw_sc, pf_sc, pn_sc, mean_sc, dev_sc, x_sem, vw_sem, pn_sem):
    channels, items, cells = x_hbm.shape
    n_views, rows, part_rows = 2 * items, BLOCK, 16
    blocks = blocks_of(channels)

    def load(at):
        first, size = blocks[at]
        return pltpu.make_async_copy(x_hbm.at[pl.ds(first, size)], xn_sc.at[at, pl.ds(0, size)], x_sem.at[at])

    def view_out(at, n):
        first = pl.multiple_of(at * rows, rows)
        return pltpu.make_async_copy(vw_sc.at[at, n], views_hbm.at[n, pl.ds(first, rows)], vw_sem.at[at, n])

    def passed_out(at, u):
        first, size = blocks[at]
        size = min(part_rows, size - part_rows * u)
        return pltpu.make_async_copy(
            pn_sc.at[at, pl.ds(part_rows * u, size)],
            passed_hbm.at[pl.ds(first + part_rows * u, size)],
            pn_sem.at[at, u],
        )

    for at in range(len(blocks)):
        load(at).start()

    def build(n, carry):
        j, v = n // 2, n % 2
        _, offset = window_start(crops_ref, j, v)
        target = chunk_target(offset, flips_ref[v, j], iota((1, CHUNK), 1))
        pick_sc[n] = (iota((SPAN, CHUNK), 0) == target).astype(BF16)
        return carry

    lax.fori_loop(0, n_views, build, 0)
    mean_sc[...] = jnp.zeros_like(mean_sc)
    dev_sc[...] = jnp.zeros_like(dev_sc)

    def block(b, carry):
        for at in range(len(blocks)):

            @pl.when(b == at)
            def _(at=at):
                load(at).wait()

        for l in range(cells // 128):
            at = slice(128 * l, 128 * (l + 1))
            wide_x = xn_sc[b, :, :, at].astype(F32)
            for ch in range(rows):
                xf_sc[l, (items + 1) * ch : (items + 1) * ch + items, :] = wide_x[ch]

        total = jnp.zeros((rows, 128), F32)
        squares = jnp.zeros((rows, 128), F32)
        pivot = None
        for j in range(items):
            for l in range(cells // 128):
                xi_sc[j, :, 128 * l : 128 * (l + 1)] = xf_sc[l, pl.ds(j, rows, stride=items + 1), :].astype(BF16)
            for v in range(2):
                n = 2 * j + v
                base, _ = window_start(crops_ref, j, v)
                spans = [xi_sc[j, :, pl.ds(pl.multiple_of(base + STRIDE * k, 128), SPAN)] for k in range(CELLS // CHUNK)]
                parts = dot(jnp.concatenate(spans, axis=0), pick_sc[n])
                for k in range(CELLS // CHUNK):
                    part = parts[rows * k : rows * (k + 1), :]
                    vw_sc[b, n, :, CHUNK * k : CHUNK * (k + 1)] = part.astype(BF16)
                    for l in range(2):
                        pf_sc[2 * k + l, pl.ds(n, rows, stride=n_views + 1), :] = part[:, 128 * l : 128 * (l + 1)]
                    if pivot is None:
                        pivot = jnp.sum(lane_fold(part), axis=1, keepdims=True) / CHUNK
                    off = part - pivot
                    total = total + lane_fold(off)
                    squares = squares + lane_fold(off * off)
                view_out(b, n).start()
        for u in range(rows // part_rows):
            for l in range(CELLS // 128):
                at = slice(128 * l, 128 * (l + 1))
                for ch in range(part_rows * u, part_rows * (u + 1)):
                    first = (n_views + 1) * ch
                    pn_sc[b, ch, :, at] = pf_sc[l, first : first + n_views, :].astype(BF16)
            for at in range(len(blocks)):

                @pl.when(b == at)
                def _(at=at):
                    passed_out(at, u).start()

        count = n_views * CELLS
        shift = jnp.sum(total, axis=1, keepdims=True) / count
        first = pl.multiple_of(b * rows, 8)
        lane = iota((rows, 128), 1)
        mean_sc[pl.ds(first, rows), :] = jnp.where(lane == 0, pivot + shift, 0.0)
        dev_sc[pl.ds(first, rows), :] = squares - jnp.where(lane == 0, shift * shift * count, 0.0)
        return carry

    lax.fori_loop(0, len(blocks), block, 0)
    stats_ref[...] = jnp.zeros_like(stats_ref)
    stats_ref[0:2, :] = cols_to_row(mean_sc, None)
    stats_ref[2:4, :] = cols_to_row(dev_sc, None)
    for at in range(len(blocks)):
        for n in range(n_views):
            view_out(at, n).wait()
        for u in range(rows // part_rows):
            passed_out(at, u).wait()


def crop_views(features, crops, flips):
    channels, items, cells = features.shape
    n_blocks = len(blocks_of(channels))
    anywhere = pl.BlockSpec(memory_space=pl.ANY)
    smem = pl.BlockSpec(memory_space=pltpu.SMEM)
    dma = pltpu.SemaphoreType.DMA
    return pl.pallas_call(
        crop_kernel,
        in_specs=[smem, smem, anywhere],
        out_specs=[anywhere, anywhere, pl.BlockSpec(memory_space=pltpu.VMEM)],
        out_shape=[
            jax.ShapeDtypeStruct((2 * items, n_blocks * BLOCK, CELLS), BF16),
            jax.ShapeDtypeStruct((channels, 2 * items, CELLS), BF16),
            jax.ShapeDtypeStruct((8, 128), F32),
        ],
        scratch_shapes=[
            pltpu.VMEM((2 * items, SPAN, CHUNK), BF16),
            pltpu.VMEM((n_blocks, BLOCK, items, cells), BF16),
            pltpu.VMEM((cells // 128, BLOCK * (items + 1), 128), F32),
            pltpu.VMEM((items, BLOCK, cells), BF16),
            pltpu.VMEM((n_blocks, 2 * items, BLOCK, CELLS), BF16),
            pltpu.VMEM((CELLS // 128, BLOCK * (2 * items + 1), 128), F32),
            pltpu.VMEM((n_blocks, BLOCK, 2 * items, CELLS), BF16),
            pltpu.VMEM((256, 128), F32),
            pltpu.VMEM((256, 128), F32),
            dma((n_blocks,)),
            dma((n_blocks, 2 * items)),
            dma((n_blocks, BLOCK // 16)),
        ],
        compiler_params=pltpu.CompilerParams(vmem_limit_bytes=VMEM_LIMIT),
        name="crop_views",
    )(crops, flips, features)


def place_kernel(crops_ref, flips_ref, dv_hbm, new_ref, wrg_ref, wsg_ref, sums_ref, out_hbm, newo_ref, wrgo_ref, wsgo_ref, gi_ref, si_ref, gm_ref, sm_ref, pick_sc, dv_sc, flat_sc, out_sc, new_sc, dv_sem, out_sem):
    channels, items, cells = out_hbm.shape
    n_views, rows, part_rows = 2 * items, BLOCK, 16
    blocks = blocks_of(channels)

    def load(at):
        first = at * rows if isinstance(at, int) else pl.multiple_of(at * rows, rows)
        return pltpu.make_async_copy(dv_hbm.at[:, pl.ds(first, rows)], dv_sc.at[at], dv_sem.at[at])

    def out(at, u):
        first, size = blocks[at]
        size = min(part_rows, size - part_rows * u)
        return pltpu.make_async_copy(
            out_sc.at[at, pl.ds(part_rows * u, size)],
            out_hbm.at[pl.ds(first + part_rows * u, size)],
            out_sem.at[at, u],
        )

    for at in range(len(blocks)):
        load(at).start()

    def build(n, carry):
        j, v = n // 2, n % 2
        _, offset = window_start(crops_ref, j, v)
        target = chunk_target(offset, flips_ref[v, j], iota((CHUNK, 1), 0))
        pick_sc[n] = (iota((CHUNK, SPAN), 1) == target).astype(BF16)
        return carry

    lax.fori_loop(0, n_views, build, 0)

    def block(b, carry):
        load(b).wait()
        flat_sc[...] = jnp.zeros_like(flat_sc)

        def place_item(j):
            for v in range(2):
                n = 2 * j + v
                base, _ = window_start(crops_ref, j, v)
                tile = base // 128
                parts = [dv_sc[b, n, :, CHUNK * k : CHUNK * (k + 1)] for k in range(CELLS // CHUNK)]
                spans = dot(jnp.concatenate(parts, axis=0), pick_sc[n])
                spans = [spans[rows * k : rows * (k + 1), :] for k in range(CELLS // CHUNK)]
                pieces = [spans[0][:, 0:STRIDE]]
                for k in range(1, CELLS // CHUNK):
                    pieces.append(spans[k - 1][:, STRIDE:SPAN] + spans[k][:, 0 : SPAN - STRIDE])
                    pieces.append(spans[k][:, SPAN - STRIDE : STRIDE])
                pieces.append(spans[-1][:, STRIDE:SPAN])
                window = jnp.concatenate(pieces, axis=1)
                of_item = pl.ds(j, rows, stride=items + 1)
                for t in range(window.shape[1] // 128):
                    piece = window[:, 128 * t : 128 * (t + 1)]
                    if v == 1:
                        piece = piece + flat_sc[tile + t, of_item, :]
                    flat_sc[tile + t, of_item, :] = piece

        def place_some(group, carry):
            for inner in range(4):
                place_item(4 * group + inner)
            return carry

        lax.fori_loop(0, items // 4, place_some, 0)
        for u in range(rows // part_rows):
            for l in range(cells // 128):
                for ch in range(part_rows * u, part_rows * (u + 1)):
                    first = (items + 1) * ch
                    out_sc[b, ch, :, 128 * l : 128 * (l + 1)] = flat_sc[l, first : first + items, :]
            for at in range(len(blocks)):

                @pl.when(b == at)
                def _(at=at):
                    out(at, u).start()

        return carry

    lax.fori_loop(0, len(blocks), block, 0)

    n_new = new_ref.shape[1]
    for n in range(n_views):
        for l in range(2):
            piece = new_ref[n, :, 128 * l : 128 * (l + 1)]
            new_sc[l, pl.ds(n, n_new, stride=n_views), :] = piece.astype(F32)
    for l in range(2):
        newo_ref[:, :, 128 * l : 128 * (l + 1)] = new_sc[l].reshape(n_new, n_views, 128).astype(BF16)
    wrgo_ref[...] = wrg_ref[...]
    for t in range(TAPS):
        wsgo_ref[t] = wsg_ref[:, NEW_PAD * t : NEW_PAD * t + wsgo_ref.shape[2]]
    for at, ref in enumerate((gi_ref, si_ref, gm_ref, sm_ref)):
        ref[...] = sums_ref[at, 0 : ref.shape[0]]
    for at in range(len(blocks)):
        for u in range(rows // part_rows):
            out(at, u).wait()


def place_views(crops, flips, dv, new_maps, wr_grad, ws_grad, sums):
    items, channels = crops.shape[2], wr_grad.shape[1]
    n_views, n_blocks = dv.shape[0], dv.shape[1] // BLOCK
    n_new, n_own = new_maps.shape[1], ws_grad.shape[0]
    cells = GRID * GRID
    anywhere = pl.BlockSpec(memory_space=pl.ANY)
    vmem = pl.BlockSpec(memory_space=pltpu.VMEM)
    smem = pl.BlockSpec(memory_space=pltpu.SMEM)
    dma = pltpu.SemaphoreType.DMA
    small = [
        ((n_new, n_views, CHUNK), BF16),
        (wr_grad.shape, F32),
        ((TAPS, n_own, n_new), F32),
        ((channels,), F32),
        ((channels,), F32),
        ((n_own,), F32),
        ((n_own,), F32),
    ]
    return pl.pallas_call(
        place_kernel,
        in_specs=[smem, smem, anywhere] + [vmem] * 4,
        out_specs=[anywhere] + [vmem] * len(small),
        out_shape=[jax.ShapeDtypeStruct((channels, items, cells), F32)]
        + [jax.ShapeDtypeStruct(shape, kind) for shape, kind in small],
        scratch_shapes=[
            pltpu.VMEM((n_views, CHUNK, SPAN), BF16),
            pltpu.VMEM((n_blocks, n_views, BLOCK, CELLS), BF16),
            pltpu.VMEM((cells // 128, BLOCK * (items + 1), 128), F32),
            pltpu.VMEM((n_blocks, BLOCK, items, cells), F32),
            pltpu.VMEM((2, n_new * n_views, 128), F32),
            dma((n_blocks,)),
            dma((n_blocks, BLOCK // 16)),
        ],
        compiler_params=pltpu.CompilerParams(vmem_limit_bytes=VMEM_LIMIT),
        name="place_views",
    )(crops, flips, dv, new_maps, wr_grad, ws_grad, sums)


def sigmoid(v):
    return 0.5 * jnp.tanh(0.5 * v) + 0.5


def combine(parts, count):
    groups = parts.shape[0]
    mean = parts[0, 0:2, :]
    dev = parts[0, 2:4, :]
    for at in range(1, groups):
        mean = mean + parts[at, 0:2, :]
        dev = dev + parts[at, 2:4, :]
    mean = mean / groups
    spread = None
    for at in range(groups):
        off = parts[at, 0:2, :] - mean
        spread = off * off if spread is None else spread + off * off
    return mean, dev + spread * count


def layer_kernel(
    nb,
    crops_ref,
    flips_ref,
    views_hbm,
    stats_ref,
    gain_in_ref,
    shift_in_ref,
    gain_mid_ref,
    shift_mid_ref,
    wr_in,
    wsp_in,
    dnew_ref,
    dpass_hbm,
    dv_hbm,
    new_ref,
    wrg_ref,
    wsg_ref,
    sums_ref,
    x_sc,
    act_sc,
    slope_sc,
    dp_sc,
    half_out,
    half_in,
    pair_sc,
    far_sc,
    pair_rest,
    far_rest,
    pack_sc,
    ext_sc,
    packed_sc,
    find_sc,
    join_sc,
    d_sc,
    dcol_sc,
    mid_sc,
    actm_sc,
    dm_out,
    dm_in,
    dno_sc,
    dn_sc,
    pack_dn,
    dnf_sc,
    dpn_sc,
    flat_sc,
    own_par,
    par_sc,
    wsp_sc,
    wr_sc,
    wrt_sc,
    wb_sc,
    wf_sc,
    stat_sc,
    cstat_sc,
    msg_sc,
    cmsg_sc,
    col_sc,
    colm_sc,
    padc_sc,
    padm_sc,
    acc_sc,
    accm_sc,
    wg_sc,
    wsg_sc,
    wsgi_sc,
    ws_out,
    ws_in,
    ws_all,
    wr_out,
    wr_back,
    wr_all,
    newo_sc,
    newi_sc,
    load_sem,
    store_sem,
    half_s,
    half_r,
    far_s,
    far_r,
    rest_s,
    rest_r,
    dm_s,
    dm_r,
    bat_s,
    bat_r,
    chan_s,
    chan_r,
    dp_sem,
):
    bi, ci = lax.axis_index("batch"), lax.axis_index("chan")
    y, c = ci // 2, lax.rem(ci, 2)
    n_views, n_in = x_sc.shape[0], act_sc.shape[1]
    quarter = n_views // 4
    n_own, n_new = wsg_ref.shape[0], dnew_ref.shape[0]
    local_count = float(n_views * CELLS)
    owned_count = float(quarter * CELLS)
    pixels = float(nb) * local_count
    mate = (bi, 2 * y + (1 - c))
    across = (bi, 2 * (1 - y) + c)

    def batch_peer(k):
        return (lax.rem(bi + k, nb), ci)

    def chan_peer(k):
        return (bi, lax.rem(ci + k, 4))

    barrier = pltpu.get_barrier_semaphore()

    def greet(k, carry):
        pl.semaphore_signal(barrier, inc=1, device_id=batch_peer(k), device_id_type=MESH)
        return carry

    lax.fori_loop(1, nb, greet, 0)
    for k in range(1, 4):
        pl.semaphore_signal(barrier, inc=1, device_id=chan_peer(k), device_id_type=MESH)

    def load(n):
        return pltpu.make_async_copy(views_hbm.at[n], x_sc.at[n], load_sem.at[n])

    def load_step(i, carry):
        load(slot_view(i, 1 - c)).start()
        load(slot_view(i, c)).start()
        return carry

    def slot_view(i, core):
        h = jnp.where(i < quarter, 1 - y, y)
        return quarter * (2 * h + core) + lax.rem(i, quarter)

    lax.fori_loop(0, 2 * quarter, load_step, 0)
    pl.semaphore_wait(barrier, nb + 2)

    def batch_copy(kind, k, src, dst):
        return pltpu.make_async_remote_copy(
            src_ref=src,
            dst_ref=dst,
            send_sem=bat_s.at[kind, k],
            recv_sem=bat_r.at[kind, k],
            device_id=batch_peer(k),
            device_id_type=MESH,
        )

    def batch_send(kind, src_of, dst):
        def step(k, carry):
            batch_copy(kind, k, src_of(lax.rem(bi + k, nb)), dst.at[bi]).start()
            return carry

        lax.fori_loop(1, nb, step, 0)

    def batch_wait(kind, src_of, dst):
        def step(k, carry):
            other = lax.rem(bi + nb - k, nb)
            batch_copy(kind, k, src_of(lax.rem(bi + k, nb)), dst.at[other]).wait()
            return carry

        lax.fori_loop(1, nb, step, 0)

    def chan_copy(kind, k, src, dst):
        return pltpu.make_async_remote_copy(
            src_ref=src,
            dst_ref=dst,
            send_sem=chan_s.at[kind, k],
            recv_sem=chan_r.at[kind, k],
            device_id=chan_peer(k),
            device_id_type=MESH,
        )

    def chan_send(kind, src_of, dst):
        for k in range(1, 4):
            chan_copy(kind, k, src_of(lax.rem(ci + k, 4)), dst.at[ci]).start()

    def chan_wait(kind, src_of, dst):
        for k in range(1, 4):
            other = lax.rem(ci + 4 - k, 4)
            chan_copy(kind, k, src_of(lax.rem(ci + k, 4)), dst.at[other]).wait()

    def wide(ref, at):
        col = ref[at]
        return jnp.concatenate([col, col], axis=1)

    def same(ref):
        return lambda other: ref

    stat_sc[0, bi] = stats_ref[...]
    batch_send(0, same(stats_ref), stat_sc.at[0])
    own_par[...] = jnp.zeros_like(own_par)
    for at, ref in enumerate((gain_in_ref, shift_in_ref, gain_mid_ref, shift_mid_ref)):
        own_par[at : at + 1, 0 : ref.shape[0]] = ref[...].astype(F32).reshape(1, ref.shape[0])
    par_sc[ci] = own_par[...]
    chan_send(0, same(own_par), par_sc)
    dnf_sc[...] = jnp.zeros_like(dnf_sc)
    for t in range(TAPS):
        dnf_sc[0:n_own, NEW_PAD * t : NEW_PAD * t + n_new] = wsp_in[t].astype(F32)
    wsp_sc[ci] = dnf_sc[:, 0 : TAPS * NEW_PAD].astype(BF16)
    wsp_own = same(wsp_sc.at[ci])

    pack_dn[...] = jnp.zeros_like(pack_dn)
    for l in range(2):
        at = slice(128 * l, 128 * (l + 1))
        native = dnew_ref[:, :, at].astype(F32)
        for ch in range(n_new):
            flat_sc[l, (n_views + 1) * ch : (n_views + 1) * ch + n_views, :] = native[ch]
        for block in range(4):
            for q in range(quarter):
                by_view = flat_sc[l, pl.ds(quarter * block + q, n_new, stride=n_views + 1), :]
                pack_dn[n_new * q : n_new * (q + 1), :] = by_view
            dno_sc[block % 2, block // 2, :, at] = pack_dn[...].astype(BF16)
    dn_sc[0, ci] = dno_sc[c, y]
    dn_sc[1, ci] = dno_sc[c, 1 - y]
    dnew_of = lambda other: dno_sc.at[lax.rem(other, 2), other // 2]
    dfar_of = lambda other: dno_sc.at[lax.rem(other, 2), 1 - other // 2]
    chan_send(2, dnew_of, dn_sc.at[0])
    chan_send(1, wsp_own, wsp_sc)

    padc_sc[...] = jnp.zeros_like(padc_sc)
    padm_sc[...] = jnp.zeros_like(padm_sc)
    acc_sc[...] = jnp.zeros_like(acc_sc)
    accm_sc[...] = jnp.zeros_like(accm_sc)
    wg_sc[...] = jnp.zeros_like(wg_sc)
    wsg_sc[...] = jnp.zeros_like(wsg_sc)
    ext_sc[...] = jnp.zeros_like(ext_sc)
    piece, place = iota((CELLS // 2, CELLS // 2), 0), iota((CELLS // 2, CELLS // 2), 1)
    joined_at = ((piece & 255) >> 4) * W + (piece >> 8) * 16 + (piece & 15)
    join_sc[...] = (joined_at == place).astype(BF16)
    ws_out[...] = jnp.zeros_like(ws_out)
    wr_out[...] = jnp.zeros_like(wr_out)
    wrt_sc[...] = jnp.zeros_like(wrt_sc)
    wrt_sc[0 : wr_in.shape[0], :] = wr_in[...]
    eye = (iota((n_in, n_in), 0) == iota((n_in, n_in), 1)).astype(BF16)
    wr_sc[...] = dot_nt(eye, wrt_sc[...]).astype(BF16)
    gain_row = two_rows(own_par[0:1, :])
    shift_row = two_rows(own_par[1:2, :])

    gain_col, shift_col = (jnp.transpose(jnp.broadcast_to(one_row(v), (256, 256)))[0:n_in, 0:128] for v in (gain_row, shift_row))
    guess = None
    for weight, offset in ((2 / 3, 0.0), (1 / 6, 3.0**0.5), (1 / 6, -(3.0**0.5))):
        pre = shift_col + offset * gain_col
        part = weight * pre * sigmoid(pre)
        guess = part if guess is None else guess + part
    colm_sc[7] = dot(wrt_sc[...], guess.astype(BF16))

    batch_wait(0, same(stats_ref), stat_sc.at[0])
    mean_row, dev_row = combine(stat_sc[0], local_count)
    rstd_row = lax.rsqrt(dev_row / pixels + EPS)
    row_to_cols(col_sc.at[0], mean_row)
    row_to_cols(col_sc.at[1], rstd_row)
    row_to_cols(col_sc.at[2], rstd_row * gain_row)
    row_to_cols(col_sc.at[3], shift_row)

    def chunks(start=0, count=CELLS // CHUNK):
        if isinstance(start, int):
            return [slice(start + CHUNK * k, start + CHUNK * (k + 1)) for k in range(count)]
        return [pl.ds(pl.multiple_of(start + CHUNK * k, CHUNK), CHUNK) for k in range(count)]

    half = CELLS // 2

    def half_cols(h):
        return pl.ds(h * half if isinstance(h, int) else pl.multiple_of(h * half, half), half)

    def activate(n):
        mean, scale, shift = wide(col_sc, 0), wide(col_sc, 2), wide(col_sc, 3)
        for cols in chunks():
            pre = (x_sc[n, 0:n_in, cols].astype(F32) - mean) * scale + shift
            s = sigmoid(pre)
            act = pre * s
            slope_sc[n, 0:n_in, cols] = (s + act * (1.0 - s)).astype(BF16)
            act_sc[n, :, cols] = act.astype(BF16)

    def partial(n, cols):
        return dot(wrt_sc[...], act_sc[n, :, cols]) - wide(colm_sc, 7)

    def half_copy(i, h):
        return pltpu.make_async_remote_copy(
            src_ref=half_out.at[i, :, half_cols(h)],
            dst_ref=half_in.at[i, :, half_cols(h)],
            send_sem=half_s.at[i, h],
            recv_sem=half_r.at[i, h],
            device_id=mate,
            device_id_type=MESH,
        )

    def rest_copy(i):
        return pltpu.make_async_remote_copy(
            src_ref=pair_rest.at[i],
            dst_ref=far_rest.at[i],
            send_sem=rest_s.at[i],
            recv_sem=rest_r.at[i],
            device_id=across,
            device_id_type=MESH,
        )

    def unpack_rest(values):
        for k in range(CELLS // CHUNK):
            ext_sc[k, 0:REST, :] = values[REST * k : REST * (k + 1), :]

    def with_rest(main, k):
        return jnp.concatenate([main, ext_sc[k], jnp.zeros((8, CHUNK), F32)], axis=0)

    def quarter_of(i):
        j = slot_view(i, c) // 2
        row_half = jnp.where(crops_ref[1, 0, j] >= crops_ref[0, 0, j], 0, 1)
        col_half = jnp.where(crops_ref[1, 1, j] >= crops_ref[0, 1, j], 0, 1)
        return j, row_half, jnp.where(flips_ref[1, j] > 0, 1 - col_half, col_half)

    def arriving(m):
        return lax.rem(2 * m + quarter, 2 * quarter)

    def find_quarter(m, carry):
        j, row_half, col_half = quarter_of(arriving(m))
        cell = iota((1, CHUNK), 1)
        row, col = (cell >> 4) + 16 * row_half, (cell & 15) + 16 * col_half
        col = jnp.where(flips_ref[1, j] > 0, W - 1 - col, col)
        row = row + crops_ref[1, 0, j] - crops_ref[0, 0, j]
        col = col + crops_ref[1, 1, j] - crops_ref[0, 1, j]
        col = jnp.where(flips_ref[0, j] > 0, W - 1 - col, col)
        find_sc[m] = (iota((CELLS, CHUNK), 0) == row * W + col).astype(BF16)
        return carry

    def pack_second(m):
        _, row_half, col_half = quarter_of(2 * m)
        low, high = pair_sc[2 * m + 1, :, 0:half], pair_sc[2 * m + 1, :, half:CELLS]
        columns = dot_nt(jnp.where(row_half == 0, low, high), join_sc[...])
        kept = jnp.where(col_half == 0, columns[:, CHUNK:half], columns[:, 0:CHUNK])
        packed_sc[m, :, 0:half] = jnp.where(row_half == 0, high, low)
        packed_sc[m, :, half : half + CHUNK] = kept.astype(BF16)

    def unpack_second(m):
        far_copy(m, 1, 0).wait_recv()
        far_copy(m, 1, 1).wait_recv()
        _, row_half, col_half = quarter_of(arriving(m))
        whole = far_sc[2 * m + 1, :, 0:half]
        kept = far_sc[2 * m + 1, :, half : half + CHUNK]
        found = dot(far_sc[2 * m], find_sc[m]).astype(BF16)
        left, right = jnp.where(col_half == 0, found, kept), jnp.where(col_half == 0, kept, found)
        joined = dot(jnp.concatenate([left, right], axis=1), join_sc[...]).astype(BF16)
        far_sc[2 * m + 1, :, 0:half] = jnp.where(row_half == 0, joined, whole)
        far_sc[2 * m + 1, :, half:CELLS] = jnp.where(row_half == 0, whole, joined)

    def far_start(m, v):
        rest_copy(2 * m + v).start()
        far_copy(m, v, 0).start()
        far_copy(m, v, 1).start()

    def far_copy(m, v, h):
        i = 2 * m + v
        if v == 0:
            cols = half_cols(h)
            src = pair_sc.at[i, :, cols]
        else:
            cols = pl.ds(half * h, half if h == 0 else CHUNK)
            src = packed_sc.at[m, :, cols]
        return pltpu.make_async_remote_copy(
            src_ref=src,
            dst_ref=far_sc.at[i, :, cols],
            send_sem=far_s.at[i, h],
            recv_sem=far_r.at[i, h],
            device_id=across,
            device_id_type=MESH,
        )

    def to_mate(i):
        theirs = slot_view(i, 1 - c)
        load(theirs).wait()
        activate(theirs)
        for k, cols in enumerate(chunks()):
            half_out[i, :, cols] = partial(theirs, cols).astype(BF16)
            if k % 2 == 1:
                half_copy(i, k // 2).start()

    def forward(m, carry):
        for v in range(2):
            i = 2 * m + v

            @pl.when(i < 2 * quarter - 1)
            def _():
                to_mate(i + 1)

            mine = slot_view(i, c)
            load(mine).wait()
            activate(mine)
            for k, cols in enumerate(chunks()):
                if k % 2 == 0:
                    half_copy(i, k // 2).wait_recv()
                both = partial(mine, cols) + half_in[i, :, cols].astype(F32)
                pair_sc[i, :, cols] = both[0:MAIN, :].astype(BF16)
                pack_sc[REST * k : REST * (k + 1), :] = both[MAIN : MAIN + REST, :]

                @pl.when(i >= quarter)
                def _():
                    mid_sc[i - quarter, :, cols] = both

                if v == 0 and k % 2 == 1:

                    @pl.when(i < quarter)
                    def _(h=k // 2):
                        far_copy(m, 0, h).start()

            pair_rest[i] = pack_sc[...].astype(BF16)
            if v == 1:
                pack_second(m)

            @pl.when(i < quarter)
            def _():
                rest_copy(i).start()
                if v == 1:
                    far_copy(m, 1, 0).start()
                    far_copy(m, 1, 1).start()

        return carry

    to_mate(0)
    lax.fori_loop(0, quarter, forward, 0)
    lax.fori_loop(0, quarter, find_quarter, 0)

    chan_send(7, dfar_of, dn_sc.at[1])

    chan_wait(1, wsp_own, wsp_sc)
    stacked = wsp_sc[...].reshape(4 * NEW_PAD, TAPS * NEW_PAD)
    lane, row = iota((MID_PAD, 4 * NEW_PAD), 1), iota((MID_PAD, 4 * NEW_PAD), 0)
    hit = None
    for b in range(4):
        inner = lane - NEW_PAD * b
        one = (inner >= 0) & (inner < n_own) & (row == inner + n_own * b)
        hit = one if hit is None else hit | one
    wb_sc[...] = dot(hit.astype(BF16), stacked).astype(BF16)
    taps_eye = iota((TAPS * NEW_PAD, TAPS * NEW_PAD), 0) == iota((TAPS * NEW_PAD, TAPS * NEW_PAD), 1)
    wf_sc[...] = dot_nt(taps_eye.astype(BF16), wb_sc[...]).astype(BF16)

    cell = iota((1, CELLS), 1)
    col_at, row_at = cell & (W - 1), cell >> 5

    def inside(values, row_step, col_step):
        ok = None
        if col_step != 0:
            ok = (col_at + col_step >= 0) & (col_at + col_step < W)
        if row_step != 0:
            on = (row_at + row_step >= 0) & (row_at + row_step < H)
            ok = on if ok is None else ok & on
        return values if ok is None else jnp.where(ok, values, 0.0)

    def at_offset(values, row_step, col_step):
        move = (-(W * row_step + col_step)) % CELLS
        rolled = values if move == 0 else pltpu.roll(values, move, 1)
        return inside(rolled, row_step, col_step)

    chan_wait(2, dnew_of, dn_sc.at[0])

    def back_slot(i, carry):
        far = jnp.where(i < quarter, 1, 0)
        keep = jnp.where(i < quarter, quarter, i - quarter)
        for b in range(4):
            for l in range(2):
                pack_dn[...] = dn_sc[far, b, :, 128 * l : 128 * (l + 1)].astype(F32)
                at = CHUNK * b + 128 * l
                dnf_sc[0:n_new, at : at + 128] = pack_dn[pl.ds(n_new * lax.rem(i, quarter), n_new), :]
        grad = dnf_sc[...]
        for b in range(3):
            moved = at_offset(grad, 0, 1 - b)
            for a in range(3):
                t = 3 * a + b
                tap = at_offset(moved, 1 - a, 0)
                dcol_sc[keep, NEW_PAD * t : NEW_PAD * (t + 1), :] = tap.astype(BF16)
        for cols in chunks():
            d_sc[i, :, cols] = dot(wb_sc[...], dcol_sc[keep, :, cols])
        return carry

    lax.fori_loop(quarter, 2 * quarter, back_slot, 0)

    group = dpn_sc.shape[1]
    full = n_in // group

    def dp_load(k, rows):
        return pltpu.make_async_copy(
            dpass_hbm.at[pl.ds(k * group, rows)],
            dpn_sc.at[lax.rem(k, 2), pl.ds(0, rows)],
            dp_sem.at[lax.rem(k, 2)],
        )

    def dp_split(k, rows):
        first = k * group if isinstance(k, int) else pl.multiple_of(k * group, group)
        for l in range(CELLS // 128):
            at = slice(128 * l, 128 * (l + 1))
            native = dpn_sc[lax.rem(k, 2), 0:rows, :, at].astype(F32)
            for ch in range(rows):
                flat_sc[l, (n_views + 1) * ch : (n_views + 1) * ch + n_views, :] = native[ch]
            for n in range(n_views):
                by_view = flat_sc[l, pl.ds(n, rows, stride=n_views + 1), :]
                dp_sc[n, pl.ds(first, rows), at] = by_view.astype(BF16)

    left = n_in - full * group

    def dp_step(k, carry):
        @pl.when(k < full - 1)
        def _():
            dp_load(k + 1, group).start()

        dp_load(k, group).wait()
        dp_split(k, group)
        return carry

    def dp_some(first, last):
        lax.fori_loop(first, last, dp_step, 0)

    early = full - 2
    dp_load(0, group).start()
    dp_some(0, early)

    chan_wait(0, same(own_par), par_sc)

    def gathered(at):
        total = None
        for b in range(4):
            piece = jnp.where(iota((8, 256), 1) < n_own, par_sc[b], 0.0)
            piece = piece if b == 0 else pltpu.roll(piece, n_own * b, 1)
            total = piece if total is None else total + piece
        return two_rows(total[at : at + 1, :])

    row_to_cols(colm_sc.at[2], gathered(2))
    row_to_cols(colm_sc.at[3], gathered(3))

    def middle_view(q, first):
        rest_copy(q).wait_recv()

        def arrive_first():
            far_copy(q // 2, 0, 0).wait_recv()
            far_copy(q // 2, 0, 1).wait_recv()

        if first:
            arrive_first()
        else:
            pl.when(lax.rem(q, 2) == 0)(arrive_first)

            @pl.when(lax.rem(q, 2) == 1)
            def _():
                unpack_second(q // 2)

        unpack_rest(far_rest[q].astype(F32))
        for k, cols in enumerate(chunks()):
            mid_sc[q, :, cols] = mid_sc[q, :, cols] + with_rest(far_sc[q, :, cols].astype(F32), k)

    def middle_sums(q, carry):
        @pl.when(q > 0)
        def _():
            middle_view(q, False)

        first, second = None, None
        for cols in chunks():
            part = mid_sc[q, :, cols] - wide(colm_sc, 8)
            one, two = lane_fold(part), lane_fold(part * part)
            first = one if first is None else first + one
            second = two if second is None else second + two
        accm_sc[0] += first
        accm_sc[1] += second
        return carry

    middle_view(0, True)
    pivot = sum(lane_fold(mid_sc[0, :, cols]) for cols in chunks())
    colm_sc[8] = jnp.broadcast_to(jnp.sum(pivot, axis=1, keepdims=True) / CELLS, colm_sc.shape[1:])
    pivot_row = cols_to_row(padm_sc, pivot) / CELLS
    lax.fori_loop(0, quarter, middle_sums, 0)
    off_row = cols_to_row(padm_sc, accm_sc[0]) / owned_count
    cmsg_sc[0] = jnp.zeros_like(cmsg_sc[0])
    cmsg_sc[0, 0:2, :] = pivot_row + off_row
    cmsg_sc[0, 2:4, :] = cols_to_row(padm_sc, accm_sc[1]) - off_row * off_row * owned_count
    accm_sc[...] = jnp.zeros_like(accm_sc)
    cstat_sc[0, ci] = cmsg_sc[0]
    chan_send(3, same(cmsg_sc.at[0]), cstat_sc.at[0])
    far_start(quarter // 2, 0)
    far_start(quarter // 2, 1)
    dp_some(early, full)
    if left > 0:
        dp_load(full, left).start()
        dp_load(full, left).wait()
        dp_split(full, left)
    chan_wait(3, same(cmsg_sc.at[0]), cstat_sc.at[0])
    group_mean, group_dev = combine(cstat_sc[0], owned_count)
    msg_sc[0] = jnp.zeros_like(msg_sc[0])
    msg_sc[0, 0:2, :] = group_mean
    msg_sc[0, 2:4, :] = group_dev
    stat_sc[1, bi] = msg_sc[0]
    batch_send(1, same(msg_sc.at[0]), stat_sc.at[1])
    chan_wait(7, dfar_of, dn_sc.at[1])
    lax.fori_loop(0, quarter, back_slot, 0)
    batch_wait(1, same(msg_sc.at[0]), stat_sc.at[1])
    meanm_row, devm_row = combine(stat_sc[1], local_count)
    rstdm_row = lax.rsqrt(devm_row / pixels + EPS)
    row_to_cols(colm_sc.at[0], meanm_row)
    row_to_cols(colm_sc.at[1], rstdm_row)

    def mid_point(values):
        mean, rstd = wide(colm_sc, 0), wide(colm_sc, 1)
        norm = (values - mean) * rstd
        pre = norm * wide(colm_sc, 2) + wide(colm_sc, 3)
        s = sigmoid(pre)
        act = pre * s
        return norm, act, s + act * (1.0 - s)

    def mid_own(q, carry):
        first, second = None, None
        for cols in chunks():
            norm, act, slope = mid_point(mid_sc[q, :, cols])
            actm_sc[q, :, cols] = act.astype(BF16)
            grad = d_sc[quarter + q, :, cols] * slope
            d_sc[quarter + q, :, cols] = grad
            mid_sc[q, :, cols] = norm
            one, two = lane_fold(grad), lane_fold(grad * norm)
            first = one if first is None else first + one
            second = two if second is None else second + two
        accm_sc[0] += first
        accm_sc[1] += second
        return carry

    lax.fori_loop(0, quarter, mid_own, 0)
    cmsg_sc[1] = jnp.zeros_like(cmsg_sc[1])
    cmsg_sc[1, 0:2, :] = cols_to_row(padm_sc, accm_sc[0])
    cmsg_sc[1, 2:4, :] = cols_to_row(padm_sc, accm_sc[1])
    cstat_sc[1, ci] = cmsg_sc[1]
    chan_send(4, same(cmsg_sc.at[1]), cstat_sc.at[1])
    for q in range(2, quarter):
        far_start((quarter + q) // 2, q % 2)

    def tiles_of(ref):
        rows, cols = ref.shape
        return [(r, l, min(128, cols - 128 * l)) for r in range(rows // 16) for l in range(-(-cols // 128))]

    def scatter(refs, kind, values):
        out, back, _ = refs
        per = out.shape[1]
        for at, (r, l, width) in enumerate(tiles_of(values)):
            tile = values[16 * r : 16 * r + 16, 128 * l : 128 * l + width]
            out[at // per, at % per, :, 0:width] = tile.astype(BF16)
        back[bi] = out[bi]
        batch_send(kind, lambda other: out.at[other], back)

    def reduce_gather(refs, kind):
        out, back, whole = refs
        batch_wait(kind, lambda other: out.at[other], back)
        total = back[0].astype(F32)
        for at in range(1, nb):
            total = total + back[at].astype(F32)
        out[bi] = total.astype(BF16)
        whole[bi] = total.astype(BF16)
        batch_send(kind + 1, same(out.at[bi]), whole)

    def gather(refs, kind, ref):
        out, _, whole = refs
        per = out.shape[1]
        batch_wait(kind + 1, same(out.at[bi]), whole)
        for at, (r, l, width) in enumerate(tiles_of(ref)):
            tile = whole[at // per, at % per, :, 0:width]
            ref[16 * r : 16 * r + 16, 128 * l : 128 * l + width] = tile.astype(F32)

    spread_refs, reduce_refs = (ws_out, ws_in, ws_all), (wr_out, wr_back, wr_all)

    def spread_grad(q, carry):
        wsg_sc[...] += dot_nt(actm_sc[q], dcol_sc[q])
        return carry

    lax.fori_loop(0, quarter, spread_grad, 0)
    scatter(spread_refs, 4, wsg_sc)
    chan_wait(4, same(cmsg_sc.at[1]), cstat_sc.at[1])
    msg_sc[1] = (cstat_sc[1, 0] + cstat_sc[1, 1]) + (cstat_sc[1, 2] + cstat_sc[1, 3])
    stat_sc[2, bi] = msg_sc[1]
    batch_send(2, same(msg_sc.at[1]), stat_sc.at[2])
    ready = quarter // 2

    def far_point(q, carry):
        m = quarter // 2 + q // 2
        rest_copy(quarter + q).wait_recv()
        unpack_rest(pair_rest[q].astype(F32) + far_rest[quarter + q].astype(F32))

        @pl.when(lax.rem(q, 2) == 0)
        def _():
            far_copy(m, 0, 0).wait_recv()
            far_copy(m, 0, 1).wait_recv()

        @pl.when(lax.rem(q, 2) == 1)
        def _():
            unpack_second(m)

        for k, cols in enumerate(chunks()):
            part = pair_sc[q, :, cols].astype(F32) + far_sc[quarter + q, :, cols].astype(F32)
            norm, act, slope = mid_point(with_rest(part, k))
            d_sc[q, :, cols] = d_sc[q, :, cols] * slope
            half_in[q, :, cols] = norm.astype(BF16)
        return carry

    lax.fori_loop(0, ready, far_point, 0)
    reduce_gather(spread_refs, 4)
    batch_wait(2, same(msg_sc.at[1]), stat_sc.at[2])
    mid_sums = stat_sc[2, 0]
    for at in range(1, nb):
        mid_sums = mid_sums + stat_sc[2, at]
    row_to_cols(colm_sc.at[4], mid_sums[0:2, :] / pixels)
    row_to_cols(colm_sc.at[5], mid_sums[2:4, :] / pixels)
    row_to_cols(colm_sc.at[6], gathered(2) * rstdm_row)

    def dm_copy(i, h):
        return pltpu.make_async_remote_copy(
            src_ref=dm_out.at[i, :, half_cols(h)],
            dst_ref=dm_in.at[i, :, half_cols(h)],
            send_sem=dm_s.at[i, h],
            recv_sem=dm_r.at[i, h],
            device_id=mate,
            device_id_type=MESH,
        )

    def store(n):
        return pltpu.make_async_copy(slope_sc.at[n], dv_hbm.at[n], store_sem.at[n])

    def back_view(n, dm_ref):
        mean, scale = wide(col_sc, 0), wide(col_sc, 2)
        first, second = None, None
        for cols in chunks():
            grad = dot(wr_sc[...], dm_ref[:, cols]) * slope_sc[n, 0:n_in, cols].astype(F32)
            slope_sc[n, 0:n_in, cols] = (grad * scale + dp_sc[n, :, cols].astype(F32)).astype(BF16)
            off = x_sc[n, 0:n_in, cols].astype(F32) - mean
            one, two = lane_fold(grad), lane_fold(grad * off)
            first = one if first is None else first + one
            second = two if second is None else second + two
        acc_sc[0] += first
        acc_sc[1] += second
        wg_sc[:, 0:n_in] += dot_nt(dm_ref[...], act_sc[n])

    def dm_own(q, carry):
        i = quarter + q
        for cols in chunks():
            grad = d_sc[i, :, cols] - wide(colm_sc, 4) - mid_sc[q, :, cols] * wide(colm_sc, 5)
            dm_out[i, :, cols] = (grad * wide(colm_sc, 6)).astype(BF16)
        dm_copy(i, 0).start()
        dm_copy(i, 1).start()
        return carry

    lax.fori_loop(0, quarter, dm_own, 0)

    def back_mate(i):
        dm_copy(i, 0).wait_recv()
        dm_copy(i, 1).wait_recv()
        back_view(slot_view(i, 1 - c), dm_in.at[i])

    def back_own(q, carry):
        back_view(slot_view(quarter + q, c), dm_out.at[quarter + q])

        @pl.when(q > 0)
        def _():
            back_mate(quarter + q - 1)

        return carry

    lax.fori_loop(0, quarter, back_own, 0)
    back_mate(2 * quarter - 1)

    def back_far(q, carry):
        @pl.when(q >= ready)
        def _():
            far_point(q, carry)

        for k, cols in enumerate(chunks()):
            grad = d_sc[q, :, cols] - wide(colm_sc, 4) - half_in[q, :, cols].astype(F32) * wide(colm_sc, 5)
            dm_out[q, :, cols] = (grad * wide(colm_sc, 6)).astype(BF16)
            if k % 2 == 1:
                dm_copy(q, k // 2).start()
        back_view(slot_view(q, c), dm_out.at[q])

        @pl.when(q > 0)
        def _():
            back_mate(q - 1)

        return carry

    lax.fori_loop(0, quarter // 2, back_far, 0)
    gather(spread_refs, 4, wsg_sc)
    for b in range(4):
        wsp_sc[b, 0:40, :] = wsg_sc[n_own * b : n_own * b + 40, :].astype(BF16)
    wsgi_sc[ci] = wsp_sc[ci]
    wsg_of = lambda other: wsp_sc.at[other]
    chan_send(6, wsg_of, wsgi_sc)
    lax.fori_loop(quarter // 2, quarter, back_far, 0)
    back_mate(quarter - 1)

    scatter(reduce_refs, 6, wg_sc)
    msg_sc[2] = jnp.zeros_like(msg_sc[2])
    msg_sc[2, 0:2, :] = cols_to_row(padc_sc, acc_sc[0])
    msg_sc[2, 2:4, :] = cols_to_row(padc_sc, acc_sc[1]) * rstd_row
    stat_sc[3, bi] = msg_sc[2]
    batch_send(3, same(msg_sc.at[2]), stat_sc.at[3])

    def spread(q, carry):
        for k, cols in enumerate(chunks()):
            taps = dot(wf_sc[...], actm_sc[q, :, cols])
            for l in range(2):
                flat_sc[2 * k + l, 0 : TAPS * NEW_PAD, :] = taps[:, 128 * l : 128 * (l + 1)]
        total = None
        for b in range(3):
            column = None
            for a in range(3):
                t = 3 * a + b
                tap = [flat_sc[l, NEW_PAD * t : NEW_PAD * t + 40, :] for l in range(CELLS // 128)]
                tap = at_offset(jnp.concatenate(tap, axis=1), a - 1, 0)
                column = tap if column is None else column + tap
            column = at_offset(column, 0, b - 1)
            total = column if total is None else total + column
        for b in range(4):
            newo_sc[b, q] = total[0:n_new, CHUNK * b : CHUNK * (b + 1)].astype(BF16)
        return carry

    lax.fori_loop(0, quarter, spread, 0)
    new_of = lambda other: newo_sc.at[other]
    newi_sc[ci] = newo_sc[ci]
    chan_send(5, new_of, newi_sc)
    reduce_gather(reduce_refs, 6)
    batch_wait(3, same(msg_sc.at[2]), stat_sc.at[3])
    total = stat_sc[3, 0]
    for at in range(1, nb):
        total = total + stat_sc[3, at]
    gain_scale = gain_row * rstd_row
    row_to_cols(col_sc.at[4], -gain_scale * rstd_row * (total[2:4, :] / pixels))
    row_to_cols(col_sc.at[5], -gain_scale * (total[0:2, :] / pixels))

    def finish(n, carry):
        mean, slant, level = wide(col_sc, 0), wide(col_sc, 4), wide(col_sc, 5)
        for cols in chunks():
            rest = (x_sc[n, 0:n_in, cols].astype(F32) - mean) * slant + level
            slope_sc[n, 0:n_in, cols] = (slope_sc[n, 0:n_in, cols].astype(F32) + rest).astype(BF16)
        store(n).start()
        return carry

    lax.fori_loop(0, n_views, finish, 0)

    sums_ref[...] = jnp.zeros_like(sums_ref)
    sums_ref[0:1, :] = one_row(total[2:4, :])
    sums_ref[1:2, :] = one_row(total[0:2, :])
    all_sums = jnp.concatenate([one_row(mid_sums[2:4, :]), one_row(mid_sums[0:2, :]), jnp.zeros((6, 256), F32)], axis=0)
    own_sums = all_sums
    for b in range(1, 4):
        own_sums = jnp.where(ci == b, pltpu.roll(all_sums, 256 - n_own * b, 1), own_sums)
    sums_ref[2:4, :] = own_sums[0:2, :]

    chan_wait(5, new_of, newi_sc)
    for b in range(4):
        for q in range(quarter):
            new_ref[quarter * b + q] = newi_sc[b, q]
    chan_wait(6, wsg_of, wsgi_sc)
    wsg_total = (wsgi_sc[0].astype(F32) + wsgi_sc[1].astype(F32)) + (
        wsgi_sc[2].astype(F32) + wsgi_sc[3].astype(F32)
    )
    wsg_ref[...] = wsg_total[0:n_own, :]
    gather(reduce_refs, 6, wg_sc)
    wrg_ref[...] = wg_sc[0 : wrg_ref.shape[0], 0:n_in]

    def stored(n, carry):
        store(n).wait()
        return carry

    lax.fori_loop(0, n_views, stored, 0)

    def sent(i, carry):
        rest_copy(i).wait_send()
        for h in range(2):
            half_copy(i, h).wait_send()
            dm_copy(i, h).wait_send()
        return carry

    lax.fori_loop(0, 2 * quarter, sent, 0)

    def sent_far(m, carry):
        for v in range(2):
            for h in range(2):
                far_copy(m, v, h).wait_send()
        return carry

    lax.fori_loop(0, quarter, sent_far, 0)


def layer(nb, crops, flips, views, stats, vectors, wr_t, w_spread, d_new, d_passed):
    n_views, n_rows, _ = views.shape
    n_mid, n_in = wr_t.shape
    n_own = n_mid // 4
    quarter = n_views // 4
    n_new = d_new.shape[0]
    n_cols = TAPS * NEW_PAD
    together = -(-quarter * n_new // 16) * 16
    in_pad = -(-n_in // 16) * 16
    ws_tiles = -(-(MID_PAD // 16 * -(-n_cols // 128)) // nb)
    wr_tiles = -(-(MID_PAD // 16 * -(-in_pad // 128)) // nb)
    group = 16
    vmem = pl.BlockSpec(memory_space=pltpu.VMEM)
    anywhere = pl.BlockSpec(memory_space=pl.ANY)
    smem = pl.BlockSpec(memory_space=pltpu.SMEM)
    dma = pltpu.SemaphoreType.DMA
    slots = 2 * quarter
    return pl.pallas_call(
        functools.partial(layer_kernel, nb),
        in_specs=[smem, smem, anywhere] + [vmem] * 8 + [anywhere],
        out_specs=[anywhere, vmem, vmem, vmem, vmem],
        out_shape=[
            jax.ShapeDtypeStruct((n_views, n_rows, CELLS), BF16),
            jax.ShapeDtypeStruct((n_views, n_new, CHUNK), BF16),
            jax.ShapeDtypeStruct((n_mid, n_in), F32),
            jax.ShapeDtypeStruct((n_own, n_cols), F32),
            jax.ShapeDtypeStruct((8, 256), F32),
        ],
        scratch_shapes=[
            pltpu.VMEM((n_views, n_rows, CELLS), BF16),
            pltpu.VMEM((n_views, n_in, CELLS), BF16),
            pltpu.VMEM((n_views, n_rows, CELLS), BF16),
            pltpu.VMEM((n_views, n_in, CELLS), BF16),
            pltpu.VMEM((slots, MID_PAD, CELLS), BF16),
            pltpu.VMEM((slots, MID_PAD, CELLS), BF16),
            pltpu.VMEM((slots, MAIN, CELLS), BF16),
            pltpu.VMEM((slots, MAIN, CELLS), BF16),
            pltpu.VMEM((slots, 16, CHUNK), BF16),
            pltpu.VMEM((slots, 16, CHUNK), BF16),
            pltpu.VMEM((16, CHUNK), F32),
            pltpu.VMEM((CELLS // CHUNK, 8, CHUNK), F32),
            pltpu.VMEM((quarter, MAIN, CELLS // 2 + CHUNK), BF16),
            pltpu.VMEM((quarter, CELLS, CHUNK), BF16),
            pltpu.VMEM((CELLS // 2, CELLS // 2), BF16),
            pltpu.VMEM((slots, MID_PAD, CELLS), F32),
            pltpu.VMEM((quarter + 1, n_cols, CELLS), BF16),
            pltpu.VMEM((quarter, MID_PAD, CELLS), F32),
            pltpu.VMEM((quarter, MID_PAD, CELLS), BF16),
            pltpu.VMEM((slots, MID_PAD, CELLS), BF16),
            pltpu.VMEM((slots, MID_PAD, CELLS), BF16),
            pltpu.VMEM((2, 2, together, CHUNK), BF16),
            pltpu.VMEM((2, 4, together, CHUNK), BF16),
            pltpu.VMEM((together, 128), F32),
            pltpu.VMEM((NEW_PAD, CELLS), F32),
            pltpu.VMEM((2, group, n_views, CELLS), BF16),
            pltpu.VMEM((CELLS // 128, max(max(group, n_new) * (n_views + 1), n_cols), 128), F32),
            pltpu.VMEM((8, 256), F32),
            pltpu.VMEM((4, 8, 256), F32),
            pltpu.VMEM((4, NEW_PAD, n_cols), BF16),
            pltpu.VMEM((n_in, MID_PAD), BF16),
            pltpu.VMEM((MID_PAD, n_in), BF16),
            pltpu.VMEM((MID_PAD, n_cols), BF16),
            pltpu.VMEM((n_cols, MID_PAD), BF16),
            pltpu.VMEM((4, nb, 8, 128), F32),
            pltpu.VMEM((2, 4, 8, 128), F32),
            pltpu.VMEM((3, 8, 128), F32),
            pltpu.VMEM((2, 8, 128), F32),
            pltpu.VMEM((6, n_in, 128), F32),
            pltpu.VMEM((9, MID_PAD, 128), F32),
            pltpu.VMEM((256, 128), F32),
            pltpu.VMEM((256, 128), F32),
            pltpu.VMEM((2, n_in, 128), F32),
            pltpu.VMEM((2, MID_PAD, 128), F32),
            pltpu.VMEM((MID_PAD, in_pad), F32),
            pltpu.VMEM((MID_PAD, n_cols), F32),
            pltpu.VMEM((4, NEW_PAD, n_cols), BF16),
            pltpu.VMEM((nb, ws_tiles, 16, 128), BF16),
            pltpu.VMEM((nb, ws_tiles, 16, 128), BF16),
            pltpu.VMEM((nb, ws_tiles, 16, 128), BF16),
            pltpu.VMEM((nb, wr_tiles, 16, 128), BF16),
            pltpu.VMEM((nb, wr_tiles, 16, 128), BF16),
            pltpu.VMEM((nb, wr_tiles, 16, 128), BF16),
            pltpu.VMEM((4, quarter, n_new, CHUNK), BF16),
            pltpu.VMEM((4, quarter, n_new, CHUNK), BF16),
            dma((n_views,)),
            dma((n_views,)),
            dma((slots, 2)),
            dma((slots, 2)),
            dma((slots, 2)),
            dma((slots, 2)),
            dma((slots,)),
            dma((slots,)),
            dma((slots, 2)),
            dma((slots, 2)),
            dma((8, nb)),
            dma((8, nb)),
            dma((8, 4)),
            dma((8, 4)),
            dma((2,)),
        ],
        compiler_params=pltpu.CompilerParams(
            collective_id=0, has_side_effects=True, vmem_limit_bytes=VMEM_LIMIT
        ),
        name="layer",
    )(crops, flips, views, stats, *vectors, wr_t, w_spread, d_new, d_passed)


def solution(mesh):
    nb = mesh.shape["batch"]

    def on_device(features, crops, flips, gain_in, shift_in, w_reduce, gain_mid, shift_mid, w_spread, d_passed, d_new):
        n_own, n_new = w_spread.shape[0], w_spread.shape[3]

        w9 = jnp.transpose(w_spread, (1, 2, 0, 3)).reshape(TAPS, n_own, n_new)
        crops_t, flips_t = jnp.transpose(crops, (1, 2, 0)), jnp.transpose(flips)
        swap = lambda v: jnp.transpose(v, (1, 0, 2))
        views, passed, stats = crop_views(swap(features), crops_t, flips_t)
        dv, new_maps, wr_grad, ws_grad, sums = layer(
            nb, crops_t, flips_t, views, stats, (gain_in, shift_in, gain_mid, shift_mid), jnp.transpose(w_reduce), w9, swap(d_new), swap(d_passed)
        )
        features_grad, new_maps, wr_grad, ws_grad, *grads = place_views(
            crops_t, flips_t, dv, new_maps, wr_grad, ws_grad, sums
        )
        ws_grad = jnp.transpose(ws_grad.reshape(3, 3, n_own, n_new), (2, 0, 1, 3))
        return (swap(passed), swap(new_maps), swap(features_grad), jnp.transpose(wr_grad), ws_grad, *grads)

    return jax.shard_map(
        on_device,
        mesh=mesh,
        in_specs=(
            P("batch", "chan", None),
            P("batch", None, None),
            P("batch", None),
            P("chan"),
            P("chan"),
            P("chan", None),
            P("chan"),
            P("chan"),
            P("chan", None, None, None),
            P("batch", "chan", None),
            P("batch", None, "chan"),
        ),
        out_specs=(
            P("batch", "chan", None),
            P("batch", None, "chan"),
            P("batch", "chan", None),
            P("chan", None),
            P("chan", None, None, None),
            P("chan"),
            P("chan"),
            P("chan"),
            P("chan"),
        ),
        check_vma=False,
    )
```

```python
import functools

import jax
import jax.numpy as jnp
from jax import lax
from jax.experimental import pallas as pl
from jax.experimental.pallas import tpu as pltpu
from jax.sharding import PartitionSpec as P

H = 32
W = 32
MARGIN = 8
GRID = H + 2 * MARGIN
CELLS = H * W
EPS = 1e-05
CHUNK = 256
SPAN = 512
STRIDE = 8 * GRID
TAPS = 9
BLOCK = 80
MID_PAD = 144
NEW_PAD = 48
MAIN = 128
REST = 4
F32 = jnp.float32
BF16 = jnp.bfloat16
MESH = pl.DeviceIdType.MESH
VMEM_LIMIT = 63 * 2**20 + 800 * 2**10


def dot(a, b):
    return jnp.dot(a, b, preferred_element_type=F32)


def dot_nt(a, b):
    return lax.dot_general(a, b, (((1,), (1,)), ((), ())), preferred_element_type=F32)


def iota(shape, axis):
    return lax.broadcasted_iota(jnp.int32, shape, axis)


def lane_fold(values):
    total = values[:, 0:128]
    for at in range(128, values.shape[1], 128):
        total = total + values[:, at : at + 128]
    return total


def cols_to_row(pad_ref, values):
    if values is not None:
        pad_ref[0 : values.shape[0], :] = values
    halves = [
        jnp.sum(jnp.transpose(pad_ref[at : at + 128, :]), axis=0, keepdims=True)
        for at in (0, 128)
    ]
    return jnp.concatenate(halves, axis=0)


def two_rows(row):
    return jnp.concatenate([row[:, 0:128], row[:, 128:256]], axis=0)


def one_row(rows):
    return jnp.concatenate([rows[0:1, :], rows[1:2, :]], axis=1)


def row_to_cols(out_ref, row):
    rows = out_ref.shape[0]
    for h, at in enumerate((0, 128)):
        height = min(128, rows - at)
        square = jnp.broadcast_to(row[h : h + 1, :], (128, 128))
        out_ref[at : at + height, :] = jnp.transpose(square)[0:height, :]


def window_start(crops_ref, j, v):
    start = crops_ref[v, 0, j] * GRID + crops_ref[v, 1, j]
    base = jnp.minimum((start // 128) * 128, GRID * GRID - 3 * STRIDE - SPAN)
    return pl.multiple_of(base, 128), start - base


def chunk_target(offset, flip, cell):
    col = cell & (W - 1)
    row = cell >> 5
    return offset + row * GRID + jnp.where(flip > 0, W - 1 - col, col)


def blocks_of(channels):
    return [(at, min(BLOCK, channels - at)) for at in range(0, channels, BLOCK)]


def crop_kernel(crops_ref, flips_ref, x_hbm, views_hbm, passed_hbm, stats_ref, pick_sc, xn_sc, xf_sc, xi_sc, vw_sc, pf_sc, pn_sc, mean_sc, dev_sc, x_sem, vw_sem, pn_sem):
    channels, items, cells = x_hbm.shape
    n_views, rows, part_rows = 2 * items, BLOCK, 16
    blocks = blocks_of(channels)

    def load(at):
        first, size = blocks[at]
        return pltpu.make_async_copy(x_hbm.at[pl.ds(first, size)], xn_sc.at[at, pl.ds(0, size)], x_sem.at[at])

    def view_out(at, n):
        first = pl.multiple_of(at * rows, rows)
        return pltpu.make_async_copy(vw_sc.at[at, n], views_hbm.at[n, pl.ds(first, rows)], vw_sem.at[at, n])

    def passed_out(at, u):
        first, size = blocks[at]
        size = min(part_rows, size - part_rows * u)
        return pltpu.make_async_copy(
            pn_sc.at[at, pl.ds(part_rows * u, size)],
            passed_hbm.at[pl.ds(first + part_rows * u, size)],
            pn_sem.at[at, u],
        )

    for at in range(len(blocks)):
        load(at).start()

    def build(n, carry):
        j, v = n // 2, n % 2
        _, offset = window_start(crops_ref, j, v)
        target = chunk_target(offset, flips_ref[v, j], iota((1, CHUNK), 1))
        pick_sc[n] = (iota((SPAN, CHUNK), 0) == target).astype(BF16)
        return carry

    lax.fori_loop(0, n_views, build, 0)
    mean_sc[...] = jnp.zeros_like(mean_sc)
    dev_sc[...] = jnp.zeros_like(dev_sc)

    def block(b, carry):
        for at in range(len(blocks)):

            @pl.when(b == at)
            def _(at=at):
                load(at).wait()

        for l in range(cells // 128):
            at = slice(128 * l, 128 * (l + 1))
            wide_x = xn_sc[b, :, :, at].astype(F32)
            for ch in range(rows):
                xf_sc[l, (items + 1) * ch : (items + 1) * ch + items, :] = wide_x[ch]

        total = jnp.zeros((rows, 128), F32)
        squares = jnp.zeros((rows, 128), F32)
        pivot = None
        for j in range(items):
            for l in range(cells // 128):
                xi_sc[j, :, 128 * l : 128 * (l + 1)] = xf_sc[l, pl.ds(j, rows, stride=items + 1), :].astype(BF16)
            for v in range(2):
                n = 2 * j + v
                base, _ = window_start(crops_ref, j, v)
                spans = [xi_sc[j, :, pl.ds(pl.multiple_of(base + STRIDE * k, 128), SPAN)] for k in range(CELLS // CHUNK)]
                parts = dot(jnp.concatenate(spans, axis=0), pick_sc[n])
                for k in range(CELLS // CHUNK):
                    part = parts[rows * k : rows * (k + 1), :]
                    vw_sc[b, n, :, CHUNK * k : CHUNK * (k + 1)] = part.astype(BF16)
                    for l in range(2):
                        pf_sc[2 * k + l, pl.ds(n, rows, stride=n_views + 1), :] = part[:, 128 * l : 128 * (l + 1)]
                    if pivot is None:
                        pivot = jnp.sum(lane_fold(part), axis=1, keepdims=True) / CHUNK
                    off = part - pivot
                    total = total + lane_fold(off)
                    squares = squares + lane_fold(off * off)
                view_out(b, n).start()
        for u in range(rows // part_rows):
            for l in range(CELLS // 128):
                at = slice(128 * l, 128 * (l + 1))
                for ch in range(part_rows * u, part_rows * (u + 1)):
                    first = (n_views + 1) * ch
                    pn_sc[b, ch, :, at] = pf_sc[l, first : first + n_views, :].astype(BF16)
            for at in range(len(blocks)):

                @pl.when(b == at)
                def _(at=at):
                    passed_out(at, u).start()

        count = n_views * CELLS
        shift = jnp.sum(total, axis=1, keepdims=True) / count
        first = pl.multiple_of(b * rows, 8)
        lane = iota((rows, 128), 1)
        mean_sc[pl.ds(first, rows), :] = jnp.where(lane == 0, pivot + shift, 0.0)
        dev_sc[pl.ds(first, rows), :] = squares - jnp.where(lane == 0, shift * shift * count, 0.0)
        return carry

    lax.fori_loop(0, len(blocks), block, 0)
    stats_ref[...] = jnp.zeros_like(stats_ref)
    stats_ref[0:2, :] = cols_to_row(mean_sc, None)
    stats_ref[2:4, :] = cols_to_row(dev_sc, None)
    for at in range(len(blocks)):
        for n in range(n_views):
            view_out(at, n).wait()
        for u in range(rows // part_rows):
            passed_out(at, u).wait()


def crop_views(features, crops, flips):
    channels, items, cells = features.shape
    n_blocks = len(blocks_of(channels))
    anywhere = pl.BlockSpec(memory_space=pl.ANY)
    smem = pl.BlockSpec(memory_space=pltpu.SMEM)
    dma = pltpu.SemaphoreType.DMA
    return pl.pallas_call(
        crop_kernel,
        in_specs=[smem, smem, anywhere],
        out_specs=[anywhere, anywhere, pl.BlockSpec(memory_space=pltpu.VMEM)],
        out_shape=[
            jax.ShapeDtypeStruct((2 * items, n_blocks * BLOCK, CELLS), BF16),
            jax.ShapeDtypeStruct((channels, 2 * items, CELLS), BF16),
            jax.ShapeDtypeStruct((8, 128), F32),
        ],
        scratch_shapes=[
            pltpu.VMEM((2 * items, SPAN, CHUNK), BF16),
            pltpu.VMEM((n_blocks, BLOCK, items, cells), BF16),
            pltpu.VMEM((cells // 128, BLOCK * (items + 1), 128), F32),
            pltpu.VMEM((items, BLOCK, cells), BF16),
            pltpu.VMEM((n_blocks, 2 * items, BLOCK, CELLS), BF16),
            pltpu.VMEM((CELLS // 128, BLOCK * (2 * items + 1), 128), F32),
            pltpu.VMEM((n_blocks, BLOCK, 2 * items, CELLS), BF16),
            pltpu.VMEM((256, 128), F32),
            pltpu.VMEM((256, 128), F32),
            dma((n_blocks,)),
            dma((n_blocks, 2 * items)),
            dma((n_blocks, BLOCK // 16)),
        ],
        compiler_params=pltpu.CompilerParams(vmem_limit_bytes=VMEM_LIMIT),
        name="crop_views",
    )(crops, flips, features)


def place_kernel(crops_ref, flips_ref, dv_hbm, new_ref, wrg_ref, wsg_ref, sums_ref, out_hbm, newo_ref, wrgo_ref, wsgo_ref, gi_ref, si_ref, gm_ref, sm_ref, pick_sc, dv_sc, flat_sc, out_sc, new_sc, dv_sem, out_sem):
    channels, items, cells = out_hbm.shape
    n_views, rows, part_rows = 2 * items, BLOCK, 16
    blocks = blocks_of(channels)

    def load(at):
        first = at * rows if isinstance(at, int) else pl.multiple_of(at * rows, rows)
        return pltpu.make_async_copy(dv_hbm.at[:, pl.ds(first, rows)], dv_sc.at[at], dv_sem.at[at])

    def out(at, u):
        first, size = blocks[at]
        size = min(part_rows, size - part_rows * u)
        return pltpu.make_async_copy(
            out_sc.at[at, pl.ds(part_rows * u, size)],
            out_hbm.at[pl.ds(first + part_rows * u, size)],
            out_sem.at[at, u],
        )

    for at in range(len(blocks)):
        load(at).start()

    def build(n, carry):
        j, v = n // 2, n % 2
        _, offset = window_start(crops_ref, j, v)
        target = chunk_target(offset, flips_ref[v, j], iota((CHUNK, 1), 0))
        pick_sc[n] = (iota((CHUNK, SPAN), 1) == target).astype(BF16)
        return carry

    lax.fori_loop(0, n_views, build, 0)

    def block(b, carry):
        flat_sc[...] = jnp.zeros_like(flat_sc)
        load(b).wait()

        def place_item(j):
            for v in range(2):
                n = 2 * j + v
                base, _ = window_start(crops_ref, j, v)
                tile = base // 128
                parts = [dv_sc[b, n, :, CHUNK * k : CHUNK * (k + 1)] for k in range(CELLS // CHUNK)]
                spans = dot(jnp.concatenate(parts, axis=0), pick_sc[n])
                spans = [spans[rows * k : rows * (k + 1), :] for k in range(CELLS // CHUNK)]
                pieces = [spans[0][:, 0:STRIDE]]
                for k in range(1, CELLS // CHUNK):
                    pieces.append(spans[k - 1][:, STRIDE:SPAN] + spans[k][:, 0 : SPAN - STRIDE])
                    pieces.append(spans[k][:, SPAN - STRIDE : STRIDE])
                pieces.append(spans[-1][:, STRIDE:SPAN])
                window = jnp.concatenate(pieces, axis=1)
                of_item = pl.ds(j, rows, stride=items + 1)
                for t in range(window.shape[1] // 128):
                    piece = window[:, 128 * t : 128 * (t + 1)]
                    if v == 1:
                        piece = piece + flat_sc[tile + t, of_item, :]
                    flat_sc[tile + t, of_item, :] = piece

        def place_some(group, carry):
            for inner in range(4):
                place_item(4 * group + inner)
            return carry

        lax.fori_loop(0, items // 4, place_some, 0)
        for u in range(rows // part_rows):
            for l in range(cells // 128):
                for ch in range(part_rows * u, part_rows * (u + 1)):
                    first = (items + 1) * ch
                    out_sc[b, ch, :, 128 * l : 128 * (l + 1)] = flat_sc[l, first : first + items, :]
            for at in range(len(blocks)):

                @pl.when(b == at)
                def _(at=at):
                    out(at, u).start()

        return carry

    lax.fori_loop(0, len(blocks), block, 0)

    n_new = new_ref.shape[1]
    for n in range(n_views):
        for l in range(2):
            piece = new_ref[n, :, 128 * l : 128 * (l + 1)]
            new_sc[l, pl.ds(n, n_new, stride=n_views), :] = piece.astype(F32)
    for l in range(2):
        newo_ref[:, :, 128 * l : 128 * (l + 1)] = new_sc[l].reshape(n_new, n_views, 128).astype(BF16)
    wrgo_ref[...] = wrg_ref[...]
    for t in range(TAPS):
        wsgo_ref[t] = wsg_ref[:, NEW_PAD * t : NEW_PAD * t + wsgo_ref.shape[2]]
    for at, ref in enumerate((gi_ref, si_ref, gm_ref, sm_ref)):
        ref[...] = sums_ref[at, 0 : ref.shape[0]]
    for at in range(len(blocks)):
        for u in range(rows // part_rows):
            out(at, u).wait()


def place_views(crops, flips, dv, new_maps, wr_grad, ws_grad, sums):
    items, channels = crops.shape[2], wr_grad.shape[1]
    n_views, n_blocks = dv.shape[0], dv.shape[1] // BLOCK
    n_new, n_own = new_maps.shape[1], ws_grad.shape[0]
    cells = GRID * GRID
    anywhere = pl.BlockSpec(memory_space=pl.ANY)
    vmem = pl.BlockSpec(memory_space=pltpu.VMEM)
    smem = pl.BlockSpec(memory_space=pltpu.SMEM)
    dma = pltpu.SemaphoreType.DMA
    small = [
        ((n_new, n_views, CHUNK), BF16),
        (wr_grad.shape, F32),
        ((TAPS, n_own, n_new), F32),
        ((channels,), F32),
        ((channels,), F32),
        ((n_own,), F32),
        ((n_own,), F32),
    ]
    return pl.pallas_call(
        place_kernel,
        in_specs=[smem, smem, anywhere] + [vmem] * 4,
        out_specs=[anywhere] + [vmem] * len(small),
        out_shape=[jax.ShapeDtypeStruct((channels, items, cells), F32)]
        + [jax.ShapeDtypeStruct(shape, kind) for shape, kind in small],
        scratch_shapes=[
            pltpu.VMEM((n_views, CHUNK, SPAN), BF16),
            pltpu.VMEM((n_blocks, n_views, BLOCK, CELLS), BF16),
            pltpu.VMEM((cells // 128, BLOCK * (items + 1), 128), F32),
            pltpu.VMEM((n_blocks, BLOCK, items, cells), F32),
            pltpu.VMEM((2, n_new * n_views, 128), F32),
            dma((n_blocks,)),
            dma((n_blocks, BLOCK // 16)),
        ],
        compiler_params=pltpu.CompilerParams(vmem_limit_bytes=VMEM_LIMIT),
        name="place_views",
    )(crops, flips, dv, new_maps, wr_grad, ws_grad, sums)


def sigmoid(v):
    return 0.5 * jnp.tanh(0.5 * v) + 0.5


def combine(parts, count):
    groups = parts.shape[0]
    mean = parts[0, 0:2, :]
    dev = parts[0, 2:4, :]
    for at in range(1, groups):
        mean = mean + parts[at, 0:2, :]
        dev = dev + parts[at, 2:4, :]
    mean = mean / groups
    spread = None
    for at in range(groups):
        off = parts[at, 0:2, :] - mean
        spread = off * off if spread is None else spread + off * off
    return mean, dev + spread * count


def layer_kernel(
    nb,
    crops_ref,
    flips_ref,
    views_hbm,
    stats_ref,
    gain_in_ref,
    shift_in_ref,
    gain_mid_ref,
    shift_mid_ref,
    wr_in,
    wsp_in,
    dnew_ref,
    dpass_hbm,
    dv_hbm,
    new_ref,
    wrg_ref,
    wsg_ref,
    sums_ref,
    x_sc,
    act_sc,
    slope_sc,
    dp_sc,
    half_out,
    half_in,
    pair_sc,
    far_sc,
    pair_rest,
    far_rest,
    pack_sc,
    ext_sc,
    packed_sc,
    find_sc,
    join_sc,
    d_sc,
    dcol_sc,
    mid_sc,
    actm_sc,
    dm_out,
    dm_in,
    dno_sc,
    dn_sc,
    pack_dn,
    dnf_sc,
    dpn_sc,
    flat_sc,
    own_par,
    par_sc,
    wsp_sc,
    wr_sc,
    wrt_sc,
    wb_sc,
    wf_sc,
    stat_sc,
    cstat_sc,
    msg_sc,
    cmsg_sc,
    col_sc,
    colm_sc,
    padc_sc,
    padm_sc,
    acc_sc,
    accm_sc,
    wg_sc,
    wsg_sc,
    wsgi_sc,
    ws_out,
    ws_in,
    ws_all,
    wr_out,
    wr_back,
    wr_all,
    newo_sc,
    newi_sc,
    load_sem,
    store_sem,
    half_s,
    half_r,
    far_s,
    far_r,
    rest_s,
    rest_r,
    dm_s,
    dm_r,
    bat_s,
    bat_r,
    chan_s,
    chan_r,
    dp_sem,
):
    bi, ci = lax.axis_index("batch"), lax.axis_index("chan")
    y, c = ci // 2, lax.rem(ci, 2)
    n_views, n_in = x_sc.shape[0], act_sc.shape[1]
    quarter = n_views // 4
    n_own, n_new = wsg_ref.shape[0], dnew_ref.shape[0]
    local_count = float(n_views * CELLS)
    owned_count = float(quarter * CELLS)
    pixels = float(nb) * local_count
    mate = (bi, 2 * y + (1 - c))
    across = (bi, 2 * (1 - y) + c)

    def batch_peer(k):
        return (lax.rem(bi + k, nb), ci)

    def chan_peer(k):
        return (bi, lax.rem(ci + k, 4))

    barrier = pltpu.get_barrier_semaphore()

    def greet(k, carry):
        pl.semaphore_signal(barrier, inc=1, device_id=batch_peer(k), device_id_type=MESH)
        return carry

    lax.fori_loop(1, nb, greet, 0)
    for k in range(1, 4):
        pl.semaphore_signal(barrier, inc=1, device_id=chan_peer(k), device_id_type=MESH)

    def load(n):
        return pltpu.make_async_copy(views_hbm.at[n], x_sc.at[n], load_sem.at[n])

    def load_step(i, carry):
        load(slot_view(i, 1 - c)).start()
        load(slot_view(i, c)).start()
        return carry

    def slot_view(i, core):
        h = jnp.where(i < quarter, 1 - y, y)
        return quarter * (2 * h + core) + lax.rem(i, quarter)

    lax.fori_loop(0, 2 * quarter, load_step, 0)
    pl.semaphore_wait(barrier, nb + 2)

    def batch_copy(kind, k, src, dst):
        return pltpu.make_async_remote_copy(
            src_ref=src,
            dst_ref=dst,
            send_sem=bat_s.at[kind, k],
            recv_sem=bat_r.at[kind, k],
            device_id=batch_peer(k),
            device_id_type=MESH,
        )

    def batch_send(kind, src_of, dst):
        def step(k, carry):
            batch_copy(kind, k, src_of(lax.rem(bi + k, nb)), dst.at[bi]).start()
            return carry

        lax.fori_loop(1, nb, step, 0)

    def batch_wait(kind, src_of, dst):
        def step(k, carry):
            other = lax.rem(bi + nb - k, nb)
            batch_copy(kind, k, src_of(lax.rem(bi + k, nb)), dst.at[other]).wait()
            return carry

        lax.fori_loop(1, nb, step, 0)

    def chan_copy(kind, k, src, dst):
        return pltpu.make_async_remote_copy(
            src_ref=src,
            dst_ref=dst,
            send_sem=chan_s.at[kind, k],
            recv_sem=chan_r.at[kind, k],
            device_id=chan_peer(k),
            device_id_type=MESH,
        )

    def chan_send(kind, src_of, dst):
        for k in range(1, 4):
            chan_copy(kind, k, src_of(lax.rem(ci + k, 4)), dst.at[ci]).start()

    def chan_wait(kind, src_of, dst):
        for k in range(1, 4):
            other = lax.rem(ci + 4 - k, 4)
            chan_copy(kind, k, src_of(lax.rem(ci + k, 4)), dst.at[other]).wait()

    def wide(ref, at):
        col = ref[at]
        return jnp.concatenate([col, col], axis=1)

    def same(ref):
        return lambda other: ref

    stat_sc[0, bi] = stats_ref[...]
    batch_send(0, same(stats_ref), stat_sc.at[0])
    own_par[...] = jnp.zeros_like(own_par)
    for at, ref in enumerate((gain_in_ref, shift_in_ref, gain_mid_ref, shift_mid_ref)):
        own_par[at : at + 1, 0 : ref.shape[0]] = ref[...].astype(F32).reshape(1, ref.shape[0])
    par_sc[ci] = own_par[...]
    chan_send(0, same(own_par), par_sc)
    dnf_sc[...] = jnp.zeros_like(dnf_sc)
    for t in range(TAPS):
        dnf_sc[0:n_own, NEW_PAD * t : NEW_PAD * t + n_new] = wsp_in[t].astype(F32)
    wsp_sc[ci] = dnf_sc[:, 0 : TAPS * NEW_PAD].astype(BF16)
    wsp_own = same(wsp_sc.at[ci])

    pack_dn[...] = jnp.zeros_like(pack_dn)
    for l in range(2):
        at = slice(128 * l, 128 * (l + 1))
        native = dnew_ref[:, :, at].astype(F32)
        for ch in range(n_new):
            flat_sc[l, (n_views + 1) * ch : (n_views + 1) * ch + n_views, :] = native[ch]
        for block in range(4):
            for q in range(quarter):
                by_view = flat_sc[l, pl.ds(quarter * block + q, n_new, stride=n_views + 1), :]
                pack_dn[n_new * q : n_new * (q + 1), :] = by_view
            dno_sc[block % 2, block // 2, :, at] = pack_dn[...].astype(BF16)
    dn_sc[0, ci] = dno_sc[c, y]
    dn_sc[1, ci] = dno_sc[c, 1 - y]
    dnew_of = lambda other: dno_sc.at[lax.rem(other, 2), other // 2]
    dfar_of = lambda other: dno_sc.at[lax.rem(other, 2), 1 - other // 2]
    chan_send(2, dnew_of, dn_sc.at[0])
    chan_send(1, wsp_own, wsp_sc)

    padc_sc[...] = jnp.zeros_like(padc_sc)
    padm_sc[...] = jnp.zeros_like(padm_sc)
    acc_sc[...] = jnp.zeros_like(acc_sc)
    accm_sc[...] = jnp.zeros_like(accm_sc)
    wg_sc[...] = jnp.zeros_like(wg_sc)
    wsg_sc[...] = jnp.zeros_like(wsg_sc)
    ext_sc[...] = jnp.zeros_like(ext_sc)
    piece, place = iota((CELLS // 2, CELLS // 2), 0), iota((CELLS // 2, CELLS // 2), 1)
    joined_at = ((piece & 255) >> 4) * W + (piece >> 8) * 16 + (piece & 15)
    join_sc[...] = (joined_at == place).astype(BF16)
    ws_out[...] = jnp.zeros_like(ws_out)
    wr_out[...] = jnp.zeros_like(wr_out)
    wrt_sc[...] = jnp.zeros_like(wrt_sc)
    wrt_sc[0 : wr_in.shape[0], :] = wr_in[...]
    eye = (iota((n_in, n_in), 0) == iota((n_in, n_in), 1)).astype(BF16)
    wr_sc[...] = dot_nt(eye, wrt_sc[...]).astype(BF16)
    gain_row = two_rows(own_par[0:1, :])
    shift_row = two_rows(own_par[1:2, :])

    gain_col, shift_col = (jnp.transpose(jnp.broadcast_to(one_row(v), (256, 256)))[0:n_in, 0:128] for v in (gain_row, shift_row))
    guess = None
    for weight, offset in ((2 / 3, 0.0), (1 / 6, 3.0**0.5), (1 / 6, -(3.0**0.5))):
        pre = shift_col + offset * gain_col
        part = weight * pre * sigmoid(pre)
        guess = part if guess is None else guess + part
    colm_sc[7] = dot(wrt_sc[...], guess.astype(BF16))

    batch_wait(0, same(stats_ref), stat_sc.at[0])
    mean_row, dev_row = combine(stat_sc[0], local_count)
    rstd_row = lax.rsqrt(dev_row / pixels + EPS)
    row_to_cols(col_sc.at[0], mean_row)
    row_to_cols(col_sc.at[1], rstd_row)
    row_to_cols(col_sc.at[2], rstd_row * gain_row)
    row_to_cols(col_sc.at[3], shift_row)

    def chunks(start=0, count=CELLS // CHUNK):
        if isinstance(start, int):
            return [slice(start + CHUNK * k, start + CHUNK * (k + 1)) for k in range(count)]
        return [pl.ds(pl.multiple_of(start + CHUNK * k, CHUNK), CHUNK) for k in range(count)]

    half = CELLS // 2

    def half_cols(h):
        return pl.ds(h * half if isinstance(h, int) else pl.multiple_of(h * half, half), half)

    def activate(n):
        mean, scale, shift = wide(col_sc, 0), wide(col_sc, 2), wide(col_sc, 3)
        for cols in chunks():
            pre = (x_sc[n, 0:n_in, cols].astype(F32) - mean) * scale + shift
            s = sigmoid(pre)
            act = pre * s
            slope_sc[n, 0:n_in, cols] = (s + act * (1.0 - s)).astype(BF16)
            act_sc[n, :, cols] = act.astype(BF16)

    def partial(n, cols):
        return dot(wrt_sc[...], act_sc[n, :, cols]) - wide(colm_sc, 7)

    def half_copy(i, h):
        return pltpu.make_async_remote_copy(
            src_ref=half_out.at[i, :, half_cols(h)],
            dst_ref=half_in.at[i, :, half_cols(h)],
            send_sem=half_s.at[i, h],
            recv_sem=half_r.at[i, h],
            device_id=mate,
            device_id_type=MESH,
        )

    def rest_copy(i):
        return pltpu.make_async_remote_copy(
            src_ref=pair_rest.at[i],
            dst_ref=far_rest.at[i],
            send_sem=rest_s.at[i],
            recv_sem=rest_r.at[i],
            device_id=across,
            device_id_type=MESH,
        )

    def unpack_rest(values):
        for k in range(CELLS // CHUNK):
            ext_sc[k, 0:REST, :] = values[REST * k : REST * (k + 1), :]

    def with_rest(main, k):
        return jnp.concatenate([main, ext_sc[k], jnp.zeros((8, CHUNK), F32)], axis=0)

    def quarter_of(i):
        j = slot_view(i, c) // 2
        row_half = jnp.where(crops_ref[1, 0, j] >= crops_ref[0, 0, j], 0, 1)
        col_half = jnp.where(crops_ref[1, 1, j] >= crops_ref[0, 1, j], 0, 1)
        return j, row_half, jnp.where(flips_ref[1, j] > 0, 1 - col_half, col_half)

    def arriving(m):
        return lax.rem(2 * m + quarter, 2 * quarter)

    def find_quarter(m, carry):
        j, row_half, col_half = quarter_of(arriving(m))
        cell = iota((1, CHUNK), 1)
        row, col = (cell >> 4) + 16 * row_half, (cell & 15) + 16 * col_half
        col = jnp.where(flips_ref[1, j] > 0, W - 1 - col, col)
        row = row + crops_ref[1, 0, j] - crops_ref[0, 0, j]
        col = col + crops_ref[1, 1, j] - crops_ref[0, 1, j]
        col = jnp.where(flips_ref[0, j] > 0, W - 1 - col, col)
        find_sc[m] = (iota((CELLS, CHUNK), 0) == row * W + col).astype(BF16)
        return carry

    def pack_second(m):
        _, row_half, col_half = quarter_of(2 * m)
        low, high = pair_sc[2 * m + 1, :, 0:half], pair_sc[2 * m + 1, :, half:CELLS]
        columns = dot_nt(jnp.where(row_half == 0, low, high), join_sc[...])
        kept = jnp.where(col_half == 0, columns[:, CHUNK:half], columns[:, 0:CHUNK])
        packed_sc[m, :, 0:half] = jnp.where(row_half == 0, high, low)
        packed_sc[m, :, half : half + CHUNK] = kept.astype(BF16)

    def unpack_second(m):
        far_copy(m, 1, 0).wait_recv()
        far_copy(m, 1, 1).wait_recv()
        _, row_half, col_half = quarter_of(arriving(m))
        whole = far_sc[2 * m + 1, :, 0:half]
        kept = far_sc[2 * m + 1, :, half : half + CHUNK]
        found = dot(far_sc[2 * m], find_sc[m]).astype(BF16)
        left, right = jnp.where(col_half == 0, found, kept), jnp.where(col_half == 0, kept, found)
        joined = dot(jnp.concatenate([left, right], axis=1), join_sc[...]).astype(BF16)
        far_sc[2 * m + 1, :, 0:half] = jnp.where(row_half == 0, joined, whole)
        far_sc[2 * m + 1, :, half:CELLS] = jnp.where(row_half == 0, whole, joined)

    def far_start(m, v):
        rest_copy(2 * m + v).start()
        far_copy(m, v, 0).start()
        far_copy(m, v, 1).start()

    def far_copy(m, v, h):
        i = 2 * m + v
        if v == 0:
            cols = half_cols(h)
            src = pair_sc.at[i, :, cols]
        else:
            cols = pl.ds(half * h, half if h == 0 else CHUNK)
            src = packed_sc.at[m, :, cols]
        return pltpu.make_async_remote_copy(
            src_ref=src,
            dst_ref=far_sc.at[i, :, cols],
            send_sem=far_s.at[i, h],
            recv_sem=far_r.at[i, h],
            device_id=across,
            device_id_type=MESH,
        )

    def to_mate(i):
        theirs = slot_view(i, 1 - c)
        load(theirs).wait()
        activate(theirs)
        for k, cols in enumerate(chunks()):
            half_out[i, :, cols] = partial(theirs, cols).astype(BF16)
            if k % 2 == 1:
                half_copy(i, k // 2).start()

    def forward(m, carry):
        for v in range(2):
            i = 2 * m + v

            @pl.when(i < 2 * quarter - 1)
            def _():
                to_mate(i + 1)

            mine = slot_view(i, c)
            load(mine).wait()
            activate(mine)
            for k, cols in enumerate(chunks()):
                if k % 2 == 0:
                    half_copy(i, k // 2).wait_recv()
                both = partial(mine, cols) + half_in[i, :, cols].astype(F32)
                pair_sc[i, :, cols] = both[0:MAIN, :].astype(BF16)
                pack_sc[REST * k : REST * (k + 1), :] = both[MAIN : MAIN + REST, :]

                @pl.when(i >= quarter)
                def _():
                    mid_sc[i - quarter, :, cols] = both

                if v == 0 and k % 2 == 1:

                    @pl.when(i < quarter)
                    def _(h=k // 2):
                        far_copy(m, 0, h).start()

            pair_rest[i] = pack_sc[...].astype(BF16)
            if v == 1:
                pack_second(m)

            @pl.when(i < quarter)
            def _():
                rest_copy(i).start()
                if v == 1:
                    far_copy(m, 1, 0).start()
                    far_copy(m, 1, 1).start()

        return carry

    to_mate(0)
    lax.fori_loop(0, quarter, forward, 0)
    lax.fori_loop(0, quarter, find_quarter, 0)

    chan_send(7, dfar_of, dn_sc.at[1])

    chan_wait(1, wsp_own, wsp_sc)
    stacked = wsp_sc[...].reshape(4 * NEW_PAD, TAPS * NEW_PAD)
    lane, row = iota((MID_PAD, 4 * NEW_PAD), 1), iota((MID_PAD, 4 * NEW_PAD), 0)
    hit = None
    for b in range(4):
        inner = lane - NEW_PAD * b
        one = (inner >= 0) & (inner < n_own) & (row == inner + n_own * b)
        hit = one if hit is None else hit | one
    wb_sc[...] = dot(hit.astype(BF16), stacked).astype(BF16)
    taps_eye = iota((TAPS * NEW_PAD, TAPS * NEW_PAD), 0) == iota((TAPS * NEW_PAD, TAPS * NEW_PAD), 1)
    wf_sc[...] = dot_nt(taps_eye.astype(BF16), wb_sc[...]).astype(BF16)

    cell = iota((1, CELLS), 1)
    col_at, row_at = cell & (W - 1), cell >> 5

    def inside(values, row_step, col_step):
        ok = None
        if col_step != 0:
            ok = (col_at + col_step >= 0) & (col_at + col_step < W)
        if row_step != 0:
            on = (row_at + row_step >= 0) & (row_at + row_step < H)
            ok = on if ok is None else ok & on
        return values if ok is None else jnp.where(ok, values, 0.0)

    def at_offset(values, row_step, col_step):
        move = (-(W * row_step + col_step)) % CELLS
        rolled = values if move == 0 else pltpu.roll(values, move, 1)
        return inside(rolled, row_step, col_step)

    chan_wait(2, dnew_of, dn_sc.at[0])

    def back_slot(i, carry):
        far = jnp.where(i < quarter, 1, 0)
        keep = jnp.where(i < quarter, quarter, i - quarter)
        for b in range(4):
            for l in range(2):
                pack_dn[...] = dn_sc[far, b, :, 128 * l : 128 * (l + 1)].astype(F32)
                at = CHUNK * b + 128 * l
                dnf_sc[0:n_new, at : at + 128] = pack_dn[pl.ds(n_new * lax.rem(i, quarter), n_new), :]
        grad = dnf_sc[...]
        for b in range(3):
            moved = at_offset(grad, 0, 1 - b)
            for a in range(3):
                t = 3 * a + b
                tap = at_offset(moved, 1 - a, 0)
                dcol_sc[keep, NEW_PAD * t : NEW_PAD * (t + 1), :] = tap.astype(BF16)
        for cols in chunks():
            d_sc[i, :, cols] = dot(wb_sc[...], dcol_sc[keep, :, cols])
        return carry

    lax.fori_loop(quarter, 2 * quarter, back_slot, 0)

    group = dpn_sc.shape[1]
    full = n_in // group

    def dp_load(k, rows):
        return pltpu.make_async_copy(
            dpass_hbm.at[pl.ds(k * group, rows)],
            dpn_sc.at[lax.rem(k, 2), pl.ds(0, rows)],
            dp_sem.at[lax.rem(k, 2)],
        )

    def dp_split(k, rows):
        first = k * group if isinstance(k, int) else pl.multiple_of(k * group, group)
        for l in range(CELLS // 128):
            at = slice(128 * l, 128 * (l + 1))
            native = dpn_sc[lax.rem(k, 2), 0:rows, :, at].astype(F32)
            for ch in range(rows):
                flat_sc[l, (n_views + 1) * ch : (n_views + 1) * ch + n_views, :] = native[ch]
            for n in range(n_views):
                by_view = flat_sc[l, pl.ds(n, rows, stride=n_views + 1), :]
                dp_sc[n, pl.ds(first, rows), at] = by_view.astype(BF16)

    left = n_in - full * group

    def dp_step(k, carry):
        @pl.when(k < full - 1)
        def _():
            dp_load(k + 1, group).start()

        dp_load(k, group).wait()
        dp_split(k, group)
        return carry

    def dp_some(first, last):
        lax.fori_loop(first, last, dp_step, 0)

    early = full - 2
    dp_load(0, group).start()
    dp_some(0, early)

    chan_wait(0, same(own_par), par_sc)

    def gathered(at):
        total = None
        for b in range(4):
            piece = jnp.where(iota((8, 256), 1) < n_own, par_sc[b], 0.0)
            piece = piece if b == 0 else pltpu.roll(piece, n_own * b, 1)
            total = piece if total is None else total + piece
        return two_rows(total[at : at + 1, :])

    row_to_cols(colm_sc.at[2], gathered(2))
    row_to_cols(colm_sc.at[3], gathered(3))

    def middle_view(q, first):
        rest_copy(q).wait_recv()

        def arrive_first():
            far_copy(q // 2, 0, 0).wait_recv()
            far_copy(q // 2, 0, 1).wait_recv()

        if first:
            arrive_first()
        else:
            pl.when(lax.rem(q, 2) == 0)(arrive_first)

            @pl.when(lax.rem(q, 2) == 1)
            def _():
                unpack_second(q // 2)

        unpack_rest(far_rest[q].astype(F32))
        for k, cols in enumerate(chunks()):
            mid_sc[q, :, cols] = mid_sc[q, :, cols] + with_rest(far_sc[q, :, cols].astype(F32), k)

    def middle_sums(q, carry):
        @pl.when(q > 0)
        def _():
            middle_view(q, False)

        first, second = None, None
        for cols in chunks():
            part = mid_sc[q, :, cols] - wide(colm_sc, 8)
            one, two = lane_fold(part), lane_fold(part * part)
            first = one if first is None else first + one
            second = two if second is None else second + two
        accm_sc[0] += first
        accm_sc[1] += second
        return carry

    middle_view(0, True)
    pivot = sum(lane_fold(mid_sc[0, :, cols]) for cols in chunks())
    colm_sc[8] = jnp.broadcast_to(jnp.sum(pivot, axis=1, keepdims=True) / CELLS, colm_sc.shape[1:])
    pivot_row = cols_to_row(padm_sc, pivot) / CELLS
    lax.fori_loop(0, quarter, middle_sums, 0)
    off_row = cols_to_row(padm_sc, accm_sc[0]) / owned_count
    cmsg_sc[0] = jnp.zeros_like(cmsg_sc[0])
    cmsg_sc[0, 0:2, :] = pivot_row + off_row
    cmsg_sc[0, 2:4, :] = cols_to_row(padm_sc, accm_sc[1]) - off_row * off_row * owned_count
    accm_sc[...] = jnp.zeros_like(accm_sc)
    cstat_sc[0, ci] = cmsg_sc[0]
    chan_send(3, same(cmsg_sc.at[0]), cstat_sc.at[0])
    far_start(quarter // 2, 0)
    far_start(quarter // 2, 1)
    dp_some(early, full)
    if left > 0:
        dp_load(full, left).start()
        dp_load(full, left).wait()
        dp_split(full, left)
    chan_wait(3, same(cmsg_sc.at[0]), cstat_sc.at[0])
    group_mean, group_dev = combine(cstat_sc[0], owned_count)
    msg_sc[0] = jnp.zeros_like(msg_sc[0])
    msg_sc[0, 0:2, :] = group_mean
    msg_sc[0, 2:4, :] = group_dev
    stat_sc[1, bi] = msg_sc[0]
    batch_send(1, same(msg_sc.at[0]), stat_sc.at[1])
    chan_wait(7, dfar_of, dn_sc.at[1])
    lax.fori_loop(0, quarter, back_slot, 0)
    batch_wait(1, same(msg_sc.at[0]), stat_sc.at[1])
    meanm_row, devm_row = combine(stat_sc[1], local_count)
    rstdm_row = lax.rsqrt(devm_row / pixels + EPS)
    row_to_cols(colm_sc.at[0], meanm_row)
    row_to_cols(colm_sc.at[1], rstdm_row)

    def mid_point(values):
        mean, rstd = wide(colm_sc, 0), wide(colm_sc, 1)
        norm = (values - mean) * rstd
        pre = norm * wide(colm_sc, 2) + wide(colm_sc, 3)
        s = sigmoid(pre)
        act = pre * s
        return norm, act, s + act * (1.0 - s)

    def mid_own(q, carry):
        first, second = None, None
        for cols in chunks():
            norm, act, slope = mid_point(mid_sc[q, :, cols])
            actm_sc[q, :, cols] = act.astype(BF16)
            grad = d_sc[quarter + q, :, cols] * slope
            d_sc[quarter + q, :, cols] = grad
            mid_sc[q, :, cols] = norm
            one, two = lane_fold(grad), lane_fold(grad * norm)
            first = one if first is None else first + one
            second = two if second is None else second + two
        accm_sc[0] += first
        accm_sc[1] += second
        return carry

    lax.fori_loop(0, quarter, mid_own, 0)
    cmsg_sc[1] = jnp.zeros_like(cmsg_sc[1])
    cmsg_sc[1, 0:2, :] = cols_to_row(padm_sc, accm_sc[0])
    cmsg_sc[1, 2:4, :] = cols_to_row(padm_sc, accm_sc[1])
    cstat_sc[1, ci] = cmsg_sc[1]
    chan_send(4, same(cmsg_sc.at[1]), cstat_sc.at[1])
    for q in range(2, quarter):
        far_start((quarter + q) // 2, q % 2)

    def tiles_of(ref):
        rows, cols = ref.shape
        return [(r, l, min(128, cols - 128 * l)) for r in range(rows // 16) for l in range(-(-cols // 128))]

    def scatter(refs, kind, values):
        out, back, _ = refs
        per = out.shape[1]
        for at, (r, l, width) in enumerate(tiles_of(values)):
            tile = values[16 * r : 16 * r + 16, 128 * l : 128 * l + width]
            out[at // per, at % per, :, 0:width] = tile.astype(BF16)
        back[bi] = out[bi]
        batch_send(kind, lambda other: out.at[other], back)

    def reduce_gather(refs, kind):
        out, back, whole = refs
        batch_wait(kind, lambda other: out.at[other], back)
        total = back[0].astype(F32)
        for at in range(1, nb):
            total = total + back[at].astype(F32)
        out[bi] = total.astype(BF16)
        whole[bi] = total.astype(BF16)
        batch_send(kind + 1, same(out.at[bi]), whole)

    def gather(refs, kind, ref):
        out, _, whole = refs
        per = out.shape[1]
        batch_wait(kind + 1, same(out.at[bi]), whole)
        for at, (r, l, width) in enumerate(tiles_of(ref)):
            tile = whole[at // per, at % per, :, 0:width]
            ref[16 * r : 16 * r + 16, 128 * l : 128 * l + width] = tile.astype(F32)

    spread_refs, reduce_refs = (ws_out, ws_in, ws_all), (wr_out, wr_back, wr_all)

    def spread_grad(q, carry):
        wsg_sc[...] += dot_nt(actm_sc[q], dcol_sc[q])
        return carry

    lax.fori_loop(0, quarter, spread_grad, 0)
    scatter(spread_refs, 4, wsg_sc)
    chan_wait(4, same(cmsg_sc.at[1]), cstat_sc.at[1])
    msg_sc[1] = (cstat_sc[1, 0] + cstat_sc[1, 1]) + (cstat_sc[1, 2] + cstat_sc[1, 3])
    stat_sc[2, bi] = msg_sc[1]
    batch_send(2, same(msg_sc.at[1]), stat_sc.at[2])
    ready = quarter // 2

    def far_point(q, carry):
        m = quarter // 2 + q // 2
        rest_copy(quarter + q).wait_recv()
        unpack_rest(pair_rest[q].astype(F32) + far_rest[quarter + q].astype(F32))

        @pl.when(lax.rem(q, 2) == 0)
        def _():
            far_copy(m, 0, 0).wait_recv()
            far_copy(m, 0, 1).wait_recv()

        @pl.when(lax.rem(q, 2) == 1)
        def _():
            unpack_second(m)

        for k, cols in enumerate(chunks()):
            part = pair_sc[q, :, cols].astype(F32) + far_sc[quarter + q, :, cols].astype(F32)
            norm, act, slope = mid_point(with_rest(part, k))
            d_sc[q, :, cols] = d_sc[q, :, cols] * slope
            half_in[q, :, cols] = norm.astype(BF16)
        return carry

    lax.fori_loop(0, ready, far_point, 0)
    reduce_gather(spread_refs, 4)
    batch_wait(2, same(msg_sc.at[1]), stat_sc.at[2])
    mid_sums = stat_sc[2, 0]
    for at in range(1, nb):
        mid_sums = mid_sums + stat_sc[2, at]
    row_to_cols(colm_sc.at[4], mid_sums[0:2, :] / pixels)
    row_to_cols(colm_sc.at[5], mid_sums[2:4, :] / pixels)
    row_to_cols(colm_sc.at[6], gathered(2) * rstdm_row)

    def dm_copy(i, h):
        return pltpu.make_async_remote_copy(
            src_ref=dm_out.at[i, :, half_cols(h)],
            dst_ref=dm_in.at[i, :, half_cols(h)],
            send_sem=dm_s.at[i, h],
            recv_sem=dm_r.at[i, h],
            device_id=mate,
            device_id_type=MESH,
        )

    def store(n):
        return pltpu.make_async_copy(slope_sc.at[n], dv_hbm.at[n], store_sem.at[n])

    def back_view(n, dm_ref):
        mean, scale = wide(col_sc, 0), wide(col_sc, 2)
        first, second = None, None
        for cols in chunks():
            grad = dot(wr_sc[...], dm_ref[:, cols]) * slope_sc[n, 0:n_in, cols].astype(F32)
            slope_sc[n, 0:n_in, cols] = (grad * scale + dp_sc[n, :, cols].astype(F32)).astype(BF16)
            off = x_sc[n, 0:n_in, cols].astype(F32) - mean
            one, two = lane_fold(grad), lane_fold(grad * off)
            first = one if first is None else first + one
            second = two if second is None else second + two
        acc_sc[0] += first
        acc_sc[1] += second
        wg_sc[:, 0:n_in] += dot_nt(dm_ref[...], act_sc[n])

    def dm_own(q, carry):
        i = quarter + q
        for cols in chunks():
            grad = d_sc[i, :, cols] - wide(colm_sc, 4) - mid_sc[q, :, cols] * wide(colm_sc, 5)
            dm_out[i, :, cols] = (grad * wide(colm_sc, 6)).astype(BF16)
        dm_copy(i, 0).start()
        dm_copy(i, 1).start()
        return carry

    lax.fori_loop(0, quarter, dm_own, 0)

    def back_mate(i):
        dm_copy(i, 0).wait_recv()
        dm_copy(i, 1).wait_recv()
        back_view(slot_view(i, 1 - c), dm_in.at[i])

    def back_own(q, carry):
        back_view(slot_view(quarter + q, c), dm_out.at[quarter + q])

        @pl.when(q > 0)
        def _():
            back_mate(quarter + q - 1)

        return carry

    lax.fori_loop(0, quarter, back_own, 0)
    back_mate(2 * quarter - 1)

    def back_far(q, carry):
        @pl.when(q >= ready)
        def _():
            far_point(q, carry)

        for k, cols in enumerate(chunks()):
            grad = d_sc[q, :, cols] - wide(colm_sc, 4) - half_in[q, :, cols].astype(F32) * wide(colm_sc, 5)
            dm_out[q, :, cols] = (grad * wide(colm_sc, 6)).astype(BF16)
            if k % 2 == 1:
                dm_copy(q, k // 2).start()
        back_view(slot_view(q, c), dm_out.at[q])

        @pl.when(q > 0)
        def _():
            back_mate(q - 1)

        return carry

    lax.fori_loop(0, quarter // 2, back_far, 0)
    gather(spread_refs, 4, wsg_sc)
    for b in range(4):
        wsp_sc[b, 0:40, :] = wsg_sc[n_own * b : n_own * b + 40, :].astype(BF16)
    wsgi_sc[ci] = wsp_sc[ci]
    wsg_of = lambda other: wsp_sc.at[other]
    chan_send(6, wsg_of, wsgi_sc)
    lax.fori_loop(quarter // 2, quarter, back_far, 0)
    back_mate(quarter - 1)

    scatter(reduce_refs, 6, wg_sc)
    msg_sc[2] = jnp.zeros_like(msg_sc[2])
    msg_sc[2, 0:2, :] = cols_to_row(padc_sc, acc_sc[0])
    msg_sc[2, 2:4, :] = cols_to_row(padc_sc, acc_sc[1]) * rstd_row
    stat_sc[3, bi] = msg_sc[2]
    batch_send(3, same(msg_sc.at[2]), stat_sc.at[3])

    def spread(q, carry):
        for k, cols in enumerate(chunks()):
            taps = dot(wf_sc[...], actm_sc[q, :, cols])
            for l in range(2):
                flat_sc[2 * k + l, 0 : TAPS * NEW_PAD, :] = taps[:, 128 * l : 128 * (l + 1)]
        total = None
        for b in range(3):
            column = None
            for a in range(3):
                t = 3 * a + b
                tap = [flat_sc[l, NEW_PAD * t : NEW_PAD * t + 40, :] for l in range(CELLS // 128)]
                tap = at_offset(jnp.concatenate(tap, axis=1), a - 1, 0)
                column = tap if column is None else column + tap
            column = at_offset(column, 0, b - 1)
            total = column if total is None else total + column
        for b in range(4):
            newo_sc[b, q] = total[0:n_new, CHUNK * b : CHUNK * (b + 1)].astype(BF16)
        return carry

    lax.fori_loop(0, quarter, spread, 0)
    new_of = lambda other: newo_sc.at[other]
    newi_sc[ci] = newo_sc[ci]
    chan_send(5, new_of, newi_sc)
    reduce_gather(reduce_refs, 6)
    batch_wait(3, same(msg_sc.at[2]), stat_sc.at[3])
    total = stat_sc[3, 0]
    for at in range(1, nb):
        total = total + stat_sc[3, at]
    gain_scale = gain_row * rstd_row
    row_to_cols(col_sc.at[4], -gain_scale * rstd_row * (total[2:4, :] / pixels))
    row_to_cols(col_sc.at[5], -gain_scale * (total[0:2, :] / pixels))

    def finish(n, carry):
        mean, slant, level = wide(col_sc, 0), wide(col_sc, 4), wide(col_sc, 5)
        for cols in chunks():
            rest = (x_sc[n, 0:n_in, cols].astype(F32) - mean) * slant + level
            slope_sc[n, 0:n_in, cols] = (slope_sc[n, 0:n_in, cols].astype(F32) + rest).astype(BF16)
        store(n).start()
        return carry

    lax.fori_loop(0, n_views, finish, 0)

    sums_ref[...] = jnp.zeros_like(sums_ref)
    sums_ref[0:1, :] = one_row(total[2:4, :])
    sums_ref[1:2, :] = one_row(total[0:2, :])
    all_sums = jnp.concatenate([one_row(mid_sums[2:4, :]), one_row(mid_sums[0:2, :]), jnp.zeros((6, 256), F32)], axis=0)
    own_sums = all_sums
    for b in range(1, 4):
        own_sums = jnp.where(ci == b, pltpu.roll(all_sums, 256 - n_own * b, 1), own_sums)
    sums_ref[2:4, :] = own_sums[0:2, :]

    chan_wait(5, new_of, newi_sc)
    for b in range(4):
        for q in range(quarter):
            new_ref[quarter * b + q] = newi_sc[b, q]
    chan_wait(6, wsg_of, wsgi_sc)
    wsg_total = (wsgi_sc[0].astype(F32) + wsgi_sc[1].astype(F32)) + (
        wsgi_sc[2].astype(F32) + wsgi_sc[3].astype(F32)
    )
    wsg_ref[...] = wsg_total[0:n_own, :]
    gather(reduce_refs, 6, wg_sc)
    wrg_ref[...] = wg_sc[0 : wrg_ref.shape[0], 0:n_in]

    def stored(n, carry):
        store(n).wait()
        return carry

    lax.fori_loop(0, n_views, stored, 0)

    def sent(i, carry):
        rest_copy(i).wait_send()
        for h in range(2):
            half_copy(i, h).wait_send()
            dm_copy(i, h).wait_send()
        return carry

    lax.fori_loop(0, 2 * quarter, sent, 0)

    def sent_far(m, carry):
        for v in range(2):
            for h in range(2):
                far_copy(m, v, h).wait_send()
        return carry

    lax.fori_loop(0, quarter, sent_far, 0)


def layer(nb, crops, flips, views, stats, vectors, wr_t, w_spread, d_new, d_passed):
    n_views, n_rows, _ = views.shape
    n_mid, n_in = wr_t.shape
    n_own = n_mid // 4
    quarter = n_views // 4
    n_new = d_new.shape[0]
    n_cols = TAPS * NEW_PAD
    together = -(-quarter * n_new // 16) * 16
    in_pad = -(-n_in // 16) * 16
    ws_tiles = -(-(MID_PAD // 16 * -(-n_cols // 128)) // nb)
    wr_tiles = -(-(MID_PAD // 16 * -(-in_pad // 128)) // nb)
    group = 16
    vmem = pl.BlockSpec(memory_space=pltpu.VMEM)
    anywhere = pl.BlockSpec(memory_space=pl.ANY)
    smem = pl.BlockSpec(memory_space=pltpu.SMEM)
    dma = pltpu.SemaphoreType.DMA
    slots = 2 * quarter
    return pl.pallas_call(
        functools.partial(layer_kernel, nb),
        in_specs=[smem, smem, anywhere] + [vmem] * 8 + [anywhere],
        out_specs=[anywhere, vmem, vmem, vmem, vmem],
        out_shape=[
            jax.ShapeDtypeStruct((n_views, n_rows, CELLS), BF16),
            jax.ShapeDtypeStruct((n_views, n_new, CHUNK), BF16),
            jax.ShapeDtypeStruct((n_mid, n_in), F32),
            jax.ShapeDtypeStruct((n_own, n_cols), F32),
            jax.ShapeDtypeStruct((8, 256), F32),
        ],
        scratch_shapes=[
            pltpu.VMEM((n_views, n_rows, CELLS), BF16),
            pltpu.VMEM((n_views, n_in, CELLS), BF16),
            pltpu.VMEM((n_views, n_rows, CELLS), BF16),
            pltpu.VMEM((n_views, n_in, CELLS), BF16),
            pltpu.VMEM((slots, MID_PAD, CELLS), BF16),
            pltpu.VMEM((slots, MID_PAD, CELLS), BF16),
            pltpu.VMEM((slots, MAIN, CELLS), BF16),
            pltpu.VMEM((slots, MAIN, CELLS), BF16),
            pltpu.VMEM((slots, 16, CHUNK), BF16),
            pltpu.VMEM((slots, 16, CHUNK), BF16),
            pltpu.VMEM((16, CHUNK), F32),
            pltpu.VMEM((CELLS // CHUNK, 8, CHUNK), F32),
            pltpu.VMEM((quarter, MAIN, CELLS // 2 + CHUNK), BF16),
            pltpu.VMEM((quarter, CELLS, CHUNK), BF16),
            pltpu.VMEM((CELLS // 2, CELLS // 2), BF16),
            pltpu.VMEM((slots, MID_PAD, CELLS), F32),
            pltpu.VMEM((quarter + 1, n_cols, CELLS), BF16),
            pltpu.VMEM((quarter, MID_PAD, CELLS), F32),
            pltpu.VMEM((quarter, MID_PAD, CELLS), BF16),
            pltpu.VMEM((slots, MID_PAD, CELLS), BF16),
            pltpu.VMEM((slots, MID_PAD, CELLS), BF16),
            pltpu.VMEM((2, 2, together, CHUNK), BF16),
            pltpu.VMEM((2, 4, together, CHUNK), BF16),
            pltpu.VMEM((together, 128), F32),
            pltpu.VMEM((NEW_PAD, CELLS), F32),
            pltpu.VMEM((2, group, n_views, CELLS), BF16),
            pltpu.VMEM((CELLS // 128, max(max(group, n_new) * (n_views + 1), n_cols), 128), F32),
            pltpu.VMEM((8, 256), F32),
            pltpu.VMEM((4, 8, 256), F32),
            pltpu.VMEM((4, NEW_PAD, n_cols), BF16),
            pltpu.VMEM((n_in, MID_PAD), BF16),
            pltpu.VMEM((MID_PAD, n_in), BF16),
            pltpu.VMEM((MID_PAD, n_cols), BF16),
            pltpu.VMEM((n_cols, MID_PAD), BF16),
            pltpu.VMEM((4, nb, 8, 128), F32),
            pltpu.VMEM((2, 4, 8, 128), F32),
            pltpu.VMEM((3, 8, 128), F32),
            pltpu.VMEM((2, 8, 128), F32),
            pltpu.VMEM((6, n_in, 128), F32),
            pltpu.VMEM((9, MID_PAD, 128), F32),
            pltpu.VMEM((256, 128), F32),
            pltpu.VMEM((256, 128), F32),
            pltpu.VMEM((2, n_in, 128), F32),
            pltpu.VMEM((2, MID_PAD, 128), F32),
            pltpu.VMEM((MID_PAD, in_pad), F32),
            pltpu.VMEM((MID_PAD, n_cols), F32),
            pltpu.VMEM((4, NEW_PAD, n_cols), BF16),
            pltpu.VMEM((nb, ws_tiles, 16, 128), BF16),
            pltpu.VMEM((nb, ws_tiles, 16, 128), BF16),
            pltpu.VMEM((nb, ws_tiles, 16, 128), BF16),
            pltpu.VMEM((nb, wr_tiles, 16, 128), BF16),
            pltpu.VMEM((nb, wr_tiles, 16, 128), BF16),
            pltpu.VMEM((nb, wr_tiles, 16, 128), BF16),
            pltpu.VMEM((4, quarter, n_new, CHUNK), BF16),
            pltpu.VMEM((4, quarter, n_new, CHUNK), BF16),
            dma((n_views,)),
            dma((n_views,)),
            dma((slots, 2)),
            dma((slots, 2)),
            dma((slots, 2)),
            dma((slots, 2)),
            dma((slots,)),
            dma((slots,)),
            dma((slots, 2)),
            dma((slots, 2)),
            dma((8, nb)),
            dma((8, nb)),
            dma((8, 4)),
            dma((8, 4)),
            dma((2,)),
        ],
        compiler_params=pltpu.CompilerParams(
            collective_id=0, has_side_effects=True, vmem_limit_bytes=VMEM_LIMIT
        ),
        name="layer",
    )(crops, flips, views, stats, *vectors, wr_t, w_spread, d_new, d_passed)


def solution(mesh):
    nb = mesh.shape["batch"]

    def on_device(features, crops, flips, gain_in, shift_in, w_reduce, gain_mid, shift_mid, w_spread, d_passed, d_new):
        n_own, n_new = w_spread.shape[0], w_spread.shape[3]

        w9 = jnp.transpose(w_spread, (1, 2, 0, 3)).reshape(TAPS, n_own, n_new)
        crops_t, flips_t = jnp.transpose(crops, (1, 2, 0)), jnp.transpose(flips)
        swap = lambda v: jnp.transpose(v, (1, 0, 2))
        views, passed, stats = crop_views(swap(features), crops_t, flips_t)
        dv, new_maps, wr_grad, ws_grad, sums = layer(
            nb, crops_t, flips_t, views, stats, (gain_in, shift_in, gain_mid, shift_mid), jnp.transpose(w_reduce), w9, swap(d_new), swap(d_passed)
        )
        features_grad, new_maps, wr_grad, ws_grad, *grads = place_views(
            crops_t, flips_t, dv, new_maps, wr_grad, ws_grad, sums
        )
        ws_grad = jnp.transpose(ws_grad.reshape(3, 3, n_own, n_new), (2, 0, 1, 3))
        return (swap(passed), swap(new_maps), swap(features_grad), jnp.transpose(wr_grad), ws_grad, *grads)

    return jax.shard_map(
        on_device,
        mesh=mesh,
        in_specs=(
            P("batch", "chan", None),
            P("batch", None, None),
            P("batch", None),
            P("chan"),
            P("chan"),
            P("chan", None),
            P("chan"),
            P("chan"),
            P("chan", None, None, None),
            P("batch", "chan", None),
            P("batch", None, "chan"),
        ),
        out_specs=(
            P("batch", "chan", None),
            P("batch", None, "chan"),
            P("batch", "chan", None),
            P("chan", None),
            P("chan", None, None, None),
            P("chan"),
            P("chan"),
            P("chan"),
            P("chan"),
        ),
        check_vma=False,
    )
```
